128 devices in a mesh: gx: 32 (over z, y, core), gy: 4 (over x).
Axes of the slice: x: 4, y: 4, z: 4, core: 2. Of those that a mesh axis runs over, the one named last changes fastest.
Arguments:
- fields: float32 [6, 512, 96, 128], P(None, 'gx', 'gy'), may hold values from -6 to 6
- material: int32 [512, 96, 128], P('gx', 'gy'), may hold values from 0 to 15
- permittivity: float32 [16], replicated, may hold values from 1 to 4
- patch_cell: int32 [32768], P(('gx', 'gy')), may hold values from 0 to 49151
- patch_owner: int32 [32768, 1], P(('gx', 'gy')), may hold values from 0 to 127; in each aligned block of 256 rows (0 to 255, 256 to 511, ...) at most 4 rows name the same one
Outputs:
- new_fields: float32 [6, 512, 96, 128], P(None, 'gx', 'gy')
- far_field: float32 [12, 16384], P(None, ('gx', 'gy'))
The draws below stay inside these ranges and needn't reach their ends.
Inputs may be any that keep to these rules, and one draw needn't show every extreme that they name: `patch_cell`: an index into the cells of the patch's own device block, x slowest and z fastest. `patch_owner`: among the rows of one device no sector is named by more than 4 rows, a bound that some block reaches; every sector is named by some row.
All inputs are finite; a program needn't handle non-finite values.
Results may differ from the reference program's by a relative error of at most 0.00022.
Values sent between devices are 32-bit elements; how exact they have to be, the bound alone decides.
No kernel may reach another device: no remote copies, remote signals or barrier semaphores. Data moves between devices by JAX's collectives and lax.ppermute only.
A program may use at most 128 MiB of HBM per device.

```python
import math
import jax
import jax.numpy as jnp
import numpy as np
from jax import lax

CX = 16
CY = 24
NZ = 128
P_DEV = 256
ANG_DEV = 128
COURANT = 64
MATERIALS = 16
NX = 512
NY = 96
OWNERS = 128
PATCHES = 32768
CAP = 4
N_GX = 32
N_GY = 4


def plant(drawn, stream_key, least, top_value):
    shape = drawn.shape
    index_at = [jax.random.randint(jax.random.fold_in(stream_key, axis), (), 0, shape[axis]) for axis in range(len(shape))]
    drawn = drawn.at[tuple(index_at)].set(least)
    longest = shape.index(max(shape))
    index_at[longest] = (index_at[longest] + 1) % shape[longest]
    return drawn.at[tuple(index_at)].set(top_value)


def steps_of(rng, dims, cuts, smallest, largest):
    level, own = 1.0, jax.random.fold_in(rng, 6)
    for dim, shards_of in cuts:
        heights = jnp.exp(jax.random.uniform(jax.random.fold_in(own, dim), (shards_of,), jnp.float32, smallest / len(cuts), largest / len(cuts)))
        level = level * jnp.repeat(heights, dims[dim] // shards_of).reshape([-1 if axis == dim else 1 for axis in range(len(dims))])
    return level


def deal_out(stream_key, own, number, rows, count, top, most, skew):
    sequence = jax.random.permutation(stream_key, count)
    packed, usual = portions_of(count, rows * top, most, skew, True), portions_of(count, rows * top, most, skew, False)
    places = jnp.arange(count)

    def named(lengths, turn):
        used = int((lengths > 0).sum())
        fixed = max(1, used // 4)
        passed = fixed + (places - fixed + turn * (used - fixed)) % max(1, count - fixed)
        return jnp.zeros((count,), jnp.int32).at[sequence[jnp.where(places < fixed, places, passed)]].set(jnp.asarray(lengths, jnp.int32))

    lengths = jnp.where(number % 4 == 0, named(packed, number // 4), named(usual, number - number // 4 - 1))
    mixed = jax.random.permutation(jax.random.fold_in(own, 3), count)
    giver, taker = mixed[0:count // 2 * 2:2], mixed[1:count // 2 * 2:2]
    room = jnp.minimum(lengths[giver] - 1, most - lengths[taker]) // 2
    room = jnp.where((giver == sequence[0]) | (taker == sequence[0]) | (lengths[taker] == 0), 0, jnp.maximum(room, 0))
    passed = jax.random.randint(jax.random.fold_in(own, 4), (count // 2,), 0, 1 << 20) % (room + 1)
    lengths = lengths.at[giver].add(-passed).at[taker].add(passed)
    labels = jnp.searchsorted(jnp.cumsum(lengths), jnp.arange(rows * top), side="right").astype(jnp.int32)
    grid = labels.reshape(top, rows).T
    grid = grid[jax.random.permutation(jax.random.fold_in(own, 1), rows)]
    turn = jax.random.randint(jax.random.fold_in(own, 2), (rows, 1), 0, top)
    return jnp.take_along_axis(grid, (jnp.arange(top)[None, :] + turn) % top, axis=1)


def portions_of(count, total, bound, skew, full):
    loads = [(1 << 20) // math.isqrt(rank ** skew) + 1 for rank in range(1, count + 1)]
    largest = bound if full else min(bound, max(-(-total // count), total * loads[0] // sum(loads)))
    least = 1 if total - largest >= count - 1 else 0
    given, spare = [largest] + [least] * (count - 1), total - largest - least * (count - 1)
    while spare > 0:
        movable = [i for i in range(1, count) if given[i] < largest] or [i for i in range(1, count) if given[i] < bound]
        mass, remaining = sum([loads[i] for i in movable]), spare
        for i in movable:
            more = min(bound - given[i], max(1, remaining * loads[i] // mass), spare)
            given[i] = given[i] + more
            spare = spare - more
    return np.array(given)


def bell_draw(stream_key, shape, deviation, limit, shards=(), held_as=jnp.bfloat16):
    result = jax.random.normal(stream_key, shape, jnp.float32) * deviation
    if len(shards) > 0:
        result = steps_of(stream_key, shape, shards, -0.22, 0.18) * result
    return jnp.clip(result, min=-limit, max=limit).astype(held_as)


def setup_inputs(seed: int = 0) -> dict:
    streams_of = jax.random.split(jax.random.key(seed), 6)
    fields = bell_draw(streams_of[0], (6, NX, NY, NZ), 1.0, 6.0, ((1, 32), (2, 4)), jnp.float32)
    material = plant(jax.random.randint(streams_of[1], (NX, NY, NZ), 0, MATERIALS), jax.random.fold_in(streams_of[1], 1), 0, MATERIALS - 1).astype(jnp.int32)
    permittivity = jnp.clip(jnp.exp(jax.random.uniform(streams_of[2], (MATERIALS,), jnp.float32, math.log(1.0), math.log(4.0))), 1.0, 4.0)
    patch_cell = plant(jax.random.randint(streams_of[3], (PATCHES,), 0, CX * CY * NZ), jax.random.fold_in(streams_of[3], 1), 0, (CX * CY * NZ) - 1).astype(jnp.int32)
    patch_owner_keys = jax.random.split(jax.random.fold_in(streams_of[4], 1), PATCHES // P_DEV)
    patch_owner_turns = jax.random.permutation(jax.random.fold_in(streams_of[4], 3), PATCHES // P_DEV)
    patch_owner = jax.vmap(lambda own, number: deal_out(jax.random.fold_in(streams_of[4], 2), own, number, P_DEV, OWNERS, 1, CAP, 2))(patch_owner_keys, patch_owner_turns).reshape((PATCHES, 1))
    return dict(fields=fields, material=material, permittivity=permittivity, patch_cell=patch_cell, patch_owner=patch_owner)


KAPPA = 0.5

def explicit(padded, curl_coef, half_step):
    centre = padded[:, 1:-1, 1:-1]

    def slope_x(member):
        return 0.5 * (padded[member, 2:, 1:-1] - padded[member, :-2, 1:-1])

    def slope_y(member):
        return 0.5 * (padded[member, 1:-1, 2:] - padded[member, 1:-1, :-2])

    def slope_z(member):
        ground = jnp.pad(centre[member], ((0, 0), (0, 0), (1, 1)))
        return 0.5 * (ground[:, :, 2:] - ground[:, :, :-2])
    curl_h = [slope_y(5) - slope_z(4), slope_z(3) - slope_x(5), slope_x(4) - slope_y(3)]
    curl_e = [slope_y(2) - slope_z(1), slope_z(0) - slope_x(2), slope_x(1) - slope_y(0)]
    electric = [centre[member] + curl_coef * curl_h[member] for member in range(3)]
    magnetic = [centre[3 + member] - half_step * curl_e[member] for member in range(3)]
    return jnp.stack(electric + magnetic)

def factor_lines(coef_lines):

    def advance(upper_prev, coef_row):
        pivot = 1.0 / (1.0 + 2.0 * coef_row + coef_row * upper_prev)
        upper_now = -coef_row * pivot
        return (upper_now, (upper_now, pivot))
    ignored, (uppers, pivots) = lax.scan(advance, jnp.zeros_like(coef_lines[0]), coef_lines)
    return (uppers, pivots)

def sweep_lines(coef_lines, uppers, pivots, right_lines):

    def forward(carry_prev, rows):
        coef_row, pivot, right_row = rows
        now_value = (right_row + coef_row * carry_prev) * pivot
        return (now_value, now_value)
    start_zero = jnp.zeros_like(right_lines[0] * coef_lines[0])
    ignored, reduced = lax.scan(forward, start_zero, (coef_lines, pivots, right_lines))

    def backward(next_value, rows):
        upper_row, reduced_row = rows
        now_value = reduced_row - upper_row * next_value
        return (now_value, now_value)
    ignored, solved = lax.scan(backward, start_zero, (uppers, reduced), reverse=True)
    return solved

def solve_leading(stack, coef_lines):
    uppers, pivots = factor_lines(coef_lines)

    def one_component(component):
        return sweep_lines(coef_lines, uppers, pivots, component)
    return lax.map(one_component, stack)

def far_phase(pos_x, pos_y, pos_z, owner_f, owners, angle_count):
    theta = math.pi * (jnp.arange(angle_count, dtype=jnp.float32) + 0.5) / angle_count
    azimuth = owner_f * (2.0 * math.pi / owners)
    sin_theta = jnp.sin(theta)[None, :]
    cos_theta = jnp.cos(theta)[None, :]
    cos_phi = jnp.cos(azimuth)[:, None]
    sin_phi = jnp.sin(azimuth)[:, None]
    return KAPPA * (pos_x[:, None] * sin_theta * cos_phi + pos_y[:, None] * sin_theta * sin_phi + pos_z[:, None] * cos_theta)

def reference(fields, material, permittivity, patch_cell, patch_owner):
    eps = permittivity[material]
    half_step = COURANT / 2.0
    implicit_coef = half_step * half_step / eps
    curl_coef = half_step / eps
    padded = jnp.pad(fields, ((0, 0), (1, 1), (1, 1), (0, 0)))
    first_side = explicit(padded, curl_coef, half_step)
    mid_fields = solve_leading(first_side, implicit_coef)
    padded = jnp.pad(mid_fields, ((0, 0), (1, 1), (1, 1), (0, 0)))
    second_side = explicit(padded, curl_coef, half_step)
    moved = jnp.moveaxis(second_side, 2, 1)
    coef_y = jnp.transpose(implicit_coef, (1, 0, 2))
    new_fields = jnp.moveaxis(solve_leading(moved, coef_y), 1, 2)
    owners = N_GX * N_GY
    device = jnp.arange(PATCHES, dtype=jnp.int32) // P_DEV
    block_x = device // N_GY
    block_y = device % N_GY
    grid_x = block_x * CX + patch_cell // (CY * NZ)
    grid_y = block_y * CY + patch_cell // NZ % CY
    grid_z = patch_cell % NZ
    samples = new_fields[:, grid_x, grid_y, grid_z]
    owner = patch_owner[:, 0]
    phases = far_phase(grid_x.astype(jnp.float32), grid_y.astype(jnp.float32), grid_z.astype(jnp.float32), owner.astype(jnp.float32), owners, ANG_DEV)
    cosine = jnp.cos(phases)
    sine = jnp.sin(phases)
    values_t = jnp.transpose(samples)
    terms = jnp.concatenate([values_t[:, :, None] * cosine[:, None, :], values_t[:, :, None] * sine[:, None, :]], axis=1)
    summed = jax.ops.segment_sum(terms, owner, num_segments=owners)
    far_field = jnp.transpose(summed, (1, 0, 2)).reshape(12, owners * ANG_DEV) * (1.0 / math.sqrt(P_DEV))
    return (new_fields, far_field)
```

```python
import math

import jax
import jax.numpy as jnp
from jax import lax
from jax.experimental import pallas as pl
from jax.experimental.pallas import tpu as pltpu
from jax.sharding import PartitionSpec as P

F32 = jnp.float32
CX, CY, NZ = 16, 24, 128
NB = 32
NBY = 4
ROWS = 32
HALF = 32.0
XC = (1, 2, 4, 5)
YC = (0, 2, 3, 5)
SLOTS = 4
PATCH = 256
KAPPA = 0.5


def ds(start, size, stride=None):
    return pl.ds(start, size) if stride is None else pl.ds(start, size, stride=stride)


def call(body, outs, args, scratch=(), smem=()):
    specs = [
        pl.BlockSpec(memory_space=pltpu.SMEM if i in smem else pltpu.VMEM) for i in range(len(args))
    ]
    return pl.pallas_call(
        body,
        out_shape=[jax.ShapeDtypeStruct(s, F32) for s in outs],
        in_specs=specs,
        out_specs=[pl.BlockSpec(memory_space=pltpu.VMEM) for _ in outs],
        scratch_shapes=[pltpu.VMEM(s, F32) for s in scratch],
        compiler_params=pltpu.CompilerParams(vmem_limit_bytes=40 * 1024 * 1024),
    )(*args)


def flag(cond):
    return jnp.where(cond, 1.0, 0.0).astype(F32)


def row_of(shape):
    return lax.broadcasted_iota(jnp.int32, shape, 0)


def lane_of(shape):
    return lax.broadcasted_iota(jnp.int32, shape, 1)


def diff_z(f):
    lane = lane_of(f.shape)
    up = jnp.where(lane == NZ - 1, 0.0, pltpu.roll(f, NZ - 1, 1))
    down = jnp.where(lane == 0, 0.0, pltpu.roll(f, 1, 1))
    return up - down


def diff_y(f, below, above):
    row = row_of(f.shape)
    up = jnp.where(row == CY - 1, above, pltpu.roll(f, CY - 1, 0))
    down = jnp.where(row == 0, below, pltpu.roll(f, 1, 0))
    return up - down


def right_sides(f, s, dx, dy, dz):
    curl_h = (dy[5] - dz[4], dz[3] - dx[5], dx[4] - dy[3])
    curl_e = (dy[2] - dz[1], dz[0] - dx[2], dx[1] - dy[0])
    electric = [s * f[m] + (0.5 / HALF) * curl_h[m] for m in range(3)]
    magnetic = [s * (f[3 + m] - (0.5 * HALF) * curl_e[m]) for m in range(3)]
    return electric + magnetic


def edges_body(f, mat, perm, xh, xl, yh, yl, eps):
    m = mat[...]
    e = jnp.full(m.shape, perm[0], F32)
    for k in range(1, 16):
        e = jnp.where(m == k, perm[k], e)
    eps[...] = e
    for i, c in enumerate(XC):
        xh[ds(i * CY, CY), :] = f[ds((c * CX + CX - 1) * CY, CY), :]
        xl[ds(i * CY, CY), :] = f[ds(c * CX * CY, CY), :]
    for out, edge, inner in ((yh, CY - 1, CY - 2), (yl, 0, 1)):
        for c in range(6):
            out[ds(c * CX, CX), :] = f[ds(c * CX * CY + edge, CX, CY), :]
        for i, c in enumerate(YC):
            out[ds((6 + i) * CX, CX), :] = f[ds(c * CX * CY + inner, CX, CY), :]
        out[ds(10 * CX, CX), :] = eps[ds(edge, CX, CY), :]


def first_body(f, eps, xlo, xhi, ylo, yhi, sol, lsp, rsp, send, ht, hu, hd, he, gs):
    gx, gy = lax.axis_index("gx"), lax.axis_index("gy")
    mxl, mxh = flag(gx > 0), flag(gx < NB - 1)
    myl, myh = flag(gy > 0), flag(gy < NBY - 1)
    ht[...] = jnp.zeros(ht.shape, F32)
    hu[...] = jnp.zeros(hu.shape, F32)
    hd[...] = jnp.zeros(hd.shape, F32)
    he[...] = jnp.ones(he.shape, F32)
    for c in range(6):
        ht[ds(c * 128, CX, 8), :] = ylo[ds(c * CX, CX), :] * myl
        ht[ds(c * 128 + 1, CX, 8), :] = yhi[ds(c * CX, CX), :] * myh
    for i, c in enumerate(YC):
        hu[ds(i * 128, CX, 8), :] = f[ds(c * CX * CY, CX, CY), :]
        hu[ds(i * 128 + 1, CX, 8), :] = yhi[ds((6 + i) * CX, CX), :] * myh
        hd[ds(i * 128, CX, 8), :] = ylo[ds((6 + i) * CX, CX), :] * myl
        hd[ds(i * 128 + 1, CX, 8), :] = f[ds(c * CX * CY + CY - 1, CX, CY), :]
    he[ds(0, CX, 8), :] = jnp.where(myl > 0, ylo[ds(10 * CX, CX), :], 1.0)
    he[ds(1, CX, 8), :] = jnp.where(myh > 0, yhi[ds(10 * CX, CX), :], 1.0)
    row8 = row_of((8, NZ))
    inside = jnp.where(row8 == 0, myl, jnp.where(row8 == 1, myh, 0.0))

    def main(c, x):
        return f[ds(pl.multiple_of((c * CX + x) * CY, 8), CY), :]

    def halo(ref, i, x):
        return ref[ds(pl.multiple_of(i * 128 + x * 8, 8), 8), :]

    def forward(x, carry):
        wg, yl, ys = carry[0], carry[1], carry[2:]
        x_up, x_down = jnp.minimum(x + 1, CX - 1), jnp.maximum(x - 1, 0)
        fm = [main(c, x) for c in range(6)]
        fh = [halo(ht, c, x) for c in range(6)]
        both = [jnp.concatenate([fm[c], fh[c]], axis=0) for c in range(6)]
        dx, dy, dz = {}, {}, {}
        for i, c in enumerate(XC):
            up = jnp.where(x == CX - 1, xhi[ds(i * CY, CY), :] * mxh, main(c, x_up))
            down = jnp.where(x == 0, xlo[ds(i * CY, CY), :] * mxl, main(c, x_down))
            up_h = jnp.where(x == CX - 1, 0.0, halo(ht, c, x_up))
            down_h = jnp.where(x == 0, 0.0, halo(ht, c, x_down))
            dx[c] = jnp.concatenate([up - down, up_h - down_h], axis=0)
        for i, c in enumerate(YC):
            inner = diff_y(fm[c], fh[c][0:1], fh[c][1:2])
            dy[c] = jnp.concatenate([inner, halo(hu, i, x) - halo(hd, i, x)], axis=0)
        for c in (0, 1, 3, 4):
            dz[c] = diff_z(both[c])
        e = jnp.concatenate([eps[ds(pl.multiple_of(x * CY, 8), CY), :], halo(he, 0, x)], axis=0)
        s = e * (1.0 / (HALF * HALF))
        right = right_sides(both, s, dx, dy, dz)
        w = s + wg
        g = 1.0 / (1.0 + w)
        at = pl.multiple_of(x * ROWS, 8)
        gs[ds(at, ROWS), :] = g
        yl = yl * g
        lsp[ds(at, ROWS), :] = yl
        new = []
        for c in range(6):
            r = jnp.concatenate([right[c][:CY], right[c][CY:] * inside], axis=0)
            y = (r + ys[c]) * g
            sol[ds(pl.multiple_of(c * CX * ROWS + x * ROWS, 8), ROWS), :] = y
            new.append(y)
        return (w * g, yl, *new)

    one, zero = jnp.ones((ROWS, NZ), F32), jnp.zeros((ROWS, NZ), F32)
    lax.fori_loop(0, CX, forward, (one, one) + (zero,) * 6)

    def backward(k, carry):
        x = CX - 1 - k
        at = pl.multiple_of(x * ROWS, 8)
        g = gs[ds(at, ROWS), :]
        ul = lsp[ds(at, ROWS), :] + g * carry[0]
        ur = g * carry[1]
        lsp[ds(at, ROWS), :] = ul
        rsp[ds(at, ROWS), :] = ur
        new = []
        for c in range(6):
            here = ds(pl.multiple_of(c * CX * ROWS + x * ROWS, 8), ROWS)
            u = sol[here, :] + g * carry[2 + c]
            sol[here, :] = u
            new.append(u)
        return (ul, ur, *new)

    lead = lax.fori_loop(0, CX, backward, (zero, one) + (zero,) * 6)
    left_first, right_first, lead = lead[0], lead[1], lead[2:]
    tail = [sol[ds((c * CX + CX - 1) * ROWS, ROWS), :] for c in range(6)]

    def with_halo(value, extra):
        return jnp.concatenate([value[:CY], extra], axis=0)

    def end(i, x):
        return ht[ds(i * 128 + x * 8, 8), :]

    scale = 0.5 / HALF
    last = CX - 1
    lead_rows, tail_rows = list(lead), list(tail)
    lead_rows[1] = with_halo(lead[1], end(1, 0))
    tail_rows[1] = with_halo(tail[1], end(1, last))
    lead_rows[4] = with_halo(lead[4], he[ds(0, 8), :] * scale)
    tail_rows[4] = with_halo(tail[4], he[ds(last * 8, 8), :] * scale)
    lead_rows[2] = with_halo(lead[2], lead[2][CY:] + scale * end(4, 0))
    tail_rows[2] = with_halo(tail[2], tail[2][CY:] - scale * end(4, last))
    for c in range(6):
        send[ds(c, ROWS, 16), :] = lead_rows[c]
        send[ds(8 + c, ROWS, 16), :] = tail_rows[c]
    send[ds(6, ROWS, 16), :] = left_first
    send[ds(7, ROWS, 16), :] = right_first
    send[ds(14, ROWS, 16), :] = right_first
    send[ds(15, ROWS, 16), :] = rsp[ds((CX - 1) * ROWS, ROWS), :]


def join_body(rec, back, phis, psis, ms, ns):
    gx = lax.axis_index("gx")
    row8 = row_of((8, NZ))
    shifted = (row8 == 5) & ((gx == CY) | (gx == CY + 1))

    def line(b, k):
        return jnp.broadcast_to(rec[ds(b * 16 + k, 1), :], (8, NZ))

    def shifts(b):
        low = high = jnp.zeros((8, NZ), F32)
        if b > 0:
            low = jnp.where(shifted, line(b, 4) * line(b - 1, 9), 0.0)
        if b < NB - 1:
            high = jnp.where(shifted, -line(b, 12) * line(b + 1, 1), 0.0)
        return low, high

    m = n = jnp.zeros((8, NZ), F32)
    for b in range(NB):
        low, high = shifts(b)
        a, cross, d = line(b, 6), line(b, 7), line(b, 15)
        p = rec[ds(b * 16, 8), :] + a * low + cross * high
        q = rec[ds(b * 16 + 8, 8), :] + cross * low + d * high
        ms[ds(b * 8, 8), :] = m
        ns[ds(b * 8, 8), :] = n
        gain = 1.0 / (1.0 - a * n)
        phi = gain * (p + a * m)
        psi = gain * cross
        phis[ds(b * 8, 8), :] = phi
        psis[ds(b * 8, 8), :] = psi
        m = q + cross * (m + n * phi)
        n = d + cross * (n * psi)
    ahead = jnp.zeros((8, NZ), F32)
    for b in reversed(range(NB)):
        low, high = shifts(b)
        lead = phis[ds(b * 8, 8), :] + psis[ds(b * 8, 8), :] * ahead
        back[ds(b * 16, 8), :] = ms[ds(b * 8, 8), :] + ns[ds(b * 8, 8), :] * lead + low
        back[ds(b * 16 + 8, 8), :] = ahead + high
        ahead = lead


def second_body(back, sol, lsp, rsp, eps, soly, ly, ry, rec, mid, inc, out, r2, gys, yls):
    for c in range(6):
        inc[ds(c * ROWS, ROWS), :] = back[ds(c, ROWS, 16), :]
        out[ds(c * ROWS, ROWS), :] = back[ds(8 + c, ROWS, 16), :]

    def settle(x, carry):
        at = pl.multiple_of(x * ROWS, 8)
        left, right = lsp[ds(at, ROWS), :], rsp[ds(at, ROWS), :]
        for c in range(6):
            here = ds(pl.multiple_of((c * CX + x) * ROWS, 8), ROWS)
            mid[here, :] = (
                sol[here, :]
                + left * inc[ds(c * ROWS, ROWS), :]
                + right * out[ds(c * ROWS, ROWS), :]
            )
        return carry

    lax.fori_loop(0, CX, settle, 0)

    def main(c, x):
        return mid[ds(pl.multiple_of((c * CX + x) * ROWS, 8), CY), :]

    def stencil(x, carry):
        x_up, x_down = jnp.minimum(x + 1, CX - 1), jnp.maximum(x - 1, 0)
        f = [main(c, x) for c in range(6)]
        dx, dy, dz = {}, {}, {}
        for c in XC:
            up = jnp.where(x == CX - 1, out[ds(c * ROWS, CY), :], main(c, x_up))
            down = jnp.where(x == 0, inc[ds(c * ROWS, CY), :], main(c, x_down))
            dx[c] = up - down
        for c in YC:
            edge = mid[ds(pl.multiple_of((c * CX + x) * ROWS + CY, 8), 8), :]
            dy[c] = diff_y(f[c], edge[0:1], edge[1:2])
        for c in (0, 1, 3, 4):
            dz[c] = diff_z(f[c])
        s = eps[ds(pl.multiple_of(x * CY, 8), CY), :] * (1.0 / (HALF * HALF))
        right = right_sides(f, s, dx, dy, dz)
        for c in range(6):
            r2[ds(pl.multiple_of((c * CX + x) * CY, 8), CY), :] = right[c]
        return carry

    lax.fori_loop(0, CX, stencil, 0)

    one, zero = jnp.ones((CX, NZ), F32), jnp.zeros((CX, NZ), F32)

    wg, yl, ys = one, one, [zero] * 6
    for y in range(CY):
        s = eps[ds(y, CX, CY), :] * (1.0 / (HALF * HALF))
        w = s + wg
        g = 1.0 / (1.0 + w)
        wg = w * g
        gys[ds(y * CX, CX), :] = g
        yl = yl * g
        yls[ds(y * CX, CX), :] = yl
        for c in range(6):
            here = ds(c * CX * CY + y, CX, CY)
            ys[c] = (r2[here, :] + ys[c]) * g
            r2[here, :] = ys[c]
    tail = list(ys)
    ul, ur, us = zero, one, [zero] * 6
    right_last = None
    for y in reversed(range(CY)):
        g = gys[ds(y * CX, CX), :]
        ul = yls[ds(y * CX, CX), :] + g * ul
        ur = g * ur
        if y == CY - 1:
            right_last = ur
        ly[ds(y, CX, CY), :] = ul
        ry[ds(y, CX, CY), :] = ur
        for c in range(6):
            here = ds(c * CX * CY + y, CX, CY)
            us[c] = r2[here, :] + g * us[c]
            soly[here, :] = us[c]
    for c in range(6):
        rec[ds(c * CX, CX), :] = us[c]
        rec[ds((8 + c) * CX, CX), :] = tail[c]
    rec[ds(6 * CX, CX), :] = ul
    rec[ds(7 * CX, CX), :] = ur
    rec[ds(14 * CX, CX), :] = ur
    rec[ds(15 * CX, CX), :] = right_last


def finish_body(
    rec0, rec1, rec2, rec3, soly, ly, ry, cell, cell_row, owner_row, new, send, recs, inc, out, table
):
    gy = lax.axis_index("gy")
    size = 16 * CX
    for k, part in enumerate((rec0, rec1, rec2, rec3)):
        at = lax.rem(gy + (NBY - k), NBY)
        recs[ds(pl.multiple_of(at * size, 8), size), :] = part[...]

    def get(b, k):
        return recs[ds(b * size + k * CX, CX), :]

    zero = jnp.zeros((CX, NZ), F32)
    m, n = [zero] * 6, zero
    kept = []
    for b in range(NBY):
        a, cross, d = get(b, 6), get(b, 7), get(b, 15)
        gain = 1.0 / (1.0 - a * n)
        phi = [gain * (get(b, c) + a * m[c]) for c in range(6)]
        psi = gain * cross
        kept.append((m, n, phi, psi))
        m = [get(b, 8 + c) + cross * (m[c] + n * phi[c]) for c in range(6)]
        n = d + cross * (n * psi)
    ahead = [zero] * 6
    incoming, outgoing = [zero] * 6, [zero] * 6
    for b in reversed(range(NBY)):
        mb, nb, phi, psi = kept[b]
        lead = [phi[c] + psi * ahead[c] for c in range(6)]
        for c in range(6):
            incoming[c] = jnp.where(gy == b, mb[c] + nb * lead[c], incoming[c])
            outgoing[c] = jnp.where(gy == b, ahead[c], outgoing[c])
        ahead = lead
    for c in range(6):
        inc[ds(c * CX, CX), :] = incoming[c]
        out[ds(c * CX, CX), :] = outgoing[c]

    def settle(x, carry):
        at = pl.multiple_of(x * CY, 8)
        left, right = ly[ds(at, CY), :], ry[ds(at, CY), :]
        for c in range(6):
            here = ds(pl.multiple_of((c * CX + x) * CY, 8), CY)
            value = (
                soly[here, :]
                + left * inc[ds(c * CX + x, 1), :]
                + right * out[ds(c * CX + x, 1), :]
            )
            new[here, :] = value
            table[ds(x * (CY * 8) + c, CY, 8), :] = value
        return carry

    lax.fori_loop(0, CX, settle, 0)

    lane = lane_of((8, NZ))
    halves = []
    for half in range(PATCH // NZ):

        def pick(j, acc):
            at = cell[half * NZ + j]
            values = table[ds(pl.multiple_of((at >> 7) * 8, 8), 8), :]
            moved = pltpu.roll(values, (j - (at & 127)) & 127, 1)
            return jnp.where(lane == j, moved, acc)

        halves.append(lax.fori_loop(0, NZ, pick, jnp.zeros((8, NZ), F32), unroll=8))
    samples = jnp.concatenate(halves, axis=1)
    row8 = row_of((8, PATCH))
    samples = jnp.where(row8 < 6, samples, jnp.where(row8 == 6, cell_row[...].astype(F32), 0.0))
    owner = jnp.broadcast_to(owner_row[...], (PATCH, PATCH))
    rows, lanes = row_of((PATCH, PATCH)), lane_of((PATCH, PATCH))
    owner_col = jnp.sum(jnp.where(rows == lanes, owner, 0), axis=1, keepdims=True)
    earlier = (owner == owner_col) & (rows < lanes)
    rank = jnp.sum(jnp.where(earlier, 1, 0), axis=0, keepdims=True)
    slot = row_of((NZ, PATCH))
    spread = jnp.where(
        (slot >> 3) == rank, jnp.concatenate([samples] * (NZ // 8), axis=0), 0.0
    )
    hot = jnp.where(slot == owner[:NZ], 1.0, 0.0)
    send[...] = lax.dot_general(
        hot, spread, (((1,), (1,)), ((), ())),
        precision=lax.Precision.HIGHEST, preferred_element_type=F32,
    )


def sine_cosine(v):
    k = jnp.floor(v * (2.0 / math.pi) + 0.5)
    r = ((v - k * 1.5703125) - k * 4.837512969970703125e-4) - k * 7.54978995489188e-8
    z = r * r
    s = ((-1.9515295891e-4 * z + 8.3321608736e-3) * z - 1.6666654611e-1) * z * r + r
    c = ((2.443315711809948e-5 * z - 1.388731625493765e-3) * z + 4.166664568298827e-2) * (z * z)
    c = c - 0.5 * z + 1.0
    q = k.astype(jnp.int32)
    odd = (q & 1) == 1
    sine, cosine = jnp.where(odd, c, s), jnp.where(odd, s, c)
    sine = jnp.where((q & 2) == 2, -sine, sine)
    cosine = jnp.where(((q + 1) & 2) == 2, -cosine, cosine)
    return sine, cosine


def sector_body(recv, far):
    sector = lax.axis_index("gx") * NBY + lax.axis_index("gy")
    angle = lane_of((8, NZ)).astype(F32)
    sin_theta, cos_theta = sine_cosine(math.pi * (angle + 0.5) / NZ)
    turn = jnp.full((8, NZ), sector, jnp.int32).astype(F32) * (2.0 * math.pi / (NB * NBY))
    sin_phi, cos_phi = sine_cosine(turn)
    sin_theta, cos_theta = sin_theta[0:1], cos_theta[0:1]
    sin_phi, cos_phi = sin_phi[0:1], cos_phi[0:1]
    values = recv[...]
    flipped = jnp.transpose(values)
    source = row_of((NZ, 1))
    base_x, base_y = (source >> 2) * CX, (source & 3) * CY
    sine_sum = jnp.zeros((8, NZ), F32)
    cosine_sum = jnp.zeros((8, NZ), F32)
    for k in range(SLOTS):
        cells = values[:, 8 * k + 6 : 8 * k + 7].astype(jnp.int32)
        line = cells >> 7
        x = (line * 2731) >> 16
        px = (base_x + x).astype(F32)
        py = (base_y + line - x * CY).astype(F32)
        pz = (cells & 127).astype(F32)
        phase = KAPPA * (
            (px * sin_theta * cos_phi + py * sin_theta * sin_phi) + pz * cos_theta
        )
        sine, cosine = sine_cosine(phase)
        part = flipped[8 * k : 8 * k + 8]
        sine_sum += jnp.dot(
            part, sine, precision=lax.Precision.HIGHEST, preferred_element_type=F32
        )
        cosine_sum += jnp.dot(
            part, cosine, precision=lax.Precision.HIGHEST, preferred_element_type=F32
        )
    scale = 1.0 / math.sqrt(PATCH)
    far[0:6, :] = cosine_sum[0:6] * scale
    far[6:12, :] = sine_sum[0:6] * scale


def shift(value, axis, by):
    count = lax.axis_size(axis)
    return lax.ppermute(value, axis, [(i, (i + by) % count) for i in range(count)])


def local(fields, material, permittivity, patch_cell, patch_owner):
    f = fields.reshape(6 * CX * CY, NZ)
    mat = material.reshape(CX * CY, NZ)
    plane, cells = (len(XC) * CY, NZ), (CX * CY, NZ)
    xh, xl, yh, yl, eps = call(
        edges_body,
        [plane, plane, (11 * CX, NZ), (11 * CX, NZ), cells],
        [f, mat, permittivity],
        smem=(2,),
    )
    xlo, xhi = shift(xh, "gx", 1), shift(xl, "gx", -1)
    ylo, yhi = shift(yh, "gy", 1), shift(yl, "gy", -1)
    tall = (CX * ROWS, NZ)
    sol, lsp, rsp, send = call(
        first_body,
        [(6 * CX * ROWS, NZ), tall, tall, (ROWS * 16, NZ)],
        [f, eps, xlo, xhi, ylo, yhi],
        [(6 * 128, NZ), (4 * 128, NZ), (4 * 128, NZ), (128, NZ), tall],
    )
    rec = lax.all_to_all(send.reshape(NB, 16, NZ), "gx", 0, 0, tiled=True)
    (back,) = call(join_body, [(NB * 16, NZ)], [rec.reshape(NB * 16, NZ)], [(NB * 8, NZ)] * 4)
    back = lax.all_to_all(back.reshape(NB, 16, NZ), "gx", 0, 0, tiled=True)
    soly, ly, ry, rec = call(
        second_body,
        [(6 * CX * CY, NZ), cells, cells, (16 * CX, NZ)],
        [back.reshape(NB * 16, NZ), sol, lsp, rsp, eps],
        [(6 * CX * ROWS, NZ), (6 * ROWS, NZ), (6 * ROWS, NZ), (6 * CX * CY, NZ), cells, cells],
    )
    others = [shift(rec, "gy", k) for k in (1, 2, 3)]
    new, send = call(
        finish_body,
        [(6 * CX * CY, NZ), (NB * NBY, NZ)],
        [
            rec, *others, soly, ly, ry,
            patch_cell, patch_cell.reshape(1, PATCH), patch_owner.reshape(1, PATCH),
        ],
        [(NBY * 16 * CX, NZ), (6 * CX, NZ), (6 * CX, NZ), (CX * CY * 8, NZ)],
        smem=(7,),
    )
    recv = lax.all_to_all(send, ("gx", "gy"), 0, 0, tiled=True)
    (far,) = call(sector_body, [(12, NZ)], [recv])
    return new.reshape(6, CX, CY, NZ), far


def solution(mesh):
    return jax.shard_map(
        local,
        mesh=mesh,
        in_specs=(
            P(None, "gx", "gy", None),
            P("gx", "gy", None),
            P(),
            P(("gx", "gy")),
            P(("gx", "gy"), None),
        ),
        out_specs=(P(None, "gx", "gy", None), P(None, ("gx", "gy"))),
        check_vma=False,
    )
```

```python
import math

import jax
import jax.numpy as jnp
from jax import lax
from jax.experimental import pallas as pl
from jax.experimental.pallas import tpu as pltpu
from jax.sharding import PartitionSpec as P

F32 = jnp.float32
CX, CY, NZ = 16, 24, 128
NB = 32
NBY = 4
ROWS = 32
HALF = 32.0
XC = (1, 2, 4, 5)
YC = (0, 2, 3, 5)
SLOTS = 4
PATCH = 256
KAPPA = 0.5
PICKS = 32
COST = 4_000_000
VM = 63


def ds(start, size, stride=None):
    return pl.ds(start, size) if stride is None else pl.ds(start, size, stride=stride)


def call(body, outs, args, scratch=(), smem=(), hbm=(), hbm_outs=(), sems=0, cost=0, vmem=40):
    def place(i, slow):
        if i in slow:
            return pl.BlockSpec(memory_space=pltpu.HBM)
        return pl.BlockSpec(memory_space=pltpu.SMEM if slow is hbm and i in smem else pltpu.VMEM)

    shapes = [o if isinstance(o, jax.ShapeDtypeStruct) else jax.ShapeDtypeStruct(o, F32) for o in outs]
    space = [o if not isinstance(o, tuple) else pltpu.VMEM(o, F32) for o in scratch]
    if sems:
        space.append(pltpu.SemaphoreType.DMA((sems,)))
    estimate = None
    if cost:
        estimate = pl.CostEstimate(flops=cost, bytes_accessed=cost, transcendentals=0)
    return pl.pallas_call(
        body,
        out_shape=shapes,
        in_specs=[place(i, hbm) for i in range(len(args))],
        out_specs=[place(i, hbm_outs) for i in range(len(outs))],
        scratch_shapes=space,
        cost_estimate=estimate,
        compiler_params=pltpu.CompilerParams(vmem_limit_bytes=vmem * 1024 * 1024),
    )(*args)


def flag(cond):
    return jnp.where(cond, 1.0, 0.0).astype(F32)


def row_of(shape):
    return lax.broadcasted_iota(jnp.int32, shape, 0)


def lane_of(shape):
    return lax.broadcasted_iota(jnp.int32, shape, 1)


def diff_z(f):
    lane = lane_of(f.shape)
    up = jnp.where(lane == NZ - 1, 0.0, pltpu.roll(f, NZ - 1, 1))
    down = jnp.where(lane == 0, 0.0, pltpu.roll(f, 1, 1))
    return up - down


def diff_y(f, below, above):
    row = row_of(f.shape)
    up = jnp.where(row == CY - 1, above, pltpu.roll(f, CY - 1, 0))
    down = jnp.where(row == 0, below, pltpu.roll(f, 1, 0))
    return up - down


def right_sides(f, s, dx, dy, dz):
    curl_h = (dy[5] - dz[4], dz[3] - dx[5], dx[4] - dy[3])
    curl_e = (dy[2] - dz[1], dz[0] - dx[2], dx[1] - dy[0])
    electric = [s * f[m] + (0.5 / HALF) * curl_h[m] for m in range(3)]
    magnetic = [s * (f[3 + m] - (0.5 * HALF) * curl_e[m]) for m in range(3)]
    return electric + magnetic


def lookup(m, perm):
    e = jnp.full(m.shape, perm[0], F32)
    for k in range(1, 16):
        e = jnp.where(m == k, perm[k], e)
    return e


def edges_body(f_hbm, mat_hbm, perm_hbm, xh, xl, yh, yl, f, mat, perm, sem):
    copies = [
        pltpu.make_async_copy(f_hbm, f, sem.at[0]),
        pltpu.make_async_copy(mat_hbm, mat, sem.at[1]),
        pltpu.make_async_copy(perm_hbm, perm, sem.at[2]),
    ]
    for copy in copies:
        copy.start()
    for copy in copies:
        copy.wait()
    for i, c in enumerate(XC):
        xh[ds(i * CY, CY), :] = f[ds((c * CX + CX - 1) * CY, CY), :]
        xl[ds(i * CY, CY), :] = f[ds(c * CX * CY, CY), :]
    for out, edge, inner in ((yh, CY - 1, CY - 2), (yl, 0, 1)):
        for c in range(6):
            out[ds(c * CX, CX), :] = f[ds(c * CX * CY + edge, CX, CY), :]
        for i, c in enumerate(YC):
            out[ds((6 + i) * CX, CX), :] = f[ds(c * CX * CY + inner, CX, CY), :]
        out[ds(10 * CX, CX), :] = lookup(mat[ds(edge, CX, CY), :], perm)


def inner_body(f, mat, perm_hbm, scaled, right, gx_out, lsp, rsp, gy_out, ly, ry, perm, yls, sem):
    copy = pltpu.make_async_copy(perm_hbm, perm, sem.at[0])
    copy.start()
    copy.wait()

    def main(c, x):
        return f[ds((c * CX + x) * CY, CY), :]

    one, zero = jnp.ones((CY, NZ), F32), jnp.zeros((CY, NZ), F32)
    wg, yl = one, one
    for x in range(CX):
        at = ds(x * CY, CY)
        s = lookup(mat[at, :], perm) * (1.0 / (HALF * HALF))
        scaled[at, :] = s
        w = s + wg
        g = 1.0 / (1.0 + w)
        wg = w * g
        gx_out[at, :] = g
        yl = yl * g
        lsp[at, :] = yl
        fm = [main(c, x) for c in range(6)]
        dx, dy, dz = {}, {}, {}
        for c in XC:
            up = main(c, x + 1) if x < CX - 1 else zero
            down = main(c, x - 1) if x > 0 else zero
            dx[c] = up - down
        for c in YC:
            dy[c] = diff_y(fm[c], 0.0, 0.0)
        for c in (0, 1, 3, 4):
            dz[c] = diff_z(fm[c])
        for c, r in enumerate(right_sides(fm, s, dx, dy, dz)):
            right[ds((c * CX + x) * CY, CY), :] = r
    ul, ur = zero, one
    for x in reversed(range(CX)):
        at = ds(x * CY, CY)
        g = gx_out[at, :]
        ul = lsp[at, :] + g * ul
        ur = g * ur
        lsp[at, :] = ul
        rsp[at, :] = ur
    one, zero = jnp.ones((CX, NZ), F32), jnp.zeros((CX, NZ), F32)
    wg, yl = one, one
    for y in range(CY):
        w = scaled[ds(y, CX, CY), :] + wg
        g = 1.0 / (1.0 + w)
        wg = w * g
        gy_out[ds(y * CX, CX), :] = g
        yl = yl * g
        yls[ds(y * CX, CX), :] = yl
    ul, ur = zero, one
    for y in reversed(range(CY)):
        g = gy_out[ds(y * CX, CX), :]
        ul = yls[ds(y * CX, CX), :] + g * ul
        ur = g * ur
        ly[ds(y, CX, CY), :] = ul
        ry[ds(y, CX, CY), :] = ur


def first_body(
    f, scaled, right, gxs, lsp, rsp, xlo, xhi, ylo, yhi,
    sol, lsp_h, rsp_h, send, ht, hu, hd, he, gs,
):
    gx, gy = lax.axis_index("gx"), lax.axis_index("gy")
    mxl, mxh = flag(gx > 0), flag(gx < NB - 1)
    myl, myh = flag(gy > 0), flag(gy < NBY - 1)
    ht[...] = jnp.zeros(ht.shape, F32)
    hu[...] = jnp.zeros(hu.shape, F32)
    hd[...] = jnp.zeros(hd.shape, F32)
    he[...] = jnp.ones(he.shape, F32)
    for c in range(6):
        ht[ds(c * 128, CX, 8), :] = ylo[ds(c * CX, CX), :] * myl
        ht[ds(c * 128 + 1, CX, 8), :] = yhi[ds(c * CX, CX), :] * myh
    for i, c in enumerate(YC):
        hu[ds(i * 128, CX, 8), :] = f[ds(c * CX * CY, CX, CY), :]
        hu[ds(i * 128 + 1, CX, 8), :] = yhi[ds((6 + i) * CX, CX), :] * myh
        hd[ds(i * 128, CX, 8), :] = ylo[ds((6 + i) * CX, CX), :] * myl
        hd[ds(i * 128 + 1, CX, 8), :] = f[ds(c * CX * CY + CY - 1, CX, CY), :]
    he[ds(0, CX, 8), :] = jnp.where(myl > 0, ylo[ds(10 * CX, CX), :], 1.0)
    he[ds(1, CX, 8), :] = jnp.where(myh > 0, yhi[ds(10 * CX, CX), :], 1.0)
    row8 = row_of((8, NZ))
    inside = jnp.where(row8 == 0, myl, jnp.where(row8 == 1, myh, 0.0))
    zero8, one8 = jnp.zeros((8, NZ), F32), jnp.ones((8, NZ), F32)
    e_scale, h_scale = 0.5 / HALF, 0.5 * HALF

    def halo(ref, i, x):
        return ref[ds(i * 128 + x * 8, 8), :]

    def x_side(i, x):
        if x == 0:
            return -xlo[ds(i * CY, CY), :] * mxl
        return xhi[ds(i * CY, CY), :] * mxh

    wg, yl = one8, one8
    ys = [jnp.zeros((ROWS, NZ), F32)] * 6
    for x in range(CX):
        fh = [halo(ht, c, x) for c in range(6)]
        dx, dy, dz = {}, {}, {}
        for c in XC:
            up = halo(ht, c, x + 1) if x < CX - 1 else zero8
            down = halo(ht, c, x - 1) if x > 0 else zero8
            dx[c] = up - down
        for i, c in enumerate(YC):
            dy[c] = halo(hu, i, x) - halo(hd, i, x)
        for c in (0, 1, 3, 4):
            dz[c] = diff_z(fh[c])
        s_h = halo(he, 0, x) * (1.0 / (HALF * HALF))
        right_h = right_sides(fh, s_h, dx, dy, dz)
        w = s_h + wg
        g_h = 1.0 / (1.0 + w)
        wg = w * g_h
        yl = yl * g_h
        gs[ds(x * 8, 8), :] = g_h
        lsp_h[ds(x * 8, 8), :] = yl
        s = scaled[ds(x * CY, CY), :]
        g = jnp.concatenate([gxs[ds(x * CY, CY), :], g_h], axis=0)
        own = [right[ds((c * CX + x) * CY, CY), :] for c in range(6)]
        if x in (0, CX - 1):
            own[1] = own[1] - e_scale * x_side(3, x)
            own[2] = own[2] + e_scale * x_side(2, x)
            own[4] = own[4] + h_scale * s * x_side(1, x)
            own[5] = own[5] - h_scale * s * x_side(0, x)
        side = {}
        for c in YC:
            low = jnp.where(row8 == 0, -fh[c][0:1], 0.0)
            high = jnp.where(row8 == 7, fh[c][1:2], 0.0)
            side[c] = (low, high)

        def at_rows(value, weight, c):
            low, high = side[c]
            return jnp.concatenate(
                [value[:8] + weight[:8] * low, value[8:16], value[16:] + weight[16:] * high], axis=0
            )

        h_weight = h_scale * s
        e_weight = jnp.full((CY, NZ), e_scale, F32)
        own[0] = at_rows(own[0], e_weight, 5)
        own[2] = at_rows(own[2], -e_weight, 3)
        own[3] = at_rows(own[3], -h_weight, 2)
        own[5] = at_rows(own[5], h_weight, 0)
        for c in range(6):
            r = jnp.concatenate([own[c], right_h[c] * inside], axis=0)
            ys[c] = (r + ys[c]) * g
            sol[ds((c * CX + x) * ROWS, ROWS), :] = ys[c]
    tail = list(ys)
    ul, ur, us = zero8, one8, [jnp.zeros((ROWS, NZ), F32)] * 6
    right_last = None
    for x in reversed(range(CX)):
        g_h = gs[ds(x * 8, 8), :]
        g = jnp.concatenate([gxs[ds(x * CY, CY), :], g_h], axis=0)
        ul = lsp_h[ds(x * 8, 8), :] + g_h * ul
        ur = g_h * ur
        if x == CX - 1:
            right_last = ur
        lsp_h[ds(x * 8, 8), :] = ul
        rsp_h[ds(x * 8, 8), :] = ur
        for c in range(6):
            here = ds((c * CX + x) * ROWS, ROWS)
            us[c] = sol[here, :] + g * us[c]
            sol[here, :] = us[c]
    lead = us
    last = CX - 1
    left_first = jnp.concatenate([lsp[ds(0, CY), :], ul], axis=0)
    right_first = jnp.concatenate([rsp[ds(0, CY), :], ur], axis=0)
    right_last = jnp.concatenate([rsp[ds(last * CY, CY), :], right_last], axis=0)

    def with_halo(value, extra):
        return jnp.concatenate([value[:CY], extra], axis=0)

    lead_rows, tail_rows = list(lead), list(tail)
    lead_rows[1] = with_halo(lead[1], halo(ht, 1, 0))
    tail_rows[1] = with_halo(tail[1], halo(ht, 1, last))
    lead_rows[4] = with_halo(lead[4], halo(he, 0, 0) * e_scale)
    tail_rows[4] = with_halo(tail[4], halo(he, 0, last) * e_scale)
    lead_rows[2] = with_halo(lead[2], lead[2][CY:] + e_scale * halo(ht, 4, 0))
    tail_rows[2] = with_halo(tail[2], tail[2][CY:] - e_scale * halo(ht, 4, last))
    for c in range(6):
        send[ds(c, ROWS, 16), :] = lead_rows[c]
        send[ds(8 + c, ROWS, 16), :] = tail_rows[c]
    send[ds(6, ROWS, 16), :] = left_first
    send[ds(7, ROWS, 16), :] = right_first
    send[ds(14, ROWS, 16), :] = right_first
    send[ds(15, ROWS, 16), :] = right_last


def join_body(rec, back, phis, psis, ms, ns):
    gx = lax.axis_index("gx")
    row8 = row_of((8, NZ))
    shifted = (row8 == 5) & ((gx == CY) | (gx == CY + 1))

    def line(b, k):
        return jnp.broadcast_to(rec[ds(b * 16 + k, 1), :], (8, NZ))

    def shifts(b):
        low = high = jnp.zeros((8, NZ), F32)
        if b > 0:
            low = jnp.where(shifted, line(b, 4) * line(b - 1, 9), 0.0)
        if b < NB - 1:
            high = jnp.where(shifted, -line(b, 12) * line(b + 1, 1), 0.0)
        return low, high

    m = n = jnp.zeros((8, NZ), F32)
    for b in range(NB):
        low, high = shifts(b)
        a, cross, d = line(b, 6), line(b, 7), line(b, 15)
        p = rec[ds(b * 16, 8), :] + a * low + cross * high
        q = rec[ds(b * 16 + 8, 8), :] + cross * low + d * high
        ms[ds(b * 8, 8), :] = m
        ns[ds(b * 8, 8), :] = n
        gain = 1.0 / (1.0 - a * n)
        phi = gain * (p + a * m)
        psi = gain * cross
        phis[ds(b * 8, 8), :] = phi
        psis[ds(b * 8, 8), :] = psi
        m = q + cross * (m + n * phi)
        n = d + cross * (n * psi)
    ahead = jnp.zeros((8, NZ), F32)
    for b in reversed(range(NB)):
        low, high = shifts(b)
        lead = phis[ds(b * 8, 8), :] + psis[ds(b * 8, 8), :] * ahead
        back[ds(b * 16, 8), :] = ms[ds(b * 8, 8), :] + ns[ds(b * 8, 8), :] * lead + low
        back[ds(b * 16 + 8, 8), :] = ahead + high
        ahead = lead


def second_body(
    back, sol, lsp, rsp, lsp_h, rsp_h, scaled, gys, ly, ry, soly, rec, mid, inc, out, r2
):
    for c in range(6):
        inc[ds(c * ROWS, ROWS), :] = back[ds(c, ROWS, 16), :]
        out[ds(c * ROWS, ROWS), :] = back[ds(8 + c, ROWS, 16), :]

    def settle(x, carry):
        at, at_h = ds(pl.multiple_of(x * CY, 8), CY), ds(pl.multiple_of(x * 8, 8), 8)
        left = jnp.concatenate([lsp[at, :], lsp_h[at_h, :]], axis=0)
        right = jnp.concatenate([rsp[at, :], rsp_h[at_h, :]], axis=0)
        for c in range(6):
            here = ds(pl.multiple_of((c * CX + x) * ROWS, 8), ROWS)
            mid[here, :] = (
                sol[here, :]
                + left * inc[ds(c * ROWS, ROWS), :]
                + right * out[ds(c * ROWS, ROWS), :]
            )
        return carry

    lax.fori_loop(0, CX, settle, 0, unroll=2)

    def main(c, x):
        return mid[ds((c * CX + x) * ROWS, CY), :]

    for x in range(CX):
        f = [main(c, x) for c in range(6)]
        dx, dy, dz = {}, {}, {}
        for c in XC:
            up = main(c, x + 1) if x < CX - 1 else out[ds(c * ROWS, CY), :]
            down = main(c, x - 1) if x > 0 else inc[ds(c * ROWS, CY), :]
            dx[c] = up - down
        for c in YC:
            edge = mid[ds((c * CX + x) * ROWS + CY, 8), :]
            dy[c] = diff_y(f[c], edge[0:1], edge[1:2])
        for c in (0, 1, 3, 4):
            dz[c] = diff_z(f[c])
        s = scaled[ds(x * CY, CY), :]
        for c, r in enumerate(right_sides(f, s, dx, dy, dz)):
            r2[ds((c * CX + x) * CY, CY), :] = r

    ys = [jnp.zeros((CX, NZ), F32)] * 6
    for y in range(CY):
        g = gys[ds(y * CX, CX), :]
        for c in range(6):
            here = ds(c * CX * CY + y, CX, CY)
            ys[c] = (r2[here, :] + ys[c]) * g
            r2[here, :] = ys[c]
    for c in range(6):
        rec[ds((8 + c) * CX, CX), :] = ys[c]
    us = [jnp.zeros((CX, NZ), F32)] * 6
    for y in reversed(range(CY)):
        g = gys[ds(y * CX, CX), :]
        for c in range(6):
            here = ds(c * CX * CY + y, CX, CY)
            us[c] = r2[here, :] + g * us[c]
            soly[here, :] = us[c]
    for c in range(6):
        rec[ds(c * CX, CX), :] = us[c]
    rec[ds(6 * CX, CX), :] = ly[ds(0, CX, CY), :]
    rec[ds(7 * CX, CX), :] = ry[ds(0, CX, CY), :]
    rec[ds(14 * CX, CX), :] = ry[ds(0, CX, CY), :]
    rec[ds(15 * CX, CX), :] = ry[ds(CY - 1, CX, CY), :]


WIDTH = NZ // SLOTS


def patches_body(cell_row, owner_row, hot, spread, ranks, table):
    gx, gy = lax.axis_index("gx"), lax.axis_index("gy")
    owner = jnp.broadcast_to(owner_row[...], (PATCH, PATCH))
    rows, lanes = row_of((PATCH, PATCH)), lane_of((PATCH, PATCH))
    owner_col = jnp.sum(jnp.where(rows == lanes, owner, 0), axis=1, keepdims=True)
    earlier = (owner == owner_col) & (rows < lanes)
    rank = jnp.sum(jnp.where(earlier, 1, 0), axis=0, keepdims=True)
    ranks[...] = jnp.broadcast_to(rank, (8, PATCH))
    hot[...] = jnp.where(row_of((NZ, PATCH)) == owner[:NZ], 1.0, 0.0)
    cell = jnp.broadcast_to(cell_row[...], (8, PATCH))
    line = cell >> 7
    x = (line * 2731) >> 16
    px, py, pz = gx * CX + x, gy * CY + line - x * CY, cell & 127
    row8 = row_of((8, PATCH))
    place = jnp.where(row8 == 0, px, jnp.where(row8 == 1, py, jnp.where(row8 == 2, pz, 0)))
    place = place.astype(F32)
    spread[...] = jnp.zeros(spread.shape, F32)
    for k in range(SLOTS):
        spread[ds(k * WIDTH + 8, 8), :] = jnp.where(ranks[...] == k, place, 0.0)
    sector = gx * NBY + gy
    angle = lane_of((8, NZ)).astype(F32)
    sin_theta, cos_theta = sine_cosine(math.pi * (angle + 0.5) / NZ)
    turn = jnp.full((8, NZ), sector, jnp.int32).astype(F32) * (2.0 * math.pi / (NB * NBY))
    sin_phi, cos_phi = sine_cosine(turn)
    table[ds(0, 8), :] = KAPPA * sin_theta * cos_phi
    table[ds(8, 8), :] = KAPPA * sin_theta * sin_phi
    table[ds(16, 8), :] = KAPPA * cos_theta


def finish_body(
    rec0, rec1, rec2, rec3, soly, ly, ry, cell, hot, static, ranks, new, send,
    value_of, inc, out, table, spread, sem,
):
    gy = lax.axis_index("gy")

    def get(rec, k):
        return rec[ds(k * CX, CX), :]

    zero = jnp.zeros((CX, NZ), F32)

    def sweep(order, up):
        m, n = [zero] * 6, zero
        near, far, own, other = (8, 0, 15, 6) if up else (0, 8, 6, 15)
        for rec, valid in order:
            cross = get(rec, 7)
            gain = 1.0 / (1.0 - get(rec, other) * n)
            value = [
                get(rec, near + c)
                + cross * (m[c] + n * (gain * (get(rec, far + c) + get(rec, other) * m[c])))
                for c in range(6)
            ]
            m = [jnp.where(valid, v, 0.0) for v in value]
            n = jnp.where(valid, get(rec, own) + cross * (n * (gain * cross)), 0.0)
        return m, n

    below, below_gain = sweep([(rec3, gy >= 3), (rec2, gy >= 2), (rec1, gy >= 1)], True)
    above, above_gain = sweep([(rec1, gy <= 0), (rec2, gy <= 1), (rec3, gy <= 2)], False)
    a, cross, d = get(rec0, 6), get(rec0, 7), get(rec0, 15)
    ll, lt = 1.0 - a * below_gain, -cross * above_gain
    tl, tt = -cross * below_gain, 1.0 - d * above_gain
    over = 1.0 / (ll * tt - lt * tl)
    for c in range(6):
        p = get(rec0, c) + a * below[c] + cross * above[c]
        q = get(rec0, 8 + c) + cross * below[c] + d * above[c]
        lead, tail = (p * tt - lt * q) * over, (ll * q - tl * p) * over
        inc[ds(c * CX, CX), :] = below[c] + below_gain * lead
        out[ds(c * CX, CX), :] = above[c] + above_gain * tail

    copies = []
    for x in range(CX):
        at = ds(x * CY, CY)
        left, right = ly[at, :], ry[at, :]
        for c in range(6):
            here = ds((c * CX + x) * CY, CY)
            value = (
                soly[here, :]
                + left * inc[ds(c * CX + x, 1), :]
                + right * out[ds(c * CX + x, 1), :]
            )
            value_of[here, :] = value
            table[ds(x * (CY * 8) + c, CY, 8), :] = value
        if x % 4 == 3:
            for c in range(6):
                part = ds((c * CX + x - 3) * CY, 4 * CY)
                copy = pltpu.make_async_copy(
                    value_of.at[part, :], new.at[part, :], sem.at[len(copies)]
                )
                copy.start()
                copies.append(copy)

    lane = lane_of((8, NZ))
    halves = []
    for half in range(PATCH // NZ):

        def pick(j, acc):
            at = cell[half * NZ + j]
            values = table[ds(pl.multiple_of((at >> 7) * 8, 8), 8), :]
            moved = pltpu.roll(values, (j - (at & 127)) & 127, 1)
            return jnp.where(lane == j, moved, acc)

        halves.append(lax.fori_loop(0, NZ, pick, jnp.zeros((8, NZ), F32), unroll=PICKS))
    samples = jnp.concatenate(halves, axis=1)
    samples = jnp.where(row_of((8, PATCH)) < 6, samples, 0.0)
    spread[...] = static[...]
    for k in range(SLOTS):
        spread[ds(k * WIDTH, 8), :] = jnp.where(ranks[...] == k, samples, 0.0)
    send[...] = lax.dot_general(
        hot[...], spread[...], (((1,), (1,)), ((), ())),
        precision=lax.Precision.HIGHEST, preferred_element_type=F32,
    )
    for copy in copies:
        copy.wait()


def sine_cosine(v):
    k = jnp.floor(v * (2.0 / math.pi) + 0.5)
    r = ((v - k * 1.5703125) - k * 4.837512969970703125e-4) - k * 7.54978995489188e-8
    z = r * r
    s = ((-1.9515295891e-4 * z + 8.3321608736e-3) * z - 1.6666654611e-1) * z * r + r
    c = ((2.443315711809948e-5 * z - 1.388731625493765e-3) * z + 4.166664568298827e-2) * (z * z)
    c = c - 0.5 * z + 1.0
    q = k.astype(jnp.int32)
    odd = (q & 1) == 1
    sine, cosine = jnp.where(odd, c, s), jnp.where(odd, s, c)
    sine = jnp.where((q & 2) == 2, -sine, sine)
    cosine = jnp.where(((q + 1) & 2) == 2, -cosine, cosine)
    return sine, cosine


def sector_body(recv, table, far):
    values = recv[...]
    flipped = jnp.transpose(values)
    along_x, along_y, along_z = (table[ds(8 * i, 1), :] for i in range(3))
    sums = jnp.zeros((8, 2 * NZ), F32)
    for k in range(SLOTS):
        px, py, pz = (values[:, k * WIDTH + 8 + i : k * WIDTH + 9 + i] for i in range(3))
        sine, cosine = sine_cosine((px * along_x + py * along_y) + pz * along_z)
        sums += jnp.dot(
            flipped[k * WIDTH : k * WIDTH + 8], jnp.concatenate([cosine, sine], axis=1),
            precision=lax.Precision.HIGHEST, preferred_element_type=F32,
        )
    scale = 1.0 / math.sqrt(PATCH)
    far[0:6, :] = sums[0:6, :NZ] * scale
    far[6:12, :] = sums[0:6, NZ:] * scale


def shift(value, axis, by):
    count = lax.axis_size(axis)
    return lax.ppermute(value, axis, [(i, (i + by) % count) for i in range(count)])


def local(fields, material, permittivity, patch_cell, patch_owner):
    f = fields.reshape(6 * CX * CY, NZ)
    mat = material.reshape(CX * CY, NZ)
    plane, cells, block = (len(XC) * CY, NZ), (CX * CY, NZ), (6 * CX * CY, NZ)
    edge, halo = (11 * CX, NZ), (CX * 8, NZ)
    table16 = pltpu.SMEM((16,), F32)
    xh, xl, yh, yl = call(
        edges_body,
        [plane, plane, edge, edge],
        [f, mat, permittivity],
        [pltpu.VMEM(block, F32), pltpu.VMEM(cells, jnp.int32), table16],
        hbm=(0, 1, 2),
        sems=3,
        vmem=VM,
    )
    xlo, xhi = shift(xh, "gx", 1), shift(xl, "gx", -1)
    ylo, yhi = shift(yh, "gy", 1), shift(yl, "gy", -1)
    scaled, right, gxs, lsp, rsp, gys, ly, ry = call(
        inner_body,
        [cells, block] + [cells] * 6,
        [f, mat, permittivity],
        [table16, cells],
        hbm=(2,),
        sems=1,
        cost=COST,
    )
    sol, lsp_h, rsp_h, send = call(
        first_body,
        [(6 * CX * ROWS, NZ), halo, halo, (ROWS * 16, NZ)],
        [f, scaled, right, gxs, lsp, rsp, xlo, xhi, ylo, yhi],
        [(6 * 128, NZ), (4 * 128, NZ), (4 * 128, NZ), halo, halo],
    )
    rec = lax.all_to_all(send.reshape(NB, 16, NZ), "gx", 0, 0, tiled=True)
    (back,) = call(join_body, [(NB * 16, NZ)], [rec.reshape(NB * 16, NZ)], [(NB * 8, NZ)] * 4)
    back = lax.all_to_all(back.reshape(NB, 16, NZ), "gx", 0, 0, tiled=True)
    soly, rec = call(
        second_body,
        [block, (16 * CX, NZ)],
        [back.reshape(NB * 16, NZ), sol, lsp, rsp, lsp_h, rsp_h, scaled, gys, ly, ry],
        [(6 * CX * ROWS, NZ), (6 * ROWS, NZ), (6 * ROWS, NZ), block],
    )
    others = [shift(rec, "gy", k) for k in (1, 2, 3)]
    hot, static, ranks, table = call(
        patches_body,
        [(NZ, PATCH), (NZ, PATCH), jax.ShapeDtypeStruct((8, PATCH), jnp.int32), (24, NZ)],
        [patch_cell.reshape(1, PATCH), patch_owner.reshape(1, PATCH)],
        cost=COST,
    )
    new, send = call(
        finish_body,
        [block, (NB * NBY, NZ)],
        [rec, *others, soly, ly, ry, patch_cell, hot, static, ranks],
        [block, (6 * CX, NZ), (6 * CX, NZ), (CX * CY * 8, NZ), (NZ, PATCH)],
        smem=(7,),
        hbm_outs=(0,),
        sems=24,
    )
    recv = lax.all_to_all(send, ("gx", "gy"), 0, 0, tiled=True)
    (far,) = call(sector_body, [(12, NZ)], [recv, table])
    return new.reshape(6, CX, CY, NZ), far


def solution(mesh):
    return jax.shard_map(
        local,
        mesh=mesh,
        in_specs=(
            P(None, "gx", "gy", None),
            P("gx", "gy", None),
            P(),
            P(("gx", "gy")),
            P(("gx", "gy"), None),
        ),
        out_specs=(P(None, "gx", "gy", None), P(None, ("gx", "gy"))),
        check_vma=False,
    )
```

```python
import math

import jax
import jax.numpy as jnp
from jax import lax
from jax.experimental import pallas as pl
from jax.experimental.pallas import tpu as pltpu
from jax.sharding import PartitionSpec as P

F32 = jnp.float32
BF16 = jnp.bfloat16
CX, CY, NZ = 16, 24, 128
NB = 32
NBY = 4
ROWS = 32
HALF = 32.0
XC = (1, 2, 4, 5)
YC = (0, 2, 3, 5)
SLOTS = 4
PATCH = 256
KAPPA = 0.5
EDGES = (CY - 1, CY - 2, 0, 1)
PICKS = 32
COST = 4_000_000
VM = 56


def ds(start, size, stride=None):
    return pl.ds(start, size) if stride is None else pl.ds(start, size, stride=stride)


def call(body, outs, args, scratch=(), smem=(), hbm=(), hbm_outs=(), sems=0, cost=0, vmem=40, pinned=False):
    def place(i, slow):
        if i in slow:
            return pl.BlockSpec(memory_space=pltpu.HBM)
        return pl.BlockSpec(memory_space=pltpu.SMEM if slow is hbm and i in smem else pltpu.VMEM)

    shapes = [o if isinstance(o, jax.ShapeDtypeStruct) else jax.ShapeDtypeStruct(o, F32) for o in outs]
    if pinned:
        shapes = [pltpu.VMEM(o.shape, o.dtype) for o in shapes]
    space = [o if not isinstance(o, tuple) else pltpu.VMEM(o, F32) for o in scratch]
    if sems:
        space.append(pltpu.SemaphoreType.DMA((sems,)))
    estimate = None
    if cost:
        estimate = pl.CostEstimate(flops=cost, bytes_accessed=cost, transcendentals=0)
    return pl.pallas_call(
        body,
        out_shape=shapes,
        in_specs=[place(i, hbm) for i in range(len(args))],
        out_specs=[place(i, hbm_outs) for i in range(len(outs))],
        scratch_shapes=space,
        cost_estimate=estimate,
        compiler_params=pltpu.CompilerParams(vmem_limit_bytes=vmem * 1024 * 1024),
    )(*args)


def flag(cond):
    return jnp.where(cond, 1.0, 0.0).astype(F32)


def row_of(shape):
    return lax.broadcasted_iota(jnp.int32, shape, 0)


def lane_of(shape):
    return lax.broadcasted_iota(jnp.int32, shape, 1)


def diff_z(f):
    lane = lane_of(f.shape)
    up = jnp.where(lane == NZ - 1, 0.0, pltpu.roll(f, NZ - 1, 1))
    down = jnp.where(lane == 0, 0.0, pltpu.roll(f, 1, 1))
    return up - down


def diff_y(f, below, above):
    row = row_of(f.shape)
    up = jnp.where(row == CY - 1, above, pltpu.roll(f, CY - 1, 0))
    down = jnp.where(row == 0, below, pltpu.roll(f, 1, 0))
    return up - down


def right_sides(f, s, dx, dy, dz):
    curl_h = (dy[5] - dz[4], dz[3] - dx[5], dx[4] - dy[3])
    curl_e = (dy[2] - dz[1], dz[0] - dx[2], dx[1] - dy[0])
    electric = [s * f[m] + (0.5 / HALF) * curl_h[m] for m in range(3)]
    magnetic = [s * (f[3 + m] - (0.5 * HALF) * curl_e[m]) for m in range(3)]
    return electric + magnetic


def lookup(m, perm):
    e = jnp.broadcast_to(perm[0], m.shape)
    for k in range(1, 16):
        e = jnp.where(m == k, perm[k], e)
    return e


def edges_body(f, mat, xh, xl, yh, yl, rows, mats, sem):
    copies = []

    def fetch(source, target):
        copy = pltpu.make_async_copy(source, target, sem.at[len(copies)])
        copy.start()
        copies.append(copy)

    for i, y in enumerate(EDGES):
        fetch(f.at[:, ds(y, 1), :], rows.at[i])
    for i, y in enumerate((CY - 1, 0)):
        fetch(mat.at[:, ds(y, 1), :], mats.at[i])
    for i, c in enumerate(XC):
        fetch(f.at[c * CX + CX - 1], xh.at[ds(i * CY, CY), :])
        fetch(f.at[c * CX], xl.at[ds(i * CY, CY), :])
    for copy in copies:
        copy.wait()
    for k, out in enumerate((yh, yl)):
        for c in range(6):
            out[ds(c * CX, CX), :] = rows[2 * k, ds(c * CX, CX), 0, :]
        for i, c in enumerate(YC):
            out[ds((6 + i) * CX, CX), :] = rows[2 * k + 1, ds(c * CX, CX), 0, :]
        out[ds(10 * CX, CX), :] = mats[k, :, 0, :].astype(F32)


def inner_body(
    f, mat, perm_hbm, scaled, right, gx_out, lsp, rsp, gy_out, ly, ry, perm_rows, perm, yls, sem
):
    copy = pltpu.make_async_copy(perm_hbm, perm, sem.at[0])
    copy.start()
    copy.wait()
    for k in range(16):
        perm_rows[ds(k, 1), :] = jnp.full((1, NZ), perm[k], F32)

    def main(c, x):
        return f[ds((c * CX + x) * CY, CY), :]

    one, zero = jnp.ones((CY, NZ), F32), jnp.zeros((CY, NZ), F32)
    wg, yl = one, one
    for x in range(CX):
        at = ds(x * CY, CY)
        s = lookup(mat[at, :], perm) * (1.0 / (HALF * HALF))
        scaled[at, :] = s
        w = s + wg
        g = 1.0 / (1.0 + w)
        wg = w * g
        gx_out[at, :] = g
        yl = yl * g
        lsp[at, :] = yl
        fm = [main(c, x) for c in range(6)]
        dx, dy, dz = {}, {}, {}
        for c in XC:
            up = main(c, x + 1) if x < CX - 1 else zero
            down = main(c, x - 1) if x > 0 else zero
            dx[c] = up - down
        for c in YC:
            dy[c] = diff_y(fm[c], 0.0, 0.0)
        for c in (0, 1, 3, 4):
            dz[c] = diff_z(fm[c])
        for c, r in enumerate(right_sides(fm, s, dx, dy, dz)):
            right[ds((c * CX + x) * CY, CY), :] = r
    ul, ur = zero, one
    for x in reversed(range(CX)):
        at = ds(x * CY, CY)
        g = gx_out[at, :]
        ul = lsp[at, :] + g * ul
        ur = g * ur
        lsp[at, :] = ul
        rsp[at, :] = ur
    one, zero = jnp.ones((CX, NZ), F32), jnp.zeros((CX, NZ), F32)
    wg, yl = one, one
    for y in range(CY):
        w = scaled[ds(y, CX, CY), :] + wg
        g = 1.0 / (1.0 + w)
        wg = w * g
        gy_out[ds(y * CX, CX), :] = g
        yl = yl * g
        yls[ds(y * CX, CX), :] = yl
    ul, ur = zero, one
    for y in reversed(range(CY)):
        g = gy_out[ds(y * CX, CX), :]
        ul = yls[ds(y * CX, CX), :] + g * ul
        ur = g * ur
        ly[ds(y, CX, CY), :] = ul
        ry[ds(y, CX, CY), :] = ur


def first_body(
    f, scaled, right, gxs, lsp, rsp, xlo, xhi, ylo, yhi, perm_rows,
    sol, lsp_h, rsp_h, send, ht, hu, hd, he, gs,
):
    gx, gy = lax.axis_index("gx"), lax.axis_index("gy")
    mxl, mxh = flag(gx > 0), flag(gx < NB - 1)
    myl, myh = flag(gy > 0), flag(gy < NBY - 1)
    ht[...] = jnp.zeros(ht.shape, F32)
    hu[...] = jnp.zeros(hu.shape, F32)
    hd[...] = jnp.zeros(hd.shape, F32)
    he[...] = jnp.ones(he.shape, F32)
    for c in range(6):
        ht[ds(c * 128, CX, 8), :] = ylo[ds(c * CX, CX), :] * myl
        ht[ds(c * 128 + 1, CX, 8), :] = yhi[ds(c * CX, CX), :] * myh
    for i, c in enumerate(YC):
        hu[ds(i * 128, CX, 8), :] = f[ds(c * CX * CY, CX, CY), :]
        hu[ds(i * 128 + 1, CX, 8), :] = yhi[ds((6 + i) * CX, CX), :] * myh
        hd[ds(i * 128, CX, 8), :] = ylo[ds((6 + i) * CX, CX), :] * myl
        hd[ds(i * 128 + 1, CX, 8), :] = f[ds(c * CX * CY + CY - 1, CX, CY), :]
    perm = [perm_rows[ds(k, 1), :] for k in range(16)]
    he[ds(0, CX, 8), :] = jnp.where(myl > 0, lookup(ylo[ds(10 * CX, CX), :], perm), 1.0)
    he[ds(1, CX, 8), :] = jnp.where(myh > 0, lookup(yhi[ds(10 * CX, CX), :], perm), 1.0)
    row8 = row_of((8, NZ))
    inside = jnp.where(row8 == 0, myl, jnp.where(row8 == 1, myh, 0.0))
    zero8, one8 = jnp.zeros((8, NZ), F32), jnp.ones((8, NZ), F32)
    e_scale, h_scale = 0.5 / HALF, 0.5 * HALF

    def halo(ref, i, x):
        return ref[ds(i * 128 + x * 8, 8), :]

    def x_side(i, x):
        if x == 0:
            return -xlo[ds(i * CY, CY), :] * mxl
        return xhi[ds(i * CY, CY), :] * mxh

    wg, yl = one8, one8
    ys = [jnp.zeros((ROWS, NZ), F32)] * 6
    for x in range(CX):
        fh = [halo(ht, c, x) for c in range(6)]
        dx, dy, dz = {}, {}, {}
        for c in XC:
            up = halo(ht, c, x + 1) if x < CX - 1 else zero8
            down = halo(ht, c, x - 1) if x > 0 else zero8
            dx[c] = up - down
        for i, c in enumerate(YC):
            dy[c] = halo(hu, i, x) - halo(hd, i, x)
        for c in (0, 1, 3, 4):
            dz[c] = diff_z(fh[c])
        s_h = halo(he, 0, x) * (1.0 / (HALF * HALF))
        right_h = right_sides(fh, s_h, dx, dy, dz)
        w = s_h + wg
        g_h = 1.0 / (1.0 + w)
        wg = w * g_h
        yl = yl * g_h
        gs[ds(x * 8, 8), :] = g_h
        lsp_h[ds(x * 8, 8), :] = yl
        s = scaled[ds(x * CY, CY), :]
        g = jnp.concatenate([gxs[ds(x * CY, CY), :], g_h], axis=0)
        own = [right[ds((c * CX + x) * CY, CY), :] for c in range(6)]
        if x in (0, CX - 1):
            own[1] = own[1] - e_scale * x_side(3, x)
            own[2] = own[2] + e_scale * x_side(2, x)
            own[4] = own[4] + h_scale * s * x_side(1, x)
            own[5] = own[5] - h_scale * s * x_side(0, x)
        side = {}
        for c in YC:
            low = jnp.where(row8 == 0, -fh[c][0:1], 0.0)
            high = jnp.where(row8 == 7, fh[c][1:2], 0.0)
            side[c] = (low, high)

        def at_rows(value, weight, c):
            low, high = side[c]
            return jnp.concatenate(
                [value[:8] + weight[:8] * low, value[8:16], value[16:] + weight[16:] * high], axis=0
            )

        h_weight = h_scale * s
        e_weight = jnp.full((CY, NZ), e_scale, F32)
        own[0] = at_rows(own[0], e_weight, 5)
        own[2] = at_rows(own[2], -e_weight, 3)
        own[3] = at_rows(own[3], -h_weight, 2)
        own[5] = at_rows(own[5], h_weight, 0)
        for c in range(6):
            r = jnp.concatenate([own[c], right_h[c] * inside], axis=0)
            ys[c] = (r + ys[c]) * g
            sol[ds((c * CX + x) * ROWS, ROWS), :] = ys[c]
    tail = list(ys)
    ul, ur, us = zero8, one8, [jnp.zeros((ROWS, NZ), F32)] * 6
    right_last = None
    for x in reversed(range(CX)):
        g_h = gs[ds(x * 8, 8), :]
        g = jnp.concatenate([gxs[ds(x * CY, CY), :], g_h], axis=0)
        ul = lsp_h[ds(x * 8, 8), :] + g_h * ul
        ur = g_h * ur
        if x == CX - 1:
            right_last = ur
        lsp_h[ds(x * 8, 8), :] = ul
        rsp_h[ds(x * 8, 8), :] = ur
        for c in range(6):
            here = ds((c * CX + x) * ROWS, ROWS)
            us[c] = sol[here, :] + g * us[c]
            sol[here, :] = us[c]
    lead = us
    last = CX - 1
    left_first = jnp.concatenate([lsp[ds(0, CY), :], ul], axis=0)
    right_first = jnp.concatenate([rsp[ds(0, CY), :], ur], axis=0)
    right_last = jnp.concatenate([rsp[ds(last * CY, CY), :], right_last], axis=0)

    def with_halo(value, extra):
        return jnp.concatenate([value[:CY], extra], axis=0)

    lead_rows, tail_rows = list(lead), list(tail)
    lead_rows[1] = with_halo(lead[1], halo(ht, 1, 0))
    tail_rows[1] = with_halo(tail[1], halo(ht, 1, last))
    lead_rows[4] = with_halo(lead[4], halo(he, 0, 0) * e_scale)
    tail_rows[4] = with_halo(tail[4], halo(he, 0, last) * e_scale)
    lead_rows[2] = with_halo(lead[2], lead[2][CY:] + e_scale * halo(ht, 4, 0))
    tail_rows[2] = with_halo(tail[2], tail[2][CY:] - e_scale * halo(ht, 4, last))
    for c in range(6):
        send[ds(c, ROWS, 16), :] = lead_rows[c]
        send[ds(8 + c, ROWS, 16), :] = tail_rows[c]
    send[ds(6, ROWS, 16), :] = left_first
    send[ds(7, ROWS, 16), :] = right_first
    send[ds(14, ROWS, 16), :] = right_first
    send[ds(15, ROWS, 16), :] = right_last


def join_body(rec, back, phis, psis, ms, ns):
    gx = lax.axis_index("gx")
    row8 = row_of((8, NZ))
    shifted = (row8 == 5) & ((gx == CY) | (gx == CY + 1))

    def line(b, k):
        return jnp.broadcast_to(rec[ds(b * 16 + k, 1), :], (8, NZ))

    def shifts(b):
        low = high = jnp.zeros((8, NZ), F32)
        if b > 0:
            low = jnp.where(shifted, line(b, 4) * line(b - 1, 9), 0.0)
        if b < NB - 1:
            high = jnp.where(shifted, -line(b, 12) * line(b + 1, 1), 0.0)
        return low, high

    m = n = jnp.zeros((8, NZ), F32)
    for b in range(NB):
        low, high = shifts(b)
        a, cross, d = line(b, 6), line(b, 7), line(b, 15)
        p = rec[ds(b * 16, 8), :] + a * low + cross * high
        q = rec[ds(b * 16 + 8, 8), :] + cross * low + d * high
        ms[ds(b * 8, 8), :] = m
        ns[ds(b * 8, 8), :] = n
        gain = 1.0 / (1.0 - a * n)
        phi = gain * (p + a * m)
        psi = gain * cross
        phis[ds(b * 8, 8), :] = phi
        psis[ds(b * 8, 8), :] = psi
        m = q + cross * (m + n * phi)
        n = d + cross * (n * psi)
    ahead = jnp.zeros((8, NZ), F32)
    for b in reversed(range(NB)):
        low, high = shifts(b)
        lead = phis[ds(b * 8, 8), :] + psis[ds(b * 8, 8), :] * ahead
        back[ds(b * 16, 8), :] = ms[ds(b * 8, 8), :] + ns[ds(b * 8, 8), :] * lead + low
        back[ds(b * 16 + 8, 8), :] = ahead + high
        ahead = lead


def second_body(
    back, sol, lsp, rsp, lsp_h, rsp_h, scaled, gys, ly, ry, soly, rec, mid, inc, out, r2
):
    for c in range(6):
        inc[ds(c * ROWS, ROWS), :] = back[ds(c, ROWS, 16), :]
        out[ds(c * ROWS, ROWS), :] = back[ds(8 + c, ROWS, 16), :]

    def settle(x, carry):
        at, at_h = ds(pl.multiple_of(x * CY, 8), CY), ds(pl.multiple_of(x * 8, 8), 8)
        left = jnp.concatenate([lsp[at, :], lsp_h[at_h, :]], axis=0)
        right = jnp.concatenate([rsp[at, :], rsp_h[at_h, :]], axis=0)
        for c in range(6):
            here = ds(pl.multiple_of((c * CX + x) * ROWS, 8), ROWS)
            mid[here, :] = (
                sol[here, :]
                + left * inc[ds(c * ROWS, ROWS), :]
                + right * out[ds(c * ROWS, ROWS), :]
            )
        return carry

    lax.fori_loop(0, CX, settle, 0, unroll=2)

    def main(c, x):
        return mid[ds((c * CX + x) * ROWS, CY), :]

    for x in range(CX):
        f = [main(c, x) for c in range(6)]
        dx, dy, dz = {}, {}, {}
        for c in XC:
            up = main(c, x + 1) if x < CX - 1 else out[ds(c * ROWS, CY), :]
            down = main(c, x - 1) if x > 0 else inc[ds(c * ROWS, CY), :]
            dx[c] = up - down
        for c in YC:
            edge = mid[ds((c * CX + x) * ROWS + CY, 8), :]
            dy[c] = diff_y(f[c], edge[0:1], edge[1:2])
        for c in (0, 1, 3, 4):
            dz[c] = diff_z(f[c])
        s = scaled[ds(x * CY, CY), :]
        for c, r in enumerate(right_sides(f, s, dx, dy, dz)):
            r2[ds((c * CX + x) * CY, CY), :] = r

    ys = [jnp.zeros((CX, NZ), F32)] * 6
    for y in range(CY):
        g = gys[ds(y * CX, CX), :]
        for c in range(6):
            here = ds(c * CX * CY + y, CX, CY)
            ys[c] = (r2[here, :] + ys[c]) * g
            r2[here, :] = ys[c]
    for c in range(6):
        rec[ds((8 + c) * CX, CX), :] = ys[c]
    us = [jnp.zeros((CX, NZ), F32)] * 6
    for y in reversed(range(CY)):
        g = gys[ds(y * CX, CX), :]
        for c in range(6):
            here = ds(c * CX * CY + y, CX, CY)
            us[c] = r2[here, :] + g * us[c]
            soly[here, :] = us[c]
    for c in range(6):
        rec[ds(c * CX, CX), :] = us[c]
    rec[ds(6 * CX, CX), :] = ly[ds(0, CX, CY), :]
    rec[ds(7 * CX, CX), :] = ry[ds(0, CX, CY), :]
    rec[ds(14 * CX, CX), :] = ry[ds(0, CX, CY), :]
    rec[ds(15 * CX, CX), :] = ry[ds(CY - 1, CX, CY), :]


WIDTH = NZ // SLOTS


def patches_body(cell_row, owner_row, hot, spread, ranks, table):
    gx, gy = lax.axis_index("gx"), lax.axis_index("gy")
    owner = jnp.broadcast_to(owner_row[...], (PATCH, PATCH))
    rows, lanes = row_of((PATCH, PATCH)), lane_of((PATCH, PATCH))
    owner_col = jnp.sum(jnp.where(rows == lanes, owner, 0), axis=1, keepdims=True)
    earlier = (owner == owner_col) & (rows < lanes)
    rank = jnp.sum(jnp.where(earlier, 1, 0), axis=0, keepdims=True)
    ranks[...] = jnp.broadcast_to(rank, (8, PATCH))
    hot[...] = jnp.where(row_of((NZ, PATCH)) == owner[:NZ], 1.0, 0.0).astype(BF16)
    cell = jnp.broadcast_to(cell_row[...], (8, PATCH))
    line = cell >> 7
    x = (line * 2731) >> 16
    px, py, pz = gx * CX + x, gy * CY + line - x * CY, cell & 127
    row8 = row_of((8, PATCH))
    place = jnp.where(row8 == 0, px, jnp.where(row8 == 1, py, jnp.where(row8 == 2, pz, 0)))
    place = place.astype(F32)
    spread[...] = jnp.zeros(spread.shape, F32)
    for k in range(SLOTS):
        spread[ds(k * WIDTH + 8, 8), :] = jnp.where(ranks[...] == k, place, 0.0)
    sector = gx * NBY + gy
    angle = row_of((NZ, NZ)).astype(F32)
    sin_theta, cos_theta = sine_cosine(math.pi * (angle + 0.5) / NZ)
    turn = jnp.full((8, NZ), sector, jnp.int32).astype(F32) * (2.0 * math.pi / (NB * NBY))
    sin_phi, cos_phi = sine_cosine(turn)
    table[ds(0, NZ), :] = KAPPA * sin_theta * cos_phi[0:1]
    table[ds(NZ, NZ), :] = KAPPA * sin_theta * sin_phi[0:1]
    table[ds(2 * NZ, NZ), :] = KAPPA * cos_theta


def finish_body(
    rec0, rec1, rec2, rec3, soly, ly, ry, cell_hbm, hot, static, ranks, new, send,
    value_of, inc, out, table, spread, cell, sem,
):
    gy = lax.axis_index("gy")
    cells = pltpu.make_async_copy(cell_hbm, cell, sem.at[24])
    cells.start()

    def get(rec, k):
        return rec[ds(k * CX, CX), :]

    zero = jnp.zeros((CX, NZ), F32)

    def sweep(order, up):
        m, n = [zero] * 6, zero
        near, far, own, other = (8, 0, 15, 6) if up else (0, 8, 6, 15)
        for rec, valid in order:
            cross = get(rec, 7)
            gain = 1.0 / (1.0 - get(rec, other) * n)
            value = [
                get(rec, near + c)
                + cross * (m[c] + n * (gain * (get(rec, far + c) + get(rec, other) * m[c])))
                for c in range(6)
            ]
            m = [jnp.where(valid, v, 0.0) for v in value]
            n = jnp.where(valid, get(rec, own) + cross * (n * (gain * cross)), 0.0)
        return m, n

    below, below_gain = sweep([(rec3, gy >= 3), (rec2, gy >= 2), (rec1, gy >= 1)], True)
    above, above_gain = sweep([(rec1, gy <= 0), (rec2, gy <= 1), (rec3, gy <= 2)], False)
    a, cross, d = get(rec0, 6), get(rec0, 7), get(rec0, 15)
    ll, lt = 1.0 - a * below_gain, -cross * above_gain
    tl, tt = -cross * below_gain, 1.0 - d * above_gain
    over = 1.0 / (ll * tt - lt * tl)
    for c in range(6):
        p = get(rec0, c) + a * below[c] + cross * above[c]
        q = get(rec0, 8 + c) + cross * below[c] + d * above[c]
        lead, tail = (p * tt - lt * q) * over, (ll * q - tl * p) * over
        inc[ds(c * CX, CX), :] = below[c] + below_gain * lead
        out[ds(c * CX, CX), :] = above[c] + above_gain * tail

    copies = []
    for x in range(CX):
        at = ds(x * CY, CY)
        left, right = ly[at, :], ry[at, :]
        for c in range(6):
            here = ds((c * CX + x) * CY, CY)
            value = (
                soly[here, :]
                + left * inc[ds(c * CX + x, 1), :]
                + right * out[ds(c * CX + x, 1), :]
            )
            value_of[here, :] = value
            table[ds(x * (CY * 8) + c, CY, 8), :] = value
        if x % 4 == 3:
            for c in range(6):
                part = ds((c * CX + x - 3) * CY, 4 * CY)
                copy = pltpu.make_async_copy(
                    value_of.at[part, :], new.at[part, :], sem.at[len(copies)]
                )
                copy.start()
                copies.append(copy)

    cells.wait()
    lane = lane_of((8, NZ))
    halves = []
    for half in range(PATCH // NZ):

        def pick(j, acc):
            at = cell[half * NZ + j]
            values = table[ds(pl.multiple_of((at >> 7) * 8, 8), 8), :]
            moved = pltpu.roll(values, (j - (at & 127)) & 127, 1)
            return jnp.where(lane == j, moved, acc)

        halves.append(lax.fori_loop(0, NZ, pick, jnp.zeros((8, NZ), F32), unroll=PICKS))
    samples = jnp.concatenate(halves, axis=1)
    samples = jnp.where(row_of((8, PATCH)) < 6, samples, 0.0)
    spread[...] = static[...]
    for k in range(SLOTS):
        spread[ds(k * WIDTH, 8), :] = jnp.where(ranks[...] == k, samples, 0.0)
    rest, total = spread[...], jnp.zeros((NZ, NZ), F32)
    for _ in range(3):
        part = rest.astype(BF16)
        rest = rest - part.astype(F32)
        total += lax.dot_general(
            hot[...], part, (((1,), (1,)), ((), ())), preferred_element_type=F32
        )
    send[...] = total
    for copy in copies:
        copy.wait()


def sine_cosine(v):
    k = jnp.floor(v * (2.0 / math.pi) + 0.5)
    r = ((v - k * 1.5703125) - k * 4.837512969970703125e-4) - k * 7.54978995489188e-8
    z = r * r
    s = ((-1.9515295891e-4 * z + 8.3321608736e-3) * z - 1.6666654611e-1) * z * r + r
    c = ((2.443315711809948e-5 * z - 1.388731625493765e-3) * z + 4.166664568298827e-2) * (z * z)
    c = c - 0.5 * z + 1.0
    q = k.astype(jnp.int32)
    odd = (q & 1) == 1
    sine, cosine = jnp.where(odd, c, s), jnp.where(odd, s, c)
    sine = jnp.where((q & 2) == 2, -sine, sine)
    cosine = jnp.where(((q + 1) & 2) == 2, -cosine, cosine)
    return sine, cosine


def sector_body(recv, table, far):
    flipped = jnp.transpose(recv[...])
    along = [table[ds(i * NZ, NZ), :] for i in range(3)]
    parts, cosines, sines = [], [], []
    for k in range(SLOTS):
        parts.append(flipped[k * WIDTH : k * WIDTH + 8])
        px, py, pz = (flipped[k * WIDTH + 8 + i : k * WIDTH + 9 + i] for i in range(3))
        sine, cosine = sine_cosine((px * along[0] + py * along[1]) + pz * along[2])
        cosines.append(cosine)
        sines.append(sine)
    value = jnp.concatenate(parts, axis=1)
    wave = jnp.concatenate(
        [jnp.concatenate(cosines, axis=1), jnp.concatenate(sines, axis=1)], axis=0
    )
    value_high = value.astype(BF16)
    value_low = (value - value_high.astype(F32)).astype(BF16)
    wave_high = wave.astype(BF16)
    wave_low = (wave - wave_high.astype(F32)).astype(BF16)
    sums = jnp.zeros((8, 2 * NZ), F32)
    for a, b in ((value_high, wave_high), (value_low, wave_high), (value_high, wave_low)):
        sums += lax.dot_general(a, b, (((1,), (1,)), ((), ())), preferred_element_type=F32)
    scale = 1.0 / math.sqrt(PATCH)
    far[0:6, :] = sums[0:6, :NZ] * scale
    far[6:12, :] = sums[0:6, NZ:] * scale


def shift(value, axis, by):
    count = lax.axis_size(axis)
    return lax.ppermute(value, axis, [(i, (i + by) % count) for i in range(count)])


def local(fields, material, permittivity, patch_cell, patch_owner):
    f = fields.reshape(6 * CX * CY, NZ)
    mat = material.reshape(CX * CY, NZ)
    plane, cells, block = (len(XC) * CY, NZ), (CX * CY, NZ), (6 * CX * CY, NZ)
    edge, halo = (11 * CX, NZ), (CX * 8, NZ)
    table16 = pltpu.SMEM((16,), F32)
    xh, xl, yh, yl = call(
        edges_body,
        [(184, NZ), (184, NZ), edge, edge],
        [fields.reshape(6 * CX, CY, NZ), material],
        [(4, 6 * CX, 1, NZ), pltpu.VMEM((2, CX, 1, NZ), jnp.int32)],
        hbm=(0, 1),
        sems=6 + 2 * len(XC),
        vmem=VM,
        pinned=True,
    )
    xlo, xhi = shift(xh, "gx", 1), shift(xl, "gx", -1)
    ylo, yhi = shift(yh, "gy", 1), shift(yl, "gy", -1)
    scaled, right, gxs, lsp, rsp, gys, ly, ry, perm_rows = call(
        inner_body,
        [cells, block] + [cells] * 6 + [(16, NZ)],
        [f, mat, permittivity],
        [table16, cells],
        hbm=(2,),
        sems=1,
        cost=COST,
    )
    sol, lsp_h, rsp_h, send = call(
        first_body,
        [(6 * CX * ROWS, NZ), halo, halo, (ROWS * 16, NZ)],
        [f, scaled, right, gxs, lsp, rsp, xlo, xhi, ylo, yhi, perm_rows],
        [(6 * 128, NZ), (4 * 128, NZ), (4 * 128, NZ), halo, halo],
    )
    rec = lax.all_to_all(send.reshape(NB, 16, NZ), "gx", 0, 0, tiled=True)
    (back,) = call(join_body, [(NB * 16, NZ)], [rec.reshape(NB * 16, NZ)], [(NB * 8, NZ)] * 4)
    back = lax.all_to_all(back.reshape(NB, 16, NZ), "gx", 0, 0, tiled=True)
    soly, rec = call(
        second_body,
        [block, (16 * CX, NZ)],
        [back.reshape(NB * 16, NZ), sol, lsp, rsp, lsp_h, rsp_h, scaled, gys, ly, ry],
        [(6 * CX * ROWS, NZ), (6 * ROWS, NZ), (6 * ROWS, NZ), block],
    )
    others = [shift(rec, "gy", k) for k in (1, 2, 3)]
    hot, static, ranks, table = call(
        patches_body,
        [
            jax.ShapeDtypeStruct((NZ, PATCH), BF16), (NZ, PATCH),
            jax.ShapeDtypeStruct((8, PATCH), jnp.int32), (3 * NZ, NZ),
        ],
        [patch_cell.reshape(1, PATCH), patch_owner.reshape(1, PATCH)],
        cost=COST,
    )
    new, send = call(
        finish_body,
        [block, (NB * NBY, NZ)],
        [rec, *others, soly, ly, ry, patch_cell, hot, static, ranks],
        [block, (6 * CX, NZ), (6 * CX, NZ), (CX * CY * 8, NZ), (NZ, PATCH)]
        + [pltpu.SMEM((PATCH,), jnp.int32)],
        hbm=(7,),
        hbm_outs=(0,),
        sems=25,
    )
    recv = lax.all_to_all(send, ("gx", "gy"), 0, 0, tiled=True)
    (far,) = call(sector_body, [(12, NZ)], [recv, table])
    return new.reshape(6, CX, CY, NZ), far


def solution(mesh):
    return jax.shard_map(
        local,
        mesh=mesh,
        in_specs=(
            P(None, "gx", "gy", None),
            P("gx", "gy", None),
            P(),
            P(("gx", "gy")),
            P(("gx", "gy"), None),
        ),
        out_specs=(P(None, "gx", "gy", None), P(None, ("gx", "gy"))),
        check_vma=False,
    )
```

```python
import math

import jax
import jax.numpy as jnp
from jax import lax
from jax.experimental import pallas as pl
from jax.experimental.pallas import tpu as pltpu
from jax.sharding import PartitionSpec as P

F32 = jnp.float32
BF16 = jnp.bfloat16
CX, CY, NZ = 16, 24, 128
NB = 32
NBY = 4
ROWS = 32
HALF = 32.0
XC = (1, 2, 4, 5)
YC = (0, 2, 3, 5)
SLOTS = 4
PATCH = 256
KAPPA = 0.5
EDGES = (CY - 1, CY - 2, 0, 1)
PICKS = 32
COST = 4_000_000
OUTS = 1
VM = 56


def ds(start, size, stride=None):
    return pl.ds(start, size) if stride is None else pl.ds(start, size, stride=stride)


def call(body, outs, args, scratch=(), smem=(), hbm=(), hbm_outs=(), sems=0, cost=0, vmem=40, pinned=()):
    def place(i, slow):
        if i in slow:
            return pl.BlockSpec(memory_space=pltpu.HBM)
        return pl.BlockSpec(memory_space=pltpu.SMEM if slow is hbm and i in smem else pltpu.VMEM)

    shapes = [o if isinstance(o, jax.ShapeDtypeStruct) else jax.ShapeDtypeStruct(o, F32) for o in outs]
    shapes = [pltpu.VMEM(o.shape, o.dtype) if i in pinned else o for i, o in enumerate(shapes)]
    space = [o if not isinstance(o, tuple) else pltpu.VMEM(o, F32) for o in scratch]
    if sems:
        space.append(pltpu.SemaphoreType.DMA((sems,)))
    estimate = None
    if cost:
        estimate = pl.CostEstimate(flops=cost, bytes_accessed=cost, transcendentals=0)
    return pl.pallas_call(
        body,
        out_shape=shapes,
        in_specs=[place(i, hbm) for i in range(len(args))],
        out_specs=[place(i, hbm_outs) for i in range(len(outs))],
        scratch_shapes=space,
        cost_estimate=estimate,
        compiler_params=pltpu.CompilerParams(vmem_limit_bytes=vmem * 1024 * 1024),
    )(*args)


def flag(cond):
    return jnp.where(cond, 1.0, 0.0).astype(F32)


def row_of(shape):
    return lax.broadcasted_iota(jnp.int32, shape, 0)


def lane_of(shape):
    return lax.broadcasted_iota(jnp.int32, shape, 1)


def diff_z(f):
    lane = lane_of(f.shape)
    up = jnp.where(lane == NZ - 1, 0.0, pltpu.roll(f, NZ - 1, 1))
    down = jnp.where(lane == 0, 0.0, pltpu.roll(f, 1, 1))
    return up - down


def diff_y(f, below, above):
    row = row_of(f.shape)
    up = jnp.where(row == CY - 1, above, pltpu.roll(f, CY - 1, 0))
    down = jnp.where(row == 0, below, pltpu.roll(f, 1, 0))
    return up - down


def right_sides(f, s, dx, dy, dz):
    curl_h = (dy[5] - dz[4], dz[3] - dx[5], dx[4] - dy[3])
    curl_e = (dy[2] - dz[1], dz[0] - dx[2], dx[1] - dy[0])
    electric = [s * f[m] + (0.5 / HALF) * curl_h[m] for m in range(3)]
    magnetic = [s * (f[3 + m] - (0.5 * HALF) * curl_e[m]) for m in range(3)]
    return electric + magnetic


def lookup(m, perm):
    e = jnp.broadcast_to(perm[0], m.shape)
    for k in range(1, 16):
        e = jnp.where(m == k, perm[k], e)
    return e


def edges_body(f, mat, xh, xl, yh, yl, rows, mats, sem):
    copies = []

    def fetch(source, target):
        copy = pltpu.make_async_copy(source, target, sem.at[len(copies)])
        copy.start()
        copies.append(copy)

    for i, y in enumerate(EDGES):
        fetch(f.at[:, ds(y, 1), :], rows.at[i])
    for i, y in enumerate((CY - 1, 0)):
        fetch(mat.at[:, ds(y, 1), :], mats.at[i])
    for i, c in enumerate(XC):
        fetch(f.at[c * CX + CX - 1], xh.at[ds(i * CY, CY), :])
        fetch(f.at[c * CX], xl.at[ds(i * CY, CY), :])
    for copy in copies:
        copy.wait()
    for k, out in enumerate((yh, yl)):
        for c in range(6):
            out[ds(c * CX, CX), :] = rows[2 * k, ds(c * CX, CX), 0, :]
        for i, c in enumerate(YC):
            out[ds((6 + i) * CX, CX), :] = rows[2 * k + 1, ds(c * CX, CX), 0, :]
        out[ds(10 * CX, CX), :] = mats[k, :, 0, :].astype(F32)


def inner_body(
    f, mat, perm_hbm, scaled, right, gx_out, lsp, rsp, gy_out, ly, ry, perm_rows, perm, yls, sem
):
    copy = pltpu.make_async_copy(perm_hbm, perm, sem.at[0])
    copy.start()
    copy.wait()
    for k in range(16):
        perm_rows[ds(k, 1), :] = jnp.full((1, NZ), perm[k], F32)

    def main(c, x):
        return f[ds((c * CX + x) * CY, CY), :]

    one, zero = jnp.ones((CY, NZ), F32), jnp.zeros((CY, NZ), F32)
    wg, yl = one, one
    for x in range(CX):
        at = ds(x * CY, CY)
        s = lookup(mat[at, :], perm) * (1.0 / (HALF * HALF))
        scaled[at, :] = s
        w = s + wg
        g = 1.0 / (1.0 + w)
        wg = w * g
        gx_out[at, :] = g
        yl = yl * g
        lsp[at, :] = yl
        fm = [main(c, x) for c in range(6)]
        dx, dy, dz = {}, {}, {}
        for c in XC:
            up = main(c, x + 1) if x < CX - 1 else zero
            down = main(c, x - 1) if x > 0 else zero
            dx[c] = up - down
        for c in YC:
            dy[c] = diff_y(fm[c], 0.0, 0.0)
        for c in (0, 1, 3, 4):
            dz[c] = diff_z(fm[c])
        for c, r in enumerate(right_sides(fm, s, dx, dy, dz)):
            right[ds((c * CX + x) * CY, CY), :] = r
    ul, ur = zero, one
    for x in reversed(range(CX)):
        at = ds(x * CY, CY)
        g = gx_out[at, :]
        ul = lsp[at, :] + g * ul
        ur = g * ur
        lsp[at, :] = ul
        rsp[at, :] = ur
    one, zero = jnp.ones((CX, NZ), F32), jnp.zeros((CX, NZ), F32)
    wg, yl = one, one
    for y in range(CY):
        w = scaled[ds(y, CX, CY), :] + wg
        g = 1.0 / (1.0 + w)
        wg = w * g
        gy_out[ds(y * CX, CX), :] = g
        yl = yl * g
        yls[ds(y * CX, CX), :] = yl
    ul, ur = zero, one
    for y in reversed(range(CY)):
        g = gy_out[ds(y * CX, CX), :]
        ul = yls[ds(y * CX, CX), :] + g * ul
        ur = g * ur
        ly[ds(y, CX, CY), :] = ul
        ry[ds(y, CX, CY), :] = ur


def first_body(
    f, scaled, right, gxs, lsp, rsp, xlo, xhi, ylo, yhi, perm_rows,
    sol, lsp_h, rsp_h, send, ht, hu, hd, he, gs,
):
    gx, gy = lax.axis_index("gx"), lax.axis_index("gy")
    mxl, mxh = flag(gx > 0), flag(gx < NB - 1)
    myl, myh = flag(gy > 0), flag(gy < NBY - 1)
    ht[...] = jnp.zeros(ht.shape, F32)
    hu[...] = jnp.zeros(hu.shape, F32)
    hd[...] = jnp.zeros(hd.shape, F32)
    he[...] = jnp.ones(he.shape, F32)
    for c in range(6):
        ht[ds(c * 128, CX, 8), :] = ylo[ds(c * CX, CX), :] * myl
        ht[ds(c * 128 + 1, CX, 8), :] = yhi[ds(c * CX, CX), :] * myh
    for i, c in enumerate(YC):
        hu[ds(i * 128, CX, 8), :] = f[ds(c * CX * CY, CX, CY), :]
        hu[ds(i * 128 + 1, CX, 8), :] = yhi[ds((6 + i) * CX, CX), :] * myh
        hd[ds(i * 128, CX, 8), :] = ylo[ds((6 + i) * CX, CX), :] * myl
        hd[ds(i * 128 + 1, CX, 8), :] = f[ds(c * CX * CY + CY - 1, CX, CY), :]
    perm = [perm_rows[ds(k, 1), :] for k in range(16)]
    he[ds(0, CX, 8), :] = jnp.where(myl > 0, lookup(ylo[ds(10 * CX, CX), :], perm), 1.0)
    he[ds(1, CX, 8), :] = jnp.where(myh > 0, lookup(yhi[ds(10 * CX, CX), :], perm), 1.0)
    row8 = row_of((8, NZ))
    inside = jnp.where(row8 == 0, myl, jnp.where(row8 == 1, myh, 0.0))
    zero8, one8 = jnp.zeros((8, NZ), F32), jnp.ones((8, NZ), F32)
    e_scale, h_scale = 0.5 / HALF, 0.5 * HALF

    def halo(ref, i, x):
        return ref[ds(i * 128 + x * 8, 8), :]

    def x_side(i, x):
        if x == 0:
            return -xlo[ds(i * CY, CY), :] * mxl
        return xhi[ds(i * CY, CY), :] * mxh

    wg, yl = one8, one8
    ys = [jnp.zeros((ROWS, NZ), F32)] * 6
    for x in range(CX):
        fh = [halo(ht, c, x) for c in range(6)]
        dx, dy, dz = {}, {}, {}
        for c in XC:
            up = halo(ht, c, x + 1) if x < CX - 1 else zero8
            down = halo(ht, c, x - 1) if x > 0 else zero8
            dx[c] = up - down
        for i, c in enumerate(YC):
            dy[c] = halo(hu, i, x) - halo(hd, i, x)
        for c in (0, 1, 3, 4):
            dz[c] = diff_z(fh[c])
        s_h = halo(he, 0, x) * (1.0 / (HALF * HALF))
        right_h = right_sides(fh, s_h, dx, dy, dz)
        w = s_h + wg
        g_h = 1.0 / (1.0 + w)
        wg = w * g_h
        yl = yl * g_h
        gs[ds(x * 8, 8), :] = g_h
        lsp_h[ds(x * 8, 8), :] = yl
        s = scaled[ds(x * CY, CY), :]
        g = jnp.concatenate([gxs[ds(x * CY, CY), :], g_h], axis=0)
        own = [right[ds((c * CX + x) * CY, CY), :] for c in range(6)]
        if x in (0, CX - 1):
            own[1] = own[1] - e_scale * x_side(3, x)
            own[2] = own[2] + e_scale * x_side(2, x)
            own[4] = own[4] + h_scale * s * x_side(1, x)
            own[5] = own[5] - h_scale * s * x_side(0, x)
        side = {}
        for c in YC:
            low = jnp.where(row8 == 0, -fh[c][0:1], 0.0)
            high = jnp.where(row8 == 7, fh[c][1:2], 0.0)
            side[c] = (low, high)

        def at_rows(value, weight, c):
            low, high = side[c]
            return jnp.concatenate(
                [value[:8] + weight[:8] * low, value[8:16], value[16:] + weight[16:] * high], axis=0
            )

        h_weight = h_scale * s
        e_weight = jnp.full((CY, NZ), e_scale, F32)
        own[0] = at_rows(own[0], e_weight, 5)
        own[2] = at_rows(own[2], -e_weight, 3)
        own[3] = at_rows(own[3], -h_weight, 2)
        own[5] = at_rows(own[5], h_weight, 0)
        for c in range(6):
            r = jnp.concatenate([own[c], right_h[c] * inside], axis=0)
            ys[c] = (r + ys[c]) * g
            sol[ds((c * CX + x) * ROWS, ROWS), :] = ys[c]
    tail = list(ys)
    ul, ur, us = zero8, one8, [jnp.zeros((ROWS, NZ), F32)] * 6
    right_last = None
    for x in reversed(range(CX)):
        g_h = gs[ds(x * 8, 8), :]
        g = jnp.concatenate([gxs[ds(x * CY, CY), :], g_h], axis=0)
        ul = lsp_h[ds(x * 8, 8), :] + g_h * ul
        ur = g_h * ur
        if x == CX - 1:
            right_last = ur
        lsp_h[ds(x * 8, 8), :] = ul
        rsp_h[ds(x * 8, 8), :] = ur
        for c in range(6):
            here = ds((c * CX + x) * ROWS, ROWS)
            us[c] = sol[here, :] + g * us[c]
            sol[here, :] = us[c]
    lead = us
    last = CX - 1
    left_first = jnp.concatenate([lsp[ds(0, CY), :], ul], axis=0)
    right_first = jnp.concatenate([rsp[ds(0, CY), :], ur], axis=0)
    right_last = jnp.concatenate([rsp[ds(last * CY, CY), :], right_last], axis=0)

    def with_halo(value, extra):
        return jnp.concatenate([value[:CY], extra], axis=0)

    lead_rows, tail_rows = list(lead), list(tail)
    lead_rows[1] = with_halo(lead[1], halo(ht, 1, 0))
    tail_rows[1] = with_halo(tail[1], halo(ht, 1, last))
    lead_rows[4] = with_halo(lead[4], halo(he, 0, 0) * e_scale)
    tail_rows[4] = with_halo(tail[4], halo(he, 0, last) * e_scale)
    lead_rows[2] = with_halo(lead[2], lead[2][CY:] + e_scale * halo(ht, 4, 0))
    tail_rows[2] = with_halo(tail[2], tail[2][CY:] - e_scale * halo(ht, 4, last))
    for c in range(6):
        send[ds(c, ROWS, 16), :] = lead_rows[c]
        send[ds(8 + c, ROWS, 16), :] = tail_rows[c]
    send[ds(6, ROWS, 16), :] = left_first
    send[ds(7, ROWS, 16), :] = right_first
    send[ds(14, ROWS, 16), :] = right_first
    send[ds(15, ROWS, 16), :] = right_last


def join_body(rec, back, phis, psis, ms, ns):
    gx = lax.axis_index("gx")
    row8 = row_of((8, NZ))
    shifted = (row8 == 5) & ((gx == CY) | (gx == CY + 1))

    def line(b, k):
        return jnp.broadcast_to(rec[ds(b * 16 + k, 1), :], (8, NZ))

    def shifts(b):
        low = high = jnp.zeros((8, NZ), F32)
        if b > 0:
            low = jnp.where(shifted, line(b, 4) * line(b - 1, 9), 0.0)
        if b < NB - 1:
            high = jnp.where(shifted, -line(b, 12) * line(b + 1, 1), 0.0)
        return low, high

    m = n = jnp.zeros((8, NZ), F32)
    for b in range(NB):
        low, high = shifts(b)
        a, cross, d = line(b, 6), line(b, 7), line(b, 15)
        p = rec[ds(b * 16, 8), :] + a * low + cross * high
        q = rec[ds(b * 16 + 8, 8), :] + cross * low + d * high
        ms[ds(b * 8, 8), :] = m
        ns[ds(b * 8, 8), :] = n
        gain = 1.0 / (1.0 - a * n)
        phi = gain * (p + a * m)
        psi = gain * cross
        phis[ds(b * 8, 8), :] = phi
        psis[ds(b * 8, 8), :] = psi
        m = q + cross * (m + n * phi)
        n = d + cross * (n * psi)
    ahead = jnp.zeros((8, NZ), F32)
    for b in reversed(range(NB)):
        low, high = shifts(b)
        lead = phis[ds(b * 8, 8), :] + psis[ds(b * 8, 8), :] * ahead
        back[ds(b * 16, 8), :] = ms[ds(b * 8, 8), :] + ns[ds(b * 8, 8), :] * lead + low
        back[ds(b * 16 + 8, 8), :] = ahead + high
        ahead = lead


def second_body(
    back, sol, lsp, rsp, lsp_h, rsp_h, scaled, gys, ly, ry, soly, rec, mid, inc, out, r2
):
    for c in range(6):
        inc[ds(c * ROWS, ROWS), :] = back[ds(c, ROWS, 16), :]
        out[ds(c * ROWS, ROWS), :] = back[ds(8 + c, ROWS, 16), :]

    def settle(x, carry):
        at, at_h = ds(pl.multiple_of(x * CY, 8), CY), ds(pl.multiple_of(x * 8, 8), 8)
        left = jnp.concatenate([lsp[at, :], lsp_h[at_h, :]], axis=0)
        right = jnp.concatenate([rsp[at, :], rsp_h[at_h, :]], axis=0)
        for c in range(6):
            here = ds(pl.multiple_of((c * CX + x) * ROWS, 8), ROWS)
            mid[here, :] = (
                sol[here, :]
                + left * inc[ds(c * ROWS, ROWS), :]
                + right * out[ds(c * ROWS, ROWS), :]
            )
        return carry

    lax.fori_loop(0, CX, settle, 0, unroll=2)

    def main(c, x):
        return mid[ds((c * CX + x) * ROWS, CY), :]

    for x in range(CX):
        f = [main(c, x) for c in range(6)]
        dx, dy, dz = {}, {}, {}
        for c in XC:
            up = main(c, x + 1) if x < CX - 1 else out[ds(c * ROWS, CY), :]
            down = main(c, x - 1) if x > 0 else inc[ds(c * ROWS, CY), :]
            dx[c] = up - down
        for c in YC:
            edge = mid[ds((c * CX + x) * ROWS + CY, 8), :]
            dy[c] = diff_y(f[c], edge[0:1], edge[1:2])
        for c in (0, 1, 3, 4):
            dz[c] = diff_z(f[c])
        s = scaled[ds(x * CY, CY), :]
        for c, r in enumerate(right_sides(f, s, dx, dy, dz)):
            r2[ds((c * CX + x) * CY, CY), :] = r

    ys = [jnp.zeros((CX, NZ), F32)] * 6
    for y in range(CY):
        g = gys[ds(y * CX, CX), :]
        for c in range(6):
            here = ds(c * CX * CY + y, CX, CY)
            ys[c] = (r2[here, :] + ys[c]) * g
            r2[here, :] = ys[c]
    for c in range(6):
        rec[ds((8 + c) * CX, CX), :] = ys[c]
    us = [jnp.zeros((CX, NZ), F32)] * 6
    for y in reversed(range(CY)):
        g = gys[ds(y * CX, CX), :]
        for c in range(6):
            here = ds(c * CX * CY + y, CX, CY)
            us[c] = r2[here, :] + g * us[c]
            soly[here, :] = us[c]
    for c in range(6):
        rec[ds(c * CX, CX), :] = us[c]
    rec[ds(6 * CX, CX), :] = ly[ds(0, CX, CY), :]
    rec[ds(7 * CX, CX), :] = ry[ds(0, CX, CY), :]
    rec[ds(14 * CX, CX), :] = ry[ds(CY - 1, CX, CY), :]


WIDTH = NZ // SLOTS


def patches_body(
    cell_row, owner_row, cell_hbm, soly, ly, ry,
    hot, spread, ranks, table, base, z_hot, x_left, x_right, lines, cell, sem,
):
    copy = pltpu.make_async_copy(cell_hbm, cell, sem.at[0])
    copy.start()
    gx, gy = lax.axis_index("gx"), lax.axis_index("gy")
    owner = jnp.broadcast_to(owner_row[...], (PATCH, PATCH))
    rows, lanes = row_of((PATCH, PATCH)), lane_of((PATCH, PATCH))
    owner_col = jnp.sum(jnp.where(rows == lanes, owner, 0), axis=1, keepdims=True)
    earlier = (owner == owner_col) & (rows < lanes)
    rank = jnp.sum(jnp.where(earlier, 1, 0), axis=0, keepdims=True)
    ranks[...] = jnp.broadcast_to(rank, (8, PATCH))
    hot[...] = jnp.where(row_of((NZ, PATCH)) == owner[:NZ], 1.0, 0.0).astype(BF16)
    place = jnp.broadcast_to(cell_row[...], (8, PATCH))
    line, pz = place >> 7, place & 127
    x = (line * 2731) >> 16
    px, py = gx * CX + x, gy * CY + line - x * CY
    row8 = row_of((8, PATCH))
    place = jnp.where(row8 == 0, px, jnp.where(row8 == 1, py, jnp.where(row8 == 2, pz, 0)))
    place = place.astype(F32)
    spread[...] = jnp.zeros(spread.shape, F32)
    for k in range(SLOTS):
        spread[ds(k * WIDTH + 8, 8), :] = jnp.where(ranks[...] == k, place, 0.0)
    sector = gx * NBY + gy
    angle = row_of((NZ, NZ)).astype(F32)
    sin_theta, cos_theta = sine_cosine(math.pi * (angle + 0.5) / NZ)
    turn = jnp.full((8, NZ), sector, jnp.int32).astype(F32) * (2.0 * math.pi / (NB * NBY))
    sin_phi, cos_phi = sine_cosine(turn)
    table[ds(0, NZ), :] = KAPPA * sin_theta * cos_phi[0:1]
    table[ds(NZ, NZ), :] = KAPPA * sin_theta * sin_phi[0:1]
    table[ds(2 * NZ, NZ), :] = KAPPA * cos_theta
    for x_own in range(CX):
        at = ds(x_own * CY, CY)
        for c in range(6):
            lines[ds(x_own * (CY * 8) + c, CY, 8), :] = soly[ds((c * CX + x_own) * CY, CY), :]
        lines[ds(x_own * (CY * 8) + 6, CY, 8), :] = ly[at, :]
        lines[ds(x_own * (CY * 8) + 7, CY, 8), :] = ry[at, :]
    copy.wait()
    lane = lane_of((8, NZ))
    halves = []
    for half in range(PATCH // NZ):

        def pick(j, acc):
            at = cell[half * NZ + j]
            values = lines[ds(pl.multiple_of((at >> 7) * 8, 8), 8), :]
            moved = pltpu.roll(values, (j - (at & 127)) & 127, 1)
            return jnp.where(lane == j, moved, acc)

        halves.append(lax.fori_loop(0, NZ, pick, jnp.zeros((8, NZ), F32), unroll=PICKS))
    samples = jnp.concatenate(halves, axis=1)
    base[...] = jnp.where(row8 < 6, samples, 0.0)
    z_hot[...] = jnp.where(row_of((NZ, PATCH)) == pz[0:1], 1.0, 0.0).astype(BF16)
    here = row_of((CX, PATCH)) == x[0:1]
    x_left[...] = jnp.where(here, samples[6:7], 0.0)
    x_right[...] = jnp.where(here, samples[7:8], 0.0)


def in_parts(value):
    parts = []
    for _ in range(3):
        parts.append(value.astype(BF16))
        value = value - parts[-1].astype(F32)
    return parts


def finish_body(
    rec0, rec1, rec2, rec3, base, z_hot, x_left, x_right, hot, static, ranks, soly, ly, ry,
    new, send, inc, out, spread,
):
    gy = lax.axis_index("gy")

    def get(rec, k):
        return rec[ds(k * CX, CX), :]

    zero = jnp.zeros((CX, NZ), F32)

    def sweep(order, up):
        m, n = [zero] * 6, zero
        near, far, own, other = (8, 0, 14, 6) if up else (0, 8, 6, 14)
        for rec, valid in order:
            cross = get(rec, 7)
            gain = 1.0 / (1.0 - get(rec, other) * n)
            value = [
                get(rec, near + c)
                + cross * (m[c] + n * (gain * (get(rec, far + c) + get(rec, other) * m[c])))
                for c in range(6)
            ]
            m = [jnp.where(valid, v, 0.0) for v in value]
            n = jnp.where(valid, get(rec, own) + cross * (n * (gain * cross)), 0.0)
        return m, n

    below, below_gain = sweep([(rec3, gy >= 3), (rec2, gy >= 2), (rec1, gy >= 1)], True)
    above, above_gain = sweep([(rec1, gy <= 0), (rec2, gy <= 1), (rec3, gy <= 2)], False)
    a, cross, d = get(rec0, 6), get(rec0, 7), get(rec0, 14)
    ll, lt = 1.0 - a * below_gain, -cross * above_gain
    tl, tt = -cross * below_gain, 1.0 - d * above_gain
    over = 1.0 / (ll * tt - lt * tl)
    for c in range(6):
        p = get(rec0, c) + a * below[c] + cross * above[c]
        q = get(rec0, 8 + c) + cross * below[c] + d * above[c]
        lead, tail = (p * tt - lt * q) * over, (ll * q - tl * p) * over
        inc[ds(c * CX, CX), :] = below[c] + below_gain * lead
        out[ds(c * CX, CX), :] = above[c] + above_gain * tail

    reach = jnp.zeros((12 * CX, PATCH), F32)
    for part in in_parts(jnp.concatenate([inc[...], out[...]], axis=0)):
        reach += jnp.dot(part, z_hot[...], preferred_element_type=F32)
    added = []
    for c in range(6):
        low, high = reach[c * CX : (c + 1) * CX], reach[(6 + c) * CX : (7 + c) * CX]
        weighed = low * x_left[...] + high * x_right[...]
        added.append(jnp.sum(weighed, axis=0, keepdims=True))
    samples = base[...] + jnp.concatenate(added + [jnp.zeros((2, PATCH), F32)], axis=0)
    spread[...] = static[...]
    for k in range(SLOTS):
        spread[ds(k * WIDTH, 8), :] = jnp.where(ranks[...] == k, samples, 0.0)
    total = jnp.zeros((NZ, NZ), F32)
    for part in in_parts(spread[...]):
        total += lax.dot_general(
            hot[...], part, (((1,), (1,)), ((), ())), preferred_element_type=F32
        )
    send[...] = total
    for x in range(CX):
        left, right = ly[ds(x * CY, CY), :], ry[ds(x * CY, CY), :]
        for c in range(6):
            here = ds((c * CX + x) * CY, CY)
            new[here, :] = (
                soly[here, :]
                + left * inc[ds(c * CX + x, 1), :]
                + right * out[ds(c * CX + x, 1), :]
            )


def sine_cosine(v):
    k = jnp.floor(v * (2.0 / math.pi) + 0.5)
    r = ((v - k * 1.5703125) - k * 4.837512969970703125e-4) - k * 7.54978995489188e-8
    z = r * r
    s = ((-1.9515295891e-4 * z + 8.3321608736e-3) * z - 1.6666654611e-1) * z * r + r
    c = ((2.443315711809948e-5 * z - 1.388731625493765e-3) * z + 4.166664568298827e-2) * (z * z)
    c = c - 0.5 * z + 1.0
    q = k.astype(jnp.int32)
    odd = (q & 1) == 1
    sine, cosine = jnp.where(odd, c, s), jnp.where(odd, s, c)
    sine = jnp.where((q & 2) == 2, -sine, sine)
    cosine = jnp.where(((q + 1) & 2) == 2, -cosine, cosine)
    return sine, cosine


def sector_body(recv, table, made, far, new, sem):
    copies = []
    for k in range(OUTS):
        part = ds(k * (6 * CX * CY // OUTS), 6 * CX * CY // OUTS)
        copies.append(pltpu.make_async_copy(made.at[part, :], new.at[part, :], sem.at[k]))
        copies[-1].start()
    flipped = jnp.transpose(recv[...])
    along = [table[ds(i * NZ, NZ), :] for i in range(3)]
    parts, cosines, sines = [], [], []
    for k in range(SLOTS):
        parts.append(flipped[k * WIDTH : k * WIDTH + 8])
        px, py, pz = (flipped[k * WIDTH + 8 + i : k * WIDTH + 9 + i] for i in range(3))
        sine, cosine = sine_cosine((px * along[0] + py * along[1]) + pz * along[2])
        cosines.append(cosine)
        sines.append(sine)
    value = jnp.concatenate(parts, axis=1)
    wave = jnp.concatenate(
        [jnp.concatenate(cosines, axis=1), jnp.concatenate(sines, axis=1)], axis=0
    )
    value_high = value.astype(BF16)
    value_low = (value - value_high.astype(F32)).astype(BF16)
    wave_high = wave.astype(BF16)
    wave_low = (wave - wave_high.astype(F32)).astype(BF16)
    sums = jnp.zeros((8, 2 * NZ), F32)
    for a, b in ((value_high, wave_high), (value_low, wave_high), (value_high, wave_low)):
        sums += lax.dot_general(a, b, (((1,), (1,)), ((), ())), preferred_element_type=F32)
    scale = 1.0 / math.sqrt(PATCH)
    far[0:6, :] = sums[0:6, :NZ] * scale
    far[6:12, :] = sums[0:6, NZ:] * scale
    for copy in copies:
        copy.wait()


def shift(value, axis, by):
    count = lax.axis_size(axis)
    return lax.ppermute(value, axis, [(i, (i + by) % count) for i in range(count)])


def local(fields, material, permittivity, patch_cell, patch_owner):
    f = fields.reshape(6 * CX * CY, NZ)
    mat = material.reshape(CX * CY, NZ)
    plane, cells, block = (len(XC) * CY, NZ), (CX * CY, NZ), (6 * CX * CY, NZ)
    edge, halo = (11 * CX, NZ), (CX * 8, NZ)
    table16 = pltpu.SMEM((16,), F32)
    xh, xl, yh, yl = call(
        edges_body,
        [(184, NZ), (184, NZ), edge, edge],
        [fields.reshape(6 * CX, CY, NZ), material],
        [(4, 6 * CX, 1, NZ), pltpu.VMEM((2, CX, 1, NZ), jnp.int32)],
        hbm=(0, 1),
        sems=6 + 2 * len(XC),
        vmem=VM,
        pinned=(0, 1, 2, 3),
    )
    xlo, xhi = shift(xh, "gx", 1), shift(xl, "gx", -1)
    ylo, yhi = shift(yh, "gy", 1), shift(yl, "gy", -1)
    scaled, right, gxs, lsp, rsp, gys, ly, ry, perm_rows = call(
        inner_body,
        [cells, block] + [cells] * 6 + [(16, NZ)],
        [f, mat, permittivity],
        [table16, cells],
        hbm=(2,),
        sems=1,
        cost=COST,
    )
    sol, lsp_h, rsp_h, send = call(
        first_body,
        [(6 * CX * ROWS, NZ), halo, halo, (ROWS * 16, NZ)],
        [f, scaled, right, gxs, lsp, rsp, xlo, xhi, ylo, yhi, perm_rows],
        [(6 * 128, NZ), (4 * 128, NZ), (4 * 128, NZ), halo, halo],
    )
    rec = lax.all_to_all(send.reshape(NB, 16, NZ), "gx", 0, 0, tiled=True)
    (back,) = call(join_body, [(NB * 16, NZ)], [rec.reshape(NB * 16, NZ)], [(NB * 8, NZ)] * 4)
    back = lax.all_to_all(back.reshape(NB, 16, NZ), "gx", 0, 0, tiled=True)
    soly, rec = call(
        second_body,
        [block, (15 * CX, NZ)],
        [back.reshape(NB * 16, NZ), sol, lsp, rsp, lsp_h, rsp_h, scaled, gys, ly, ry],
        [(6 * CX * ROWS, NZ), (6 * ROWS, NZ), (6 * ROWS, NZ), block],
    )
    others = [shift(rec, "gy", k) for k in (1, 2, 3)]
    ints, sampled = jax.ShapeDtypeStruct((8, PATCH), jnp.int32), (CX, PATCH)
    ones = jax.ShapeDtypeStruct((NZ, PATCH), BF16)
    hot, static, ranks, table, base, z_hot, x_left, x_right = call(
        patches_body,
        [ones, (NZ, PATCH), ints, (3 * NZ, NZ), (8, PATCH), ones, sampled, sampled],
        [
            patch_cell.reshape(1, PATCH), patch_owner.reshape(1, PATCH), patch_cell,
            soly, ly, ry,
        ],
        [(CX * CY * 8, NZ), pltpu.SMEM((PATCH,), jnp.int32)],
        hbm=(2,),
        sems=1,
        cost=COST,
    )
    new, send = call(
        finish_body,
        [block, (NB * NBY, NZ)],
        [rec, *others, base, z_hot, x_left, x_right, hot, static, ranks, soly, ly, ry],
        [(6 * CX, NZ), (6 * CX, NZ), (NZ, PATCH)],
        pinned=(0,),
    )
    recv = lax.all_to_all(send, ("gx", "gy"), 0, 0, tiled=True)
    far, new = call(
        sector_body, [(12, NZ), block], [recv, table, new], hbm_outs=(1,), sems=OUTS
    )
    return new.reshape(6, CX, CY, NZ), far


def solution(mesh):
    return jax.shard_map(
        local,
        mesh=mesh,
        in_specs=(
            P(None, "gx", "gy", None),
            P("gx", "gy", None),
            P(),
            P(("gx", "gy")),
            P(("gx", "gy"), None),
        ),
        out_specs=(P(None, "gx", "gy", None), P(None, ("gx", "gy"))),
        check_vma=False,
    )
```

```python
import math

import jax
import jax.numpy as jnp
from jax import lax
from jax.experimental import pallas as pl
from jax.experimental.pallas import tpu as pltpu
from jax.sharding import PartitionSpec as P

F32 = jnp.float32
BF16 = jnp.bfloat16
CX, CY, NZ = 16, 24, 128
NB = 32
NBY = 4
ROWS = 32
HALF = 32.0
XC = (1, 2, 4, 5)
YC = (0, 2, 3, 5)
SLOTS = 4
PATCH = 256
KAPPA = 0.5
EDGES = (CY - 1, CY - 2, 0, 1)
PICKS = 32
COST = 4_000_000
OUTS = 1
VM = 56


def ds(start, size, stride=None):
    return pl.ds(start, size) if stride is None else pl.ds(start, size, stride=stride)


def call(body, outs, args, scratch=(), smem=(), hbm=(), hbm_outs=(), sems=0, cost=0, vmem=40, pinned=()):
    def place(i, slow):
        if i in slow:
            return pl.BlockSpec(memory_space=pltpu.HBM)
        return pl.BlockSpec(memory_space=pltpu.SMEM if slow is hbm and i in smem else pltpu.VMEM)

    shapes = [o if isinstance(o, jax.ShapeDtypeStruct) else jax.ShapeDtypeStruct(o, F32) for o in outs]
    shapes = [pltpu.VMEM(o.shape, o.dtype) if i in pinned else o for i, o in enumerate(shapes)]
    space = [o if not isinstance(o, tuple) else pltpu.VMEM(o, F32) for o in scratch]
    if sems:
        space.append(pltpu.SemaphoreType.DMA((sems,)))
    estimate = None
    if cost:
        estimate = pl.CostEstimate(flops=cost, bytes_accessed=cost, transcendentals=0)
    return pl.pallas_call(
        body,
        out_shape=shapes,
        in_specs=[place(i, hbm) for i in range(len(args))],
        out_specs=[place(i, hbm_outs) for i in range(len(outs))],
        scratch_shapes=space,
        cost_estimate=estimate,
        compiler_params=pltpu.CompilerParams(vmem_limit_bytes=vmem * 1024 * 1024),
    )(*args)


def flag(cond):
    return jnp.where(cond, 1.0, 0.0).astype(F32)


def row_of(shape):
    return lax.broadcasted_iota(jnp.int32, shape, 0)


def lane_of(shape):
    return lax.broadcasted_iota(jnp.int32, shape, 1)


def diff_z(f):
    lane = lane_of(f.shape)
    up = jnp.where(lane == NZ - 1, 0.0, pltpu.roll(f, NZ - 1, 1))
    down = jnp.where(lane == 0, 0.0, pltpu.roll(f, 1, 1))
    return up - down


def diff_y(f, below, above):
    row = row_of(f.shape)
    up = jnp.where(row == CY - 1, above, pltpu.roll(f, CY - 1, 0))
    down = jnp.where(row == 0, below, pltpu.roll(f, 1, 0))
    return up - down


def right_sides(f, s, dx, dy, dz):
    curl_h = (dy[5] - dz[4], dz[3] - dx[5], dx[4] - dy[3])
    curl_e = (dy[2] - dz[1], dz[0] - dx[2], dx[1] - dy[0])
    electric = [s * f[m] + (0.5 / HALF) * curl_h[m] for m in range(3)]
    magnetic = [s * (f[3 + m] - (0.5 * HALF) * curl_e[m]) for m in range(3)]
    return electric + magnetic


def lookup(m, perm):
    e = jnp.broadcast_to(perm[0], m.shape)
    for k in range(1, 16):
        e = jnp.where(m == k, perm[k], e)
    return e


def edges_body(f, mat, xh, xl, yh, yl, rows, mats, sem):
    copies = []

    def fetch(source, target):
        copy = pltpu.make_async_copy(source, target, sem.at[len(copies)])
        copy.start()
        copies.append(copy)

    for i, y in enumerate(EDGES):
        fetch(f.at[:, ds(y, 1), :], rows.at[i])
    for i, y in enumerate((CY - 1, 0)):
        fetch(mat.at[:, ds(y, 1), :], mats.at[i])
    for i, c in enumerate(XC):
        fetch(f.at[c * CX + CX - 1], xh.at[ds(i * CY, CY), :])
        fetch(f.at[c * CX], xl.at[ds(i * CY, CY), :])
    for copy in copies:
        copy.wait()
    for k, out in enumerate((yh, yl)):
        for c in range(6):
            out[ds(c * CX, CX), :] = rows[2 * k, ds(c * CX, CX), 0, :]
        for i, c in enumerate(YC):
            out[ds((6 + i) * CX, CX), :] = rows[2 * k + 1, ds(c * CX, CX), 0, :]
        out[ds(10 * CX, CX), :] = mats[k, :, 0, :].astype(F32)


def inner_body(
    f, mat, perm_hbm, scaled, right, gx_out, lsp, rsp, gy_out, ly, ry, perm_rows, perm, yls, sem
):
    copy = pltpu.make_async_copy(perm_hbm, perm, sem.at[0])
    copy.start()
    copy.wait()
    for k in range(16):
        perm_rows[ds(k, 1), :] = jnp.full((1, NZ), perm[k], F32)

    def main(c, x):
        return f[ds((c * CX + x) * CY, CY), :]

    one, zero = jnp.ones((CY, NZ), F32), jnp.zeros((CY, NZ), F32)
    wg, yl = one, one
    for x in range(CX):
        at = ds(x * CY, CY)
        s = lookup(mat[at, :], perm) * (1.0 / (HALF * HALF))
        scaled[at, :] = s
        w = s + wg
        g = 1.0 / (1.0 + w)
        wg = w * g
        gx_out[at, :] = g
        yl = yl * g
        lsp[at, :] = yl
        fm = [main(c, x) for c in range(6)]
        dx, dy, dz = {}, {}, {}
        for c in XC:
            up = main(c, x + 1) if x < CX - 1 else zero
            down = main(c, x - 1) if x > 0 else zero
            dx[c] = up - down
        for c in YC:
            dy[c] = diff_y(fm[c], 0.0, 0.0)
        for c in (0, 1, 3, 4):
            dz[c] = diff_z(fm[c])
        for c, r in enumerate(right_sides(fm, s, dx, dy, dz)):
            right[ds((c * CX + x) * CY, CY), :] = r
    ul, ur = zero, one
    for x in reversed(range(CX)):
        at = ds(x * CY, CY)
        g = gx_out[at, :]
        ul = lsp[at, :] + g * ul
        ur = g * ur
        lsp[at, :] = ul
        rsp[at, :] = ur
    one, zero = jnp.ones((CX, NZ), F32), jnp.zeros((CX, NZ), F32)
    wg, yl = one, one
    for y in range(CY):
        w = scaled[ds(y, CX, CY), :] + wg
        g = 1.0 / (1.0 + w)
        wg = w * g
        gy_out[ds(y * CX, CX), :] = g
        yl = yl * g
        yls[ds(y * CX, CX), :] = yl
    ul, ur = zero, one
    for y in reversed(range(CY)):
        g = gy_out[ds(y * CX, CX), :]
        ul = yls[ds(y * CX, CX), :] + g * ul
        ur = g * ur
        ly[ds(y, CX, CY), :] = ul
        ry[ds(y, CX, CY), :] = ur


def first_body(
    f, scaled, right, gxs, lsp, rsp, xlo, xhi, ylo, yhi, perm_rows,
    sol, lsp_h, rsp_h, send, ht, hu, hd, he, gs,
):
    gx, gy = lax.axis_index("gx"), lax.axis_index("gy")
    mxl, mxh = flag(gx > 0), flag(gx < NB - 1)
    myl, myh = flag(gy > 0), flag(gy < NBY - 1)
    ht[...] = jnp.zeros(ht.shape, F32)
    hu[...] = jnp.zeros(hu.shape, F32)
    hd[...] = jnp.zeros(hd.shape, F32)
    he[...] = jnp.ones(he.shape, F32)
    for c in range(6):
        ht[ds(c * 128, CX, 8), :] = ylo[ds(c * CX, CX), :] * myl
        ht[ds(c * 128 + 1, CX, 8), :] = yhi[ds(c * CX, CX), :] * myh
    for i, c in enumerate(YC):
        hu[ds(i * 128, CX, 8), :] = f[ds(c * CX * CY, CX, CY), :]
        hu[ds(i * 128 + 1, CX, 8), :] = yhi[ds((6 + i) * CX, CX), :] * myh
        hd[ds(i * 128, CX, 8), :] = ylo[ds((6 + i) * CX, CX), :] * myl
        hd[ds(i * 128 + 1, CX, 8), :] = f[ds(c * CX * CY + CY - 1, CX, CY), :]
    perm = [perm_rows[ds(k, 1), :] for k in range(16)]
    he[ds(0, CX, 8), :] = jnp.where(myl > 0, lookup(ylo[ds(10 * CX, CX), :], perm), 1.0)
    he[ds(1, CX, 8), :] = jnp.where(myh > 0, lookup(yhi[ds(10 * CX, CX), :], perm), 1.0)
    row8 = row_of((8, NZ))
    inside = jnp.where(row8 == 0, myl, jnp.where(row8 == 1, myh, 0.0))
    zero8, one8 = jnp.zeros((8, NZ), F32), jnp.ones((8, NZ), F32)
    e_scale, h_scale = 0.5 / HALF, 0.5 * HALF

    def halo(ref, i, x):
        return ref[ds(i * 128 + x * 8, 8), :]

    def x_side(i, x):
        if x == 0:
            return -xlo[ds(i * CY, CY), :] * mxl
        return xhi[ds(i * CY, CY), :] * mxh

    wg, yl = one8, one8
    ys = [jnp.zeros((ROWS, NZ), F32)] * 6
    for x in range(CX):
        fh = [halo(ht, c, x) for c in range(6)]
        dx, dy, dz = {}, {}, {}
        for c in XC:
            up = halo(ht, c, x + 1) if x < CX - 1 else zero8
            down = halo(ht, c, x - 1) if x > 0 else zero8
            dx[c] = up - down
        for i, c in enumerate(YC):
            dy[c] = halo(hu, i, x) - halo(hd, i, x)
        for c in (0, 1, 3, 4):
            dz[c] = diff_z(fh[c])
        s_h = halo(he, 0, x) * (1.0 / (HALF * HALF))
        right_h = right_sides(fh, s_h, dx, dy, dz)
        w = s_h + wg
        g_h = 1.0 / (1.0 + w)
        wg = w * g_h
        yl = yl * g_h
        gs[ds(x * 8, 8), :] = g_h
        lsp_h[ds(x * 8, 8), :] = yl
        s = scaled[ds(x * CY, CY), :]
        g = jnp.concatenate([gxs[ds(x * CY, CY), :], g_h], axis=0)
        own = [right[ds((c * CX + x) * CY, CY), :] for c in range(6)]
        if x in (0, CX - 1):
            own[1] = own[1] - e_scale * x_side(3, x)
            own[2] = own[2] + e_scale * x_side(2, x)
            own[4] = own[4] + h_scale * s * x_side(1, x)
            own[5] = own[5] - h_scale * s * x_side(0, x)
        side = {}
        for c in YC:
            low = jnp.where(row8 == 0, -fh[c][0:1], 0.0)
            high = jnp.where(row8 == 7, fh[c][1:2], 0.0)
            side[c] = (low, high)

        def at_rows(value, weight, c):
            low, high = side[c]
            return jnp.concatenate(
                [value[:8] + weight[:8] * low, value[8:16], value[16:] + weight[16:] * high], axis=0
            )

        h_weight = h_scale * s
        e_weight = jnp.full((CY, NZ), e_scale, F32)
        own[0] = at_rows(own[0], e_weight, 5)
        own[2] = at_rows(own[2], -e_weight, 3)
        own[3] = at_rows(own[3], -h_weight, 2)
        own[5] = at_rows(own[5], h_weight, 0)
        for c in range(6):
            r = jnp.concatenate([own[c], right_h[c] * inside], axis=0)
            ys[c] = (r + ys[c]) * g
            sol[ds((c * CX + x) * ROWS, ROWS), :] = ys[c]
    tail = list(ys)
    ul, ur, us = zero8, one8, [jnp.zeros((ROWS, NZ), F32)] * 6
    right_last = None
    for x in reversed(range(CX)):
        g_h = gs[ds(x * 8, 8), :]
        g = jnp.concatenate([gxs[ds(x * CY, CY), :], g_h], axis=0)
        ul = lsp_h[ds(x * 8, 8), :] + g_h * ul
        ur = g_h * ur
        if x == CX - 1:
            right_last = ur
        lsp_h[ds(x * 8, 8), :] = ul
        rsp_h[ds(x * 8, 8), :] = ur
        for c in range(6):
            here = ds((c * CX + x) * ROWS, ROWS)
            us[c] = sol[here, :] + g * us[c]
            sol[here, :] = us[c]
    lead = us
    last = CX - 1
    left_first = jnp.concatenate([lsp[ds(0, CY), :], ul], axis=0)
    right_first = jnp.concatenate([rsp[ds(0, CY), :], ur], axis=0)
    right_last = jnp.concatenate([rsp[ds(last * CY, CY), :], right_last], axis=0)

    def with_halo(value, extra):
        return jnp.concatenate([value[:CY], extra], axis=0)

    lead_rows, tail_rows = list(lead), list(tail)
    lead_rows[1] = with_halo(lead[1], halo(ht, 1, 0))
    tail_rows[1] = with_halo(tail[1], halo(ht, 1, last))
    lead_rows[4] = with_halo(lead[4], halo(he, 0, 0) * e_scale)
    tail_rows[4] = with_halo(tail[4], halo(he, 0, last) * e_scale)
    lead_rows[2] = with_halo(lead[2], lead[2][CY:] + e_scale * halo(ht, 4, 0))
    tail_rows[2] = with_halo(tail[2], tail[2][CY:] - e_scale * halo(ht, 4, last))
    for c in range(6):
        send[ds(c, ROWS, 16), :] = lead_rows[c]
        send[ds(8 + c, ROWS, 16), :] = tail_rows[c]
    send[ds(6, ROWS, 16), :] = left_first
    send[ds(7, ROWS, 16), :] = right_first
    send[ds(14, ROWS, 16), :] = right_first
    send[ds(15, ROWS, 16), :] = right_last


def join_body(rec, back, phis, psis, ms, ns):
    gx = lax.axis_index("gx")
    row8 = row_of((8, NZ))
    shifted = (row8 == 5) & ((gx == CY) | (gx == CY + 1))

    def line(b, k):
        return jnp.broadcast_to(rec[ds(b * 16 + k, 1), :], (8, NZ))

    def shifts(b):
        low = high = jnp.zeros((8, NZ), F32)
        if b > 0:
            low = jnp.where(shifted, line(b, 4) * line(b - 1, 9), 0.0)
        if b < NB - 1:
            high = jnp.where(shifted, -line(b, 12) * line(b + 1, 1), 0.0)
        return low, high

    m = n = jnp.zeros((8, NZ), F32)
    for b in range(NB):
        low, high = shifts(b)
        a, cross, d = line(b, 6), line(b, 7), line(b, 15)
        p = rec[ds(b * 16, 8), :] + a * low + cross * high
        q = rec[ds(b * 16 + 8, 8), :] + cross * low + d * high
        ms[ds(b * 8, 8), :] = m
        ns[ds(b * 8, 8), :] = n
        gain = 1.0 / (1.0 - a * n)
        phi = gain * (p + a * m)
        psi = gain * cross
        phis[ds(b * 8, 8), :] = phi
        psis[ds(b * 8, 8), :] = psi
        m = q + cross * (m + n * phi)
        n = d + cross * (n * psi)
    ahead = jnp.zeros((8, NZ), F32)
    for b in reversed(range(NB)):
        low, high = shifts(b)
        lead = phis[ds(b * 8, 8), :] + psis[ds(b * 8, 8), :] * ahead
        back[ds(b * 16, 8), :] = ms[ds(b * 8, 8), :] + ns[ds(b * 8, 8), :] * lead + low
        back[ds(b * 16 + 8, 8), :] = ahead + high
        ahead = lead


def second_body(
    back, sol, lsp, rsp, lsp_h, rsp_h, scaled, gys, ly, ry, r2, rec, mid, inc, out
):
    for c in range(6):
        inc[ds(c * ROWS, ROWS), :] = back[ds(c, ROWS, 16), :]
        out[ds(c * ROWS, ROWS), :] = back[ds(8 + c, ROWS, 16), :]

    def settle(x, carry):
        at, at_h = ds(pl.multiple_of(x * CY, 8), CY), ds(pl.multiple_of(x * 8, 8), 8)
        left = jnp.concatenate([lsp[at, :], lsp_h[at_h, :]], axis=0)
        right = jnp.concatenate([rsp[at, :], rsp_h[at_h, :]], axis=0)
        for c in range(6):
            here = ds(pl.multiple_of((c * CX + x) * ROWS, 8), ROWS)
            mid[here, :] = (
                sol[here, :]
                + left * inc[ds(c * ROWS, ROWS), :]
                + right * out[ds(c * ROWS, ROWS), :]
            )
        return carry

    lax.fori_loop(0, CX, settle, 0, unroll=2)

    def main(c, x):
        return mid[ds((c * CX + x) * ROWS, CY), :]

    for x in range(CX):
        f = [main(c, x) for c in range(6)]
        dx, dy, dz = {}, {}, {}
        for c in XC:
            up = main(c, x + 1) if x < CX - 1 else out[ds(c * ROWS, CY), :]
            down = main(c, x - 1) if x > 0 else inc[ds(c * ROWS, CY), :]
            dx[c] = up - down
        for c in YC:
            edge = mid[ds((c * CX + x) * ROWS + CY, 8), :]
            dy[c] = diff_y(f[c], edge[0:1], edge[1:2])
        for c in (0, 1, 3, 4):
            dz[c] = diff_z(f[c])
        s = scaled[ds(x * CY, CY), :]
        for c, r in enumerate(right_sides(f, s, dx, dy, dz)):
            r2[ds((c * CX + x) * CY, CY), :] = r

    ys = [jnp.zeros((CX, NZ), F32)] * 6
    for y in range(CY):
        g = gys[ds(y * CX, CX), :]
        for c in range(6):
            here = ds(c * CX * CY + y, CX, CY)
            ys[c] = (r2[here, :] + ys[c]) * g
            r2[here, :] = ys[c]
    for c in range(6):
        rec[ds((8 + c) * CX, CX), :] = ys[c]
    us = [jnp.zeros((CX, NZ), F32)] * 6
    for y in reversed(range(CY)):
        g = gys[ds(y * CX, CX), :]
        for c in range(6):
            here = ds(c * CX * CY + y, CX, CY)
            us[c] = r2[here, :] + g * us[c]
    for c in range(6):
        rec[ds(c * CX, CX), :] = us[c]
    rec[ds(6 * CX, CX), :] = ly[ds(0, CX, CY), :]
    rec[ds(7 * CX, CX), :] = ry[ds(0, CX, CY), :]
    rec[ds(14 * CX, CX), :] = ry[ds(CY - 1, CX, CY), :]


WIDTH = NZ // SLOTS


def patches_body(
    cell_row, owner_row, cell_hbm, reduced, gys, ly, ry,
    soly, hot, spread, ranks, table, base, z_hot, x_left, x_right, lines, cell, sem,
):
    copy = pltpu.make_async_copy(cell_hbm, cell, sem.at[0])
    copy.start()
    gx, gy = lax.axis_index("gx"), lax.axis_index("gy")
    owner = jnp.broadcast_to(owner_row[...], (PATCH, PATCH))
    rows, lanes = row_of((PATCH, PATCH)), lane_of((PATCH, PATCH))
    owner_col = jnp.sum(jnp.where(rows == lanes, owner, 0), axis=1, keepdims=True)
    earlier = (owner == owner_col) & (rows < lanes)
    rank = jnp.sum(jnp.where(earlier, 1, 0), axis=0, keepdims=True)
    ranks[...] = jnp.broadcast_to(rank, (8, PATCH))
    hot[...] = jnp.where(row_of((NZ, PATCH)) == owner[:NZ], 1.0, 0.0).astype(BF16)
    place = jnp.broadcast_to(cell_row[...], (8, PATCH))
    line, pz = place >> 7, place & 127
    x = (line * 2731) >> 16
    px, py = gx * CX + x, gy * CY + line - x * CY
    row8 = row_of((8, PATCH))
    place = jnp.where(row8 == 0, px, jnp.where(row8 == 1, py, jnp.where(row8 == 2, pz, 0)))
    place = place.astype(F32)
    spread[...] = jnp.zeros(spread.shape, F32)
    for k in range(SLOTS):
        spread[ds(k * WIDTH + 8, 8), :] = jnp.where(ranks[...] == k, place, 0.0)
    sector = gx * NBY + gy
    angle = row_of((NZ, NZ)).astype(F32)
    sin_theta, cos_theta = sine_cosine(math.pi * (angle + 0.5) / NZ)
    turn = jnp.full((8, NZ), sector, jnp.int32).astype(F32) * (2.0 * math.pi / (NB * NBY))
    sin_phi, cos_phi = sine_cosine(turn)
    table[ds(0, NZ), :] = KAPPA * sin_theta * cos_phi[0:1]
    table[ds(NZ, NZ), :] = KAPPA * sin_theta * sin_phi[0:1]
    table[ds(2 * NZ, NZ), :] = KAPPA * cos_theta
    us = [jnp.zeros((CX, NZ), F32)] * 6
    for y in reversed(range(CY)):
        g = gys[ds(y * CX, CX), :]
        for c in range(6):
            at = ds(c * CX * CY + y, CX, CY)
            us[c] = reduced[at, :] + g * us[c]
            soly[at, :] = us[c]
            lines[ds(y * 8 + c, CX, CY * 8), :] = us[c]
    for x_own in range(CX):
        at = ds(x_own * CY, CY)
        lines[ds(x_own * (CY * 8) + 6, CY, 8), :] = ly[at, :]
        lines[ds(x_own * (CY * 8) + 7, CY, 8), :] = ry[at, :]
    copy.wait()
    lane = lane_of((8, NZ))
    halves = []
    for half in range(PATCH // NZ):

        def pick(j, acc):
            at = cell[half * NZ + j]
            values = lines[ds(pl.multiple_of((at >> 7) * 8, 8), 8), :]
            moved = pltpu.roll(values, (j - (at & 127)) & 127, 1)
            return jnp.where(lane == j, moved, acc)

        halves.append(lax.fori_loop(0, NZ, pick, jnp.zeros((8, NZ), F32), unroll=PICKS))
    samples = jnp.concatenate(halves, axis=1)
    base[...] = jnp.where(row8 < 6, samples, 0.0)
    z_hot[...] = jnp.where(row_of((NZ, PATCH)) == pz[0:1], 1.0, 0.0).astype(BF16)
    here = row_of((CX, PATCH)) == x[0:1]
    x_left[...] = jnp.where(here, samples[6:7], 0.0)
    x_right[...] = jnp.where(here, samples[7:8], 0.0)


def in_parts(value):
    parts = []
    for _ in range(3):
        parts.append(value.astype(BF16))
        value = value - parts[-1].astype(F32)
    return parts


def finish_body(
    rec0, rec1, rec2, rec3, base, z_hot, x_left, x_right, hot, static, ranks, soly, ly, ry,
    new, send, inc, out, spread,
):
    gy = lax.axis_index("gy")

    def get(choices, k):
        value = choices[-1][ds(k * CX, CX), :]
        for at, rec in choices[:-1]:
            value = jnp.where(gy == at, rec[ds(k * CX, CX), :], value)
        return value

    zero = jnp.zeros((CX, NZ), F32)

    def sweep(order, up):
        m, n = [zero] * 6, zero
        near, far, mine, other = (8, 0, 14, 6) if up else (0, 8, 6, 14)
        for rec, valid in order:
            cross = get(rec, 7)
            gain = 1.0 / (1.0 - get(rec, other) * n)
            value = [
                get(rec, near + c)
                + cross * (m[c] + n * (gain * (get(rec, far + c) + get(rec, other) * m[c])))
                for c in range(6)
            ]
            m = [jnp.where(valid, v, old) for v, old in zip(value, m)]
            n = jnp.where(valid, get(rec, mine) + cross * (n * (gain * cross)), n)
        return m, n

    below, below_gain = sweep(
        [
            (((1, rec1), (2, rec2), rec3), gy >= 1),
            (((2, rec3), rec2), gy >= 2),
            ((rec1,), gy >= 3),
        ],
        True,
    )
    above, above_gain = sweep(
        [
            (((0, rec3), (1, rec2), rec1), gy <= 2),
            (((0, rec2), rec3), gy <= 1),
            ((rec1,), gy <= 0),
        ],
        False,
    )
    own = (rec0,)
    a, cross, d = get(own, 6), get(own, 7), get(own, 14)
    ll, lt = 1.0 - a * below_gain, -cross * above_gain
    tl, tt = -cross * below_gain, 1.0 - d * above_gain
    over = 1.0 / (ll * tt - lt * tl)
    for c in range(6):
        p = get(own, c) + a * below[c] + cross * above[c]
        q = get(own, 8 + c) + cross * below[c] + d * above[c]
        lead, tail = (p * tt - lt * q) * over, (ll * q - tl * p) * over
        inc[ds(c * CX, CX), :] = below[c] + below_gain * lead
        out[ds(c * CX, CX), :] = above[c] + above_gain * tail

    reach = jnp.zeros((12 * CX, PATCH), F32)
    for part in in_parts(jnp.concatenate([inc[...], out[...]], axis=0)):
        reach += jnp.dot(part, z_hot[...], preferred_element_type=F32)
    added = []
    for c in range(6):
        low, high = reach[c * CX : (c + 1) * CX], reach[(6 + c) * CX : (7 + c) * CX]
        weighed = low * x_left[...] + high * x_right[...]
        added.append(jnp.sum(weighed, axis=0, keepdims=True))
    samples = base[...] + jnp.concatenate(added + [jnp.zeros((2, PATCH), F32)], axis=0)
    spread[...] = static[...]
    for k in range(SLOTS):
        spread[ds(k * WIDTH, 8), :] = jnp.where(ranks[...] == k, samples, 0.0)
    total = jnp.zeros((NZ, NZ), F32)
    for part in in_parts(spread[...]):
        total += lax.dot_general(
            hot[...], part, (((1,), (1,)), ((), ())), preferred_element_type=F32
        )
    send[...] = total
    for x in range(CX):
        left, right = ly[ds(x * CY, CY), :], ry[ds(x * CY, CY), :]
        for c in range(6):
            here = ds((c * CX + x) * CY, CY)
            new[here, :] = (
                soly[here, :]
                + left * inc[ds(c * CX + x, 1), :]
                + right * out[ds(c * CX + x, 1), :]
            )


def sine_cosine(v):
    k = jnp.floor(v * (2.0 / math.pi) + 0.5)
    r = ((v - k * 1.5703125) - k * 4.837512969970703125e-4) - k * 7.54978995489188e-8
    z = r * r
    s = ((-1.9515295891e-4 * z + 8.3321608736e-3) * z - 1.6666654611e-1) * z * r + r
    c = ((2.443315711809948e-5 * z - 1.388731625493765e-3) * z + 4.166664568298827e-2) * (z * z)
    c = c - 0.5 * z + 1.0
    q = k.astype(jnp.int32)
    odd = (q & 1) == 1
    sine, cosine = jnp.where(odd, c, s), jnp.where(odd, s, c)
    sine = jnp.where((q & 2) == 2, -sine, sine)
    cosine = jnp.where(((q + 1) & 2) == 2, -cosine, cosine)
    return sine, cosine


def sector_body(recv, table, made, far, new, sem):
    copies = []
    for k in range(OUTS):
        part = ds(k * (6 * CX * CY // OUTS), 6 * CX * CY // OUTS)
        copies.append(pltpu.make_async_copy(made.at[part, :], new.at[part, :], sem.at[k]))
        copies[-1].start()
    flipped = jnp.transpose(recv[...])
    along = [table[ds(i * NZ, NZ), :] for i in range(3)]
    parts, cosines, sines = [], [], []
    for k in range(SLOTS):
        parts.append(flipped[k * WIDTH : k * WIDTH + 8])
        px, py, pz = (flipped[k * WIDTH + 8 + i : k * WIDTH + 9 + i] for i in range(3))
        sine, cosine = sine_cosine((px * along[0] + py * along[1]) + pz * along[2])
        cosines.append(cosine)
        sines.append(sine)
    value = jnp.concatenate(parts, axis=1)
    wave = jnp.concatenate(
        [jnp.concatenate(cosines, axis=1), jnp.concatenate(sines, axis=1)], axis=0
    )
    value_high = value.astype(BF16)
    value_low = (value - value_high.astype(F32)).astype(BF16)
    wave_high = wave.astype(BF16)
    wave_low = (wave - wave_high.astype(F32)).astype(BF16)
    sums = jnp.zeros((8, 2 * NZ), F32)
    for a, b in ((value_high, wave_high), (value_low, wave_high), (value_high, wave_low)):
        sums += lax.dot_general(a, b, (((1,), (1,)), ((), ())), preferred_element_type=F32)
    scale = 1.0 / math.sqrt(PATCH)
    far[0:6, :] = sums[0:6, :NZ] * scale
    far[6:12, :] = sums[0:6, NZ:] * scale
    for copy in copies:
        copy.wait()


def shift(value, axis, by):
    count = lax.axis_size(axis)
    return lax.ppermute(value, axis, [(i, (i + by) % count) for i in range(count)])


def local(fields, material, permittivity, patch_cell, patch_owner):
    f = fields.reshape(6 * CX * CY, NZ)
    mat = material.reshape(CX * CY, NZ)
    plane, cells, block = (len(XC) * CY, NZ), (CX * CY, NZ), (6 * CX * CY, NZ)
    edge, halo = (11 * CX, NZ), (CX * 8, NZ)
    table16 = pltpu.SMEM((16,), F32)
    xh, xl, yh, yl = call(
        edges_body,
        [(184, NZ), (184, NZ), edge, edge],
        [fields.reshape(6 * CX, CY, NZ), material],
        [(4, 6 * CX, 1, NZ), pltpu.VMEM((2, CX, 1, NZ), jnp.int32)],
        hbm=(0, 1),
        sems=6 + 2 * len(XC),
        vmem=VM,
        pinned=(0, 1, 2, 3),
    )
    xlo, xhi = shift(xh, "gx", 1), shift(xl, "gx", -1)
    ylo, yhi = shift(yh, "gy", 1), shift(yl, "gy", -1)
    scaled, right, gxs, lsp, rsp, gys, ly, ry, perm_rows = call(
        inner_body,
        [cells, block] + [cells] * 6 + [(16, NZ)],
        [f, mat, permittivity],
        [table16, cells],
        hbm=(2,),
        sems=1,
        cost=COST,
    )
    sol, lsp_h, rsp_h, send = call(
        first_body,
        [(6 * CX * ROWS, NZ), halo, halo, (ROWS * 16, NZ)],
        [f, scaled, right, gxs, lsp, rsp, xlo, xhi, ylo, yhi, perm_rows],
        [(6 * 128, NZ), (4 * 128, NZ), (4 * 128, NZ), halo, halo],
    )
    rec = lax.all_to_all(send.reshape(NB, 16, NZ), "gx", 0, 0, tiled=True)
    (back,) = call(join_body, [(NB * 16, NZ)], [rec.reshape(NB * 16, NZ)], [(NB * 8, NZ)] * 4)
    back = lax.all_to_all(back.reshape(NB, 16, NZ), "gx", 0, 0, tiled=True)
    reduced, rec = call(
        second_body,
        [block, (15 * CX, NZ)],
        [back.reshape(NB * 16, NZ), sol, lsp, rsp, lsp_h, rsp_h, scaled, gys, ly, ry],
        [(6 * CX * ROWS, NZ), (6 * ROWS, NZ), (6 * ROWS, NZ)],
    )
    others = [
        lax.ppermute(rec, "gy", [(i, i ^ k) for i in range(NBY)]) for k in (1, 2, 3)
    ]
    ints, sampled = jax.ShapeDtypeStruct((8, PATCH), jnp.int32), (CX, PATCH)
    ones = jax.ShapeDtypeStruct((NZ, PATCH), BF16)
    soly, hot, static, ranks, table, base, z_hot, x_left, x_right = call(
        patches_body,
        [block, ones, (NZ, PATCH), ints, (3 * NZ, NZ), (8, PATCH), ones, sampled, sampled],
        [
            patch_cell.reshape(1, PATCH), patch_owner.reshape(1, PATCH), patch_cell,
            reduced, gys, ly, ry,
        ],
        [(CX * CY * 8, NZ), pltpu.SMEM((PATCH,), jnp.int32)],
        hbm=(2,),
        sems=1,
        cost=COST,
    )
    new, send = call(
        finish_body,
        [block, (NB * NBY, NZ)],
        [rec, *others, base, z_hot, x_left, x_right, hot, static, ranks, soly, ly, ry],
        [(6 * CX, NZ), (6 * CX, NZ), (NZ, PATCH)],
        pinned=(0,),
    )
    recv = lax.all_to_all(send, ("gx", "gy"), 0, 0, tiled=True)
    far, new = call(
        sector_body, [(12, NZ), block], [recv, table, new], hbm_outs=(1,), sems=OUTS
    )
    return new.reshape(6, CX, CY, NZ), far


def solution(mesh):
    return jax.shard_map(
        local,
        mesh=mesh,
        in_specs=(
            P(None, "gx", "gy", None),
            P("gx", "gy", None),
            P(),
            P(("gx", "gy")),
            P(("gx", "gy"), None),
        ),
        out_specs=(P(None, "gx", "gy", None), P(None, ("gx", "gy"))),
        check_vma=False,
    )
```

```python
import math

import jax
import jax.numpy as jnp
from jax import lax
from jax.experimental import pallas as pl
from jax.experimental.pallas import tpu as pltpu
from jax.sharding import PartitionSpec as P

F32 = jnp.float32
BF16 = jnp.bfloat16
CX, CY, NZ = 16, 24, 128
NB = 32
NBY = 4
ROWS = 32
HALF = 32.0
XC = (1, 2, 4, 5)
YC = (0, 2, 3, 5)
SLOTS = 4
PATCH = 256
KAPPA = 0.5
EDGES = (CY - 1, CY - 2, 0, 1)
PICKS = 32
COST = 4_000_000
OUTS = 1
VM = 56


def ds(start, size, stride=None):
    return pl.ds(start, size) if stride is None else pl.ds(start, size, stride=stride)


def call(body, outs, args, scratch=(), smem=(), hbm=(), hbm_outs=(), sems=0, cost=0, vmem=40, pinned=()):
    def place(i, slow):
        if i in slow:
            return pl.BlockSpec(memory_space=pltpu.HBM)
        return pl.BlockSpec(memory_space=pltpu.SMEM if slow is hbm and i in smem else pltpu.VMEM)

    shapes = [o if isinstance(o, jax.ShapeDtypeStruct) else jax.ShapeDtypeStruct(o, F32) for o in outs]
    shapes = [pltpu.VMEM(o.shape, o.dtype) if i in pinned else o for i, o in enumerate(shapes)]
    space = [o if not isinstance(o, tuple) else pltpu.VMEM(o, F32) for o in scratch]
    if sems:
        space.append(pltpu.SemaphoreType.DMA((sems,)))
    estimate = None
    if cost:
        estimate = pl.CostEstimate(flops=cost, bytes_accessed=cost, transcendentals=0)
    return pl.pallas_call(
        body,
        out_shape=shapes,
        in_specs=[place(i, hbm) for i in range(len(args))],
        out_specs=[place(i, hbm_outs) for i in range(len(outs))],
        scratch_shapes=space,
        cost_estimate=estimate,
        compiler_params=pltpu.CompilerParams(vmem_limit_bytes=vmem * 1024 * 1024),
    )(*args)


def flag(cond):
    return jnp.where(cond, 1.0, 0.0).astype(F32)


def row_of(shape):
    return lax.broadcasted_iota(jnp.int32, shape, 0)


def lane_of(shape):
    return lax.broadcasted_iota(jnp.int32, shape, 1)


def diff_z(f):
    lane = lane_of(f.shape)
    up = jnp.where(lane == NZ - 1, 0.0, pltpu.roll(f, NZ - 1, 1))
    down = jnp.where(lane == 0, 0.0, pltpu.roll(f, 1, 1))
    return up - down


def diff_y(f, below, above):
    row = row_of(f.shape)
    up = jnp.where(row == CY - 1, above, pltpu.roll(f, CY - 1, 0))
    down = jnp.where(row == 0, below, pltpu.roll(f, 1, 0))
    return up - down


def right_sides(f, s, dx, dy, dz):
    curl_h = (dy[5] - dz[4], dz[3] - dx[5], dx[4] - dy[3])
    curl_e = (dy[2] - dz[1], dz[0] - dx[2], dx[1] - dy[0])
    electric = [s * f[m] + (0.5 / HALF) * curl_h[m] for m in range(3)]
    magnetic = [s * (f[3 + m] - (0.5 * HALF) * curl_e[m]) for m in range(3)]
    return electric + magnetic


def lookup(m, perm):
    e = jnp.broadcast_to(perm[0], m.shape)
    for k in range(1, 16):
        e = jnp.where(m == k, perm[k], e)
    return e


def edges_body(f, mat, xh, xl, yh, yl, rows, mats, sem):
    copies = []

    def fetch(source, target):
        copy = pltpu.make_async_copy(source, target, sem.at[len(copies)])
        copy.start()
        copies.append(copy)

    for i, y in enumerate(EDGES):
        fetch(f.at[:, ds(y, 1), :], rows.at[i])
    for i, y in enumerate((CY - 1, 0)):
        fetch(mat.at[:, ds(y, 1), :], mats.at[i])
    for i, c in enumerate(XC):
        fetch(f.at[c * CX + CX - 1], xh.at[ds(i * CY, CY), :])
        fetch(f.at[c * CX], xl.at[ds(i * CY, CY), :])
    for copy in copies:
        copy.wait()
    for k, out in enumerate((yh, yl)):
        for c in range(6):
            out[ds(c * CX, CX), :] = rows[2 * k, ds(c * CX, CX), 0, :]
        for i, c in enumerate(YC):
            out[ds((6 + i) * CX, CX), :] = rows[2 * k + 1, ds(c * CX, CX), 0, :]
        out[ds(10 * CX, CX), :] = mats[k, :, 0, :].astype(F32)


def inner_body(
    f, mat, perm_hbm, scaled, right, gx_out, lsp, rsp, gy_out, ly, ry, perm_rows, perm, yls, sem
):
    copy = pltpu.make_async_copy(perm_hbm, perm, sem.at[0])
    copy.start()
    copy.wait()
    for k in range(16):
        perm_rows[ds(k, 1), :] = jnp.full((1, NZ), perm[k], F32)

    def main(c, x):
        return f[ds((c * CX + x) * CY, CY), :]

    one, zero = jnp.ones((CY, NZ), F32), jnp.zeros((CY, NZ), F32)
    wg, yl = one, one
    for x in range(CX):
        at = ds(x * CY, CY)
        s = lookup(mat[at, :], perm) * (1.0 / (HALF * HALF))
        scaled[at, :] = s
        w = s + wg
        g = 1.0 / (1.0 + w)
        wg = w * g
        gx_out[at, :] = g
        yl = yl * g
        lsp[at, :] = yl
        fm = [main(c, x) for c in range(6)]
        dx, dy, dz = {}, {}, {}
        for c in XC:
            up = main(c, x + 1) if x < CX - 1 else zero
            down = main(c, x - 1) if x > 0 else zero
            dx[c] = up - down
        for c in YC:
            dy[c] = diff_y(fm[c], 0.0, 0.0)
        for c in (0, 1, 3, 4):
            dz[c] = diff_z(fm[c])
        for c, r in enumerate(right_sides(fm, s, dx, dy, dz)):
            right[ds((c * CX + x) * CY, CY), :] = r
    ul, ur = zero, one
    for x in reversed(range(CX)):
        at = ds(x * CY, CY)
        g = gx_out[at, :]
        ul = lsp[at, :] + g * ul
        ur = g * ur
        lsp[at, :] = ul
        rsp[at, :] = ur
    one, zero = jnp.ones((CX, NZ), F32), jnp.zeros((CX, NZ), F32)
    wg, yl = one, one
    for y in range(CY):
        w = scaled[ds(y, CX, CY), :] + wg
        g = 1.0 / (1.0 + w)
        wg = w * g
        gy_out[ds(y * CX, CX), :] = g
        yl = yl * g
        yls[ds(y * CX, CX), :] = yl
    ul, ur = zero, one
    for y in reversed(range(CY)):
        g = gy_out[ds(y * CX, CX), :]
        ul = yls[ds(y * CX, CX), :] + g * ul
        ur = g * ur
        ly[ds(y, CX, CY), :] = ul
        ry[ds(y, CX, CY), :] = ur


def first_body(
    f, scaled, right, gxs, lsp, rsp, xlo, xhi, ylo, yhi, perm_rows,
    sol, lsp_h, rsp_h, send, ht, hu, hd, he, gs,
):
    gx, gy = lax.axis_index("gx"), lax.axis_index("gy")
    mxl, mxh = flag(gx > 0), flag(gx < NB - 1)
    myl, myh = flag(gy > 0), flag(gy < NBY - 1)
    ht[...] = jnp.zeros(ht.shape, F32)
    hu[...] = jnp.zeros(hu.shape, F32)
    hd[...] = jnp.zeros(hd.shape, F32)
    he[...] = jnp.ones(he.shape, F32)
    for c in range(6):
        ht[ds(c * 128, CX, 8), :] = ylo[ds(c * CX, CX), :] * myl
        ht[ds(c * 128 + 1, CX, 8), :] = yhi[ds(c * CX, CX), :] * myh
    for i, c in enumerate(YC):
        hu[ds(i * 128, CX, 8), :] = f[ds(c * CX * CY, CX, CY), :]
        hu[ds(i * 128 + 1, CX, 8), :] = yhi[ds((6 + i) * CX, CX), :] * myh
        hd[ds(i * 128, CX, 8), :] = ylo[ds((6 + i) * CX, CX), :] * myl
        hd[ds(i * 128 + 1, CX, 8), :] = f[ds(c * CX * CY + CY - 1, CX, CY), :]
    perm = [perm_rows[ds(k, 1), :] for k in range(16)]
    he[ds(0, CX, 8), :] = jnp.where(myl > 0, lookup(ylo[ds(10 * CX, CX), :], perm), 1.0)
    he[ds(1, CX, 8), :] = jnp.where(myh > 0, lookup(yhi[ds(10 * CX, CX), :], perm), 1.0)
    row8 = row_of((8, NZ))
    inside = jnp.where(row8 == 0, myl, jnp.where(row8 == 1, myh, 0.0))
    zero8, one8 = jnp.zeros((8, NZ), F32), jnp.ones((8, NZ), F32)
    e_scale, h_scale = 0.5 / HALF, 0.5 * HALF

    def halo(ref, i, x):
        return ref[ds(i * 128 + x * 8, 8), :]

    def x_side(i, x):
        if x == 0:
            return -xlo[ds(i * CY, CY), :] * mxl
        return xhi[ds(i * CY, CY), :] * mxh

    wg, yl = one8, one8
    ys = [jnp.zeros((ROWS, NZ), F32)] * 6
    for x in range(CX):
        fh = [halo(ht, c, x) for c in range(6)]
        dx, dy, dz = {}, {}, {}
        for c in XC:
            up = halo(ht, c, x + 1) if x < CX - 1 else zero8
            down = halo(ht, c, x - 1) if x > 0 else zero8
            dx[c] = up - down
        for i, c in enumerate(YC):
            dy[c] = halo(hu, i, x) - halo(hd, i, x)
        for c in (0, 1, 3, 4):
            dz[c] = diff_z(fh[c])
        s_h = halo(he, 0, x) * (1.0 / (HALF * HALF))
        right_h = right_sides(fh, s_h, dx, dy, dz)
        w = s_h + wg
        g_h = 1.0 / (1.0 + w)
        wg = w * g_h
        yl = yl * g_h
        gs[ds(x * 8, 8), :] = g_h
        lsp_h[ds(x * 8, 8), :] = yl
        s = scaled[ds(x * CY, CY), :]
        g = jnp.concatenate([gxs[ds(x * CY, CY), :], g_h], axis=0)
        own = [right[ds((c * CX + x) * CY, CY), :] for c in range(6)]
        if x in (0, CX - 1):
            own[1] = own[1] - e_scale * x_side(3, x)
            own[2] = own[2] + e_scale * x_side(2, x)
            own[4] = own[4] + h_scale * s * x_side(1, x)
            own[5] = own[5] - h_scale * s * x_side(0, x)
        side = {}
        for c in YC:
            low = jnp.where(row8 == 0, -fh[c][0:1], 0.0)
            high = jnp.where(row8 == 7, fh[c][1:2], 0.0)
            side[c] = (low, high)

        def at_rows(value, weight, c):
            low, high = side[c]
            return jnp.concatenate(
                [value[:8] + weight[:8] * low, value[8:16], value[16:] + weight[16:] * high], axis=0
            )

        h_weight = h_scale * s
        e_weight = jnp.full((CY, NZ), e_scale, F32)
        own[0] = at_rows(own[0], e_weight, 5)
        own[2] = at_rows(own[2], -e_weight, 3)
        own[3] = at_rows(own[3], -h_weight, 2)
        own[5] = at_rows(own[5], h_weight, 0)
        for c in range(6):
            r = jnp.concatenate([own[c], right_h[c] * inside], axis=0)
            ys[c] = (r + ys[c]) * g
            sol[ds((c * CX + x) * ROWS, ROWS), :] = ys[c]
    tail = list(ys)
    ul, ur, us = zero8, one8, [jnp.zeros((ROWS, NZ), F32)] * 6
    right_last = None
    for x in reversed(range(CX)):
        g_h = gs[ds(x * 8, 8), :]
        g = jnp.concatenate([gxs[ds(x * CY, CY), :], g_h], axis=0)
        ul = lsp_h[ds(x * 8, 8), :] + g_h * ul
        ur = g_h * ur
        if x == CX - 1:
            right_last = ur
        lsp_h[ds(x * 8, 8), :] = ul
        rsp_h[ds(x * 8, 8), :] = ur
        for c in range(6):
            here = ds((c * CX + x) * ROWS, ROWS)
            us[c] = sol[here, :] + g * us[c]
            sol[here, :] = us[c]
    lead = us
    last = CX - 1
    left_first = jnp.concatenate([lsp[ds(0, CY), :], ul], axis=0)
    right_first = jnp.concatenate([rsp[ds(0, CY), :], ur], axis=0)
    right_last = jnp.concatenate([rsp[ds(last * CY, CY), :], right_last], axis=0)

    def with_halo(value, extra):
        return jnp.concatenate([value[:CY], extra], axis=0)

    lead_rows, tail_rows = list(lead), list(tail)
    lead_rows[1] = with_halo(lead[1], halo(ht, 1, 0))
    tail_rows[1] = with_halo(tail[1], halo(ht, 1, last))
    lead_rows[4] = with_halo(lead[4], halo(he, 0, 0) * e_scale)
    tail_rows[4] = with_halo(tail[4], halo(he, 0, last) * e_scale)
    lead_rows[2] = with_halo(lead[2], lead[2][CY:] + e_scale * halo(ht, 4, 0))
    tail_rows[2] = with_halo(tail[2], tail[2][CY:] - e_scale * halo(ht, 4, last))
    for c in range(6):
        send[ds(c, ROWS, 16), :] = lead_rows[c]
        send[ds(8 + c, ROWS, 16), :] = tail_rows[c]
    send[ds(6, ROWS, 16), :] = left_first
    send[ds(7, ROWS, 16), :] = right_first
    send[ds(14, ROWS, 16), :] = right_first
    send[ds(15, ROWS, 16), :] = right_last


def join_body(rec, back, phis, psis, ms, ns):
    gx = lax.axis_index("gx")
    row8 = row_of((8, NZ))
    shifted = (row8 == 5) & ((gx == CY) | (gx == CY + 1))

    def line(b, k):
        return jnp.broadcast_to(rec[ds(b * 16 + k, 1), :], (8, NZ))

    def shifts(b):
        low = high = jnp.zeros((8, NZ), F32)
        if b > 0:
            low = jnp.where(shifted, line(b, 4) * line(b - 1, 9), 0.0)
        if b < NB - 1:
            high = jnp.where(shifted, -line(b, 12) * line(b + 1, 1), 0.0)
        return low, high

    m = n = jnp.zeros((8, NZ), F32)
    for b in range(NB):
        low, high = shifts(b)
        a, cross, d = line(b, 6), line(b, 7), line(b, 15)
        p = rec[ds(b * 16, 8), :] + a * low + cross * high
        q = rec[ds(b * 16 + 8, 8), :] + cross * low + d * high
        ms[ds(b * 8, 8), :] = m
        ns[ds(b * 8, 8), :] = n
        gain = 1.0 / (1.0 - a * n)
        phi = gain * (p + a * m)
        psi = gain * cross
        phis[ds(b * 8, 8), :] = phi
        psis[ds(b * 8, 8), :] = psi
        m = q + cross * (m + n * phi)
        n = d + cross * (n * psi)
    ahead = jnp.zeros((8, NZ), F32)
    for b in reversed(range(NB)):
        low, high = shifts(b)
        lead = phis[ds(b * 8, 8), :] + psis[ds(b * 8, 8), :] * ahead
        back[ds(b * 16, 8), :] = ms[ds(b * 8, 8), :] + ns[ds(b * 8, 8), :] * lead + low
        back[ds(b * 16 + 8, 8), :] = ahead + high
        ahead = lead


def second_body(
    back, sol, lsp, rsp, lsp_h, rsp_h, scaled, gys, ly, ry, r2, rec, mid, inc, out
):
    for c in range(6):
        inc[ds(c * ROWS, ROWS), :] = back[ds(c, ROWS, 16), :]
        out[ds(c * ROWS, ROWS), :] = back[ds(8 + c, ROWS, 16), :]

    def settle(x, carry):
        at, at_h = ds(pl.multiple_of(x * CY, 8), CY), ds(pl.multiple_of(x * 8, 8), 8)
        left = jnp.concatenate([lsp[at, :], lsp_h[at_h, :]], axis=0)
        right = jnp.concatenate([rsp[at, :], rsp_h[at_h, :]], axis=0)
        for c in range(6):
            here = ds(pl.multiple_of((c * CX + x) * ROWS, 8), ROWS)
            mid[here, :] = (
                sol[here, :]
                + left * inc[ds(c * ROWS, ROWS), :]
                + right * out[ds(c * ROWS, ROWS), :]
            )
        return carry

    lax.fori_loop(0, CX, settle, 0, unroll=CX)

    def main(c, x):
        return mid[ds((c * CX + x) * ROWS, CY), :]

    for x in range(CX):
        f = [main(c, x) for c in range(6)]
        dx, dy, dz = {}, {}, {}
        for c in XC:
            up = main(c, x + 1) if x < CX - 1 else out[ds(c * ROWS, CY), :]
            down = main(c, x - 1) if x > 0 else inc[ds(c * ROWS, CY), :]
            dx[c] = up - down
        for c in YC:
            edge = mid[ds((c * CX + x) * ROWS + CY, 8), :]
            dy[c] = diff_y(f[c], edge[0:1], edge[1:2])
        for c in (0, 1, 3, 4):
            dz[c] = diff_z(f[c])
        s = scaled[ds(x * CY, CY), :]
        for c, r in enumerate(right_sides(f, s, dx, dy, dz)):
            r2[ds((c * CX + x) * CY, CY), :] = r

    ys = [jnp.zeros((CX, NZ), F32)] * 6
    for y in range(CY):
        g = gys[ds(y * CX, CX), :]
        for c in range(6):
            here = ds(c * CX * CY + y, CX, CY)
            ys[c] = (r2[here, :] + ys[c]) * g
            r2[here, :] = ys[c]
    for c in range(6):
        rec[ds((8 + c) * CX, CX), :] = ys[c]
    us = [jnp.zeros((CX, NZ), F32)] * 6
    for y in reversed(range(CY)):
        g = gys[ds(y * CX, CX), :]
        for c in range(6):
            here = ds(c * CX * CY + y, CX, CY)
            us[c] = r2[here, :] + g * us[c]
    for c in range(6):
        rec[ds(c * CX, CX), :] = us[c]
    rec[ds(6 * CX, CX), :] = ly[ds(0, CX, CY), :]
    rec[ds(7 * CX, CX), :] = ry[ds(0, CX, CY), :]
    rec[ds(14 * CX, CX), :] = ry[ds(CY - 1, CX, CY), :]


WIDTH = NZ // SLOTS


def patches_body(
    cell_row, owner_row, cell_hbm, reduced, gys, ly, ry,
    soly, hot, spread, ranks, table, base, z_hot, x_left, x_right, lines, cell, sem,
):
    copy = pltpu.make_async_copy(cell_hbm, cell, sem.at[0])
    copy.start()
    gx, gy = lax.axis_index("gx"), lax.axis_index("gy")
    owner = jnp.broadcast_to(owner_row[...], (PATCH, PATCH))
    rows, lanes = row_of((PATCH, PATCH)), lane_of((PATCH, PATCH))
    owner_col = jnp.sum(jnp.where(rows == lanes, owner, 0), axis=1, keepdims=True)
    earlier = (owner == owner_col) & (rows < lanes)
    rank = jnp.sum(jnp.where(earlier, 1, 0), axis=0, keepdims=True)
    ranks[...] = jnp.broadcast_to(rank, (8, PATCH))
    hot[...] = jnp.where(row_of((NZ, PATCH)) == owner[:NZ], 1.0, 0.0).astype(BF16)
    place = jnp.broadcast_to(cell_row[...], (8, PATCH))
    line, pz = place >> 7, place & 127
    x = (line * 2731) >> 16
    px, py = gx * CX + x, gy * CY + line - x * CY
    row8 = row_of((8, PATCH))
    place = jnp.where(row8 == 0, px, jnp.where(row8 == 1, py, jnp.where(row8 == 2, pz, 0)))
    place = place.astype(F32)
    spread[...] = jnp.zeros(spread.shape, F32)
    for k in range(SLOTS):
        spread[ds(k * WIDTH + 8, 8), :] = jnp.where(ranks[...] == k, place, 0.0)
    sector = gx * NBY + gy
    angle = row_of((NZ, NZ)).astype(F32)
    sin_theta, cos_theta = sine_cosine(math.pi * (angle + 0.5) / NZ)
    turn = jnp.full((8, NZ), sector, jnp.int32).astype(F32) * (2.0 * math.pi / (NB * NBY))
    sin_phi, cos_phi = sine_cosine(turn)
    table[ds(0, NZ), :] = KAPPA * sin_theta * cos_phi[0:1]
    table[ds(NZ, NZ), :] = KAPPA * sin_theta * sin_phi[0:1]
    table[ds(2 * NZ, NZ), :] = KAPPA * cos_theta
    us = [jnp.zeros((CX, NZ), F32)] * 6
    for y in reversed(range(CY)):
        g = gys[ds(y * CX, CX), :]
        for c in range(6):
            at = ds(c * CX * CY + y, CX, CY)
            us[c] = reduced[at, :] + g * us[c]
            soly[at, :] = us[c]
            lines[ds(y * 8 + c, CX, CY * 8), :] = us[c]
    for x_own in range(CX):
        at = ds(x_own * CY, CY)
        lines[ds(x_own * (CY * 8) + 6, CY, 8), :] = ly[at, :]
        lines[ds(x_own * (CY * 8) + 7, CY, 8), :] = ry[at, :]
    copy.wait()
    lane = lane_of((8, NZ))
    halves = []
    for half in range(PATCH // NZ):

        def pick(j, acc):
            at = cell[half * NZ + j]
            values = lines[ds(pl.multiple_of((at >> 7) * 8, 8), 8), :]
            moved = pltpu.roll(values, (j - (at & 127)) & 127, 1)
            return jnp.where(lane == j, moved, acc)

        halves.append(lax.fori_loop(0, NZ, pick, jnp.zeros((8, NZ), F32), unroll=PICKS))
    samples = jnp.concatenate(halves, axis=1)
    base[...] = jnp.where(row8 < 6, samples, 0.0)
    z_hot[...] = jnp.where(row_of((NZ, PATCH)) == pz[0:1], 1.0, 0.0).astype(BF16)
    here = row_of((CX, PATCH)) == x[0:1]
    x_left[...] = jnp.where(here, samples[6:7], 0.0)
    x_right[...] = jnp.where(here, samples[7:8], 0.0)


def in_parts(value):
    parts = []
    for _ in range(3):
        parts.append(value.astype(BF16))
        value = value - parts[-1].astype(F32)
    return parts


def finish_body(
    rec0, rec1, rec2, rec3, base, z_hot, x_left, x_right, hot, static, ranks, soly, ly, ry,
    new, send, inc, out, spread,
):
    gy = lax.axis_index("gy")

    def get(choices, k):
        value = choices[-1][ds(k * CX, CX), :]
        for at, rec in choices[:-1]:
            value = jnp.where(gy == at, rec[ds(k * CX, CX), :], value)
        return value

    zero = jnp.zeros((CX, NZ), F32)

    def sweep(order, up):
        m, n = [zero] * 6, zero
        near, far, mine, other = (8, 0, 14, 6) if up else (0, 8, 6, 14)
        for rec, valid in order:
            cross = get(rec, 7)
            gain = 1.0 / (1.0 - get(rec, other) * n)
            value = [
                get(rec, near + c)
                + cross * (m[c] + n * (gain * (get(rec, far + c) + get(rec, other) * m[c])))
                for c in range(6)
            ]
            m = [jnp.where(valid, v, old) for v, old in zip(value, m)]
            n = jnp.where(valid, get(rec, mine) + cross * (n * (gain * cross)), n)
        return m, n

    below, below_gain = sweep(
        [
            (((1, rec1), (2, rec2), rec3), gy >= 1),
            (((2, rec3), rec2), gy >= 2),
            ((rec1,), gy >= 3),
        ],
        True,
    )
    above, above_gain = sweep(
        [
            (((0, rec3), (1, rec2), rec1), gy <= 2),
            (((0, rec2), rec3), gy <= 1),
            ((rec1,), gy <= 0),
        ],
        False,
    )
    own = (rec0,)
    a, cross, d = get(own, 6), get(own, 7), get(own, 14)
    ll, lt = 1.0 - a * below_gain, -cross * above_gain
    tl, tt = -cross * below_gain, 1.0 - d * above_gain
    over = 1.0 / (ll * tt - lt * tl)
    for c in range(6):
        p = get(own, c) + a * below[c] + cross * above[c]
        q = get(own, 8 + c) + cross * below[c] + d * above[c]
        lead, tail = (p * tt - lt * q) * over, (ll * q - tl * p) * over
        inc[ds(c * CX, CX), :] = below[c] + below_gain * lead
        out[ds(c * CX, CX), :] = above[c] + above_gain * tail

    reach = jnp.zeros((12 * CX, PATCH), F32)
    for part in in_parts(jnp.concatenate([inc[...], out[...]], axis=0)):
        reach += jnp.dot(part, z_hot[...], preferred_element_type=F32)
    added = []
    for c in range(6):
        low, high = reach[c * CX : (c + 1) * CX], reach[(6 + c) * CX : (7 + c) * CX]
        weighed = low * x_left[...] + high * x_right[...]
        added.append(jnp.sum(weighed, axis=0, keepdims=True))
    samples = base[...] + jnp.concatenate(added + [jnp.zeros((2, PATCH), F32)], axis=0)
    spread[...] = static[...]
    for k in range(SLOTS):
        spread[ds(k * WIDTH, 8), :] = jnp.where(ranks[...] == k, samples, 0.0)
    total = jnp.zeros((NZ, NZ), F32)
    for part in in_parts(spread[...]):
        total += lax.dot_general(
            hot[...], part, (((1,), (1,)), ((), ())), preferred_element_type=F32
        )
    send[...] = total
    for x in range(CX):
        left, right = ly[ds(x * CY, CY), :], ry[ds(x * CY, CY), :]
        for c in range(6):
            here = ds((c * CX + x) * CY, CY)
            new[here, :] = (
                soly[here, :]
                + left * inc[ds(c * CX + x, 1), :]
                + right * out[ds(c * CX + x, 1), :]
            )


def sine_cosine(v):
    k = jnp.floor(v * (2.0 / math.pi) + 0.5)
    r = ((v - k * 1.5703125) - k * 4.837512969970703125e-4) - k * 7.54978995489188e-8
    z = r * r
    s = ((-1.9515295891e-4 * z + 8.3321608736e-3) * z - 1.6666654611e-1) * z * r + r
    c = ((2.443315711809948e-5 * z - 1.388731625493765e-3) * z + 4.166664568298827e-2) * (z * z)
    c = c - 0.5 * z + 1.0
    q = k.astype(jnp.int32)
    odd = (q & 1) == 1
    sine, cosine = jnp.where(odd, c, s), jnp.where(odd, s, c)
    sine = jnp.where((q & 2) == 2, -sine, sine)
    cosine = jnp.where(((q + 1) & 2) == 2, -cosine, cosine)
    return sine, cosine


def sector_body(recv, table, made, far, new, sem):
    copies = []
    for k in range(OUTS):
        part = ds(k * (6 * CX * CY // OUTS), 6 * CX * CY // OUTS)
        copies.append(pltpu.make_async_copy(made.at[part, :], new.at[part, :], sem.at[k]))
        copies[-1].start()
    flipped = jnp.transpose(recv[...])
    along = [table[ds(i * NZ, NZ), :] for i in range(3)]
    parts, cosines, sines = [], [], []
    for k in range(SLOTS):
        parts.append(flipped[k * WIDTH : k * WIDTH + 8])
        px, py, pz = (flipped[k * WIDTH + 8 + i : k * WIDTH + 9 + i] for i in range(3))
        sine, cosine = sine_cosine((px * along[0] + py * along[1]) + pz * along[2])
        cosines.append(cosine)
        sines.append(sine)
    value = jnp.concatenate(parts, axis=1)
    wave = jnp.concatenate(
        [jnp.concatenate(cosines, axis=1), jnp.concatenate(sines, axis=1)], axis=0
    )
    value_high = value.astype(BF16)
    value_low = (value - value_high.astype(F32)).astype(BF16)
    wave_high = wave.astype(BF16)
    wave_low = (wave - wave_high.astype(F32)).astype(BF16)
    sums = jnp.zeros((8, 2 * NZ), F32)
    for a, b in ((value_high, wave_high), (value_low, wave_high), (value_high, wave_low)):
        sums += lax.dot_general(a, b, (((1,), (1,)), ((), ())), preferred_element_type=F32)
    scale = 1.0 / math.sqrt(PATCH)
    far[0:6, :] = sums[0:6, :NZ] * scale
    far[6:12, :] = sums[0:6, NZ:] * scale
    for copy in copies:
        copy.wait()


def shift(value, axis, by):
    count = lax.axis_size(axis)
    return lax.ppermute(value, axis, [(i, (i + by) % count) for i in range(count)])


def local(fields, material, permittivity, patch_cell, patch_owner):
    f = fields.reshape(6 * CX * CY, NZ)
    mat = material.reshape(CX * CY, NZ)
    plane, cells, block = (len(XC) * CY, NZ), (CX * CY, NZ), (6 * CX * CY, NZ)
    edge, halo = (11 * CX, NZ), (CX * 8, NZ)
    table16 = pltpu.SMEM((16,), F32)
    xh, xl, yh, yl = call(
        edges_body,
        [(184, NZ), (184, NZ), edge, edge],
        [fields.reshape(6 * CX, CY, NZ), material],
        [(4, 6 * CX, 1, NZ), pltpu.VMEM((2, CX, 1, NZ), jnp.int32)],
        hbm=(0, 1),
        sems=6 + 2 * len(XC),
        vmem=VM,
        pinned=(0, 1, 2, 3),
    )
    xlo, xhi = shift(xh, "gx", 1), shift(xl, "gx", -1)
    ylo, yhi = shift(yh, "gy", 1), shift(yl, "gy", -1)
    scaled, right, gxs, lsp, rsp, gys, ly, ry, perm_rows = call(
        inner_body,
        [cells, block] + [cells] * 6 + [(16, NZ)],
        [f, mat, permittivity],
        [table16, cells],
        hbm=(2,),
        sems=1,
        cost=COST,
    )
    sol, lsp_h, rsp_h, send = call(
        first_body,
        [(6 * CX * ROWS, NZ), halo, halo, (ROWS * 16, NZ)],
        [f, scaled, right, gxs, lsp, rsp, xlo, xhi, ylo, yhi, perm_rows],
        [(6 * 128, NZ), (4 * 128, NZ), (4 * 128, NZ), halo, halo],
    )
    rec = lax.all_to_all(send.reshape(NB, 16, NZ), "gx", 0, 0, tiled=True)
    (back,) = call(join_body, [(NB * 16, NZ)], [rec.reshape(NB * 16, NZ)], [(NB * 8, NZ)] * 4)
    back = lax.all_to_all(back.reshape(NB, 16, NZ), "gx", 0, 0, tiled=True)
    reduced, rec = call(
        second_body,
        [block, (15 * CX, NZ)],
        [back.reshape(NB * 16, NZ), sol, lsp, rsp, lsp_h, rsp_h, scaled, gys, ly, ry],
        [(6 * CX * ROWS, NZ), (6 * ROWS, NZ), (6 * ROWS, NZ)],
    )
    others = [
        lax.ppermute(rec, "gy", [(i, i ^ k) for i in range(NBY)]) for k in (1, 2, 3)
    ]
    ints, sampled = jax.ShapeDtypeStruct((8, PATCH), jnp.int32), (CX, PATCH)
    ones = jax.ShapeDtypeStruct((NZ, PATCH), BF16)
    soly, hot, static, ranks, table, base, z_hot, x_left, x_right = call(
        patches_body,
        [block, ones, (NZ, PATCH), ints, (3 * NZ, NZ), (8, PATCH), ones, sampled, sampled],
        [
            patch_cell.reshape(1, PATCH), patch_owner.reshape(1, PATCH), patch_cell,
            reduced, gys, ly, ry,
        ],
        [(CX * CY * 8, NZ), pltpu.SMEM((PATCH,), jnp.int32)],
        hbm=(2,),
        sems=1,
        cost=COST,
    )
    new, send = call(
        finish_body,
        [block, (NB * NBY, NZ)],
        [rec, *others, base, z_hot, x_left, x_right, hot, static, ranks, soly, ly, ry],
        [(6 * CX, NZ), (6 * CX, NZ), (NZ, PATCH)],
        pinned=(0,),
    )
    recv = lax.all_to_all(send, ("gx", "gy"), 0, 0, tiled=True)
    far, new = call(
        sector_body, [(12, NZ), block], [recv, table, new], hbm_outs=(1,), sems=OUTS
    )
    return new.reshape(6, CX, CY, NZ), far


def solution(mesh):
    return jax.shard_map(
        local,
        mesh=mesh,
        in_specs=(
            P(None, "gx", "gy", None),
            P("gx", "gy", None),
            P(),
            P(("gx", "gy")),
            P(("gx", "gy"), None),
        ),
        out_specs=(P(None, "gx", "gy", None), P(None, ("gx", "gy"))),
        check_vma=False,
    )
```

```python
import math

import jax
import jax.numpy as jnp
from jax import lax
from jax.experimental import pallas as pl
from jax.experimental.pallas import tpu as pltpu
from jax.sharding import PartitionSpec as P

F32 = jnp.float32
BF16 = jnp.bfloat16
CX, CY, NZ = 16, 24, 128
NB = 32
NBY = 4
ROWS = 32
HALF = 32.0
XC = (1, 2, 4, 5)
YC = (0, 2, 3, 5)
SLOTS = 4
PATCH = 256
KAPPA = 0.5
EDGES = (CY - 1, CY - 2, 0, 1)
PICKS = 32
COST = 4_000_000
OUTS = 1
VM = 56


def ds(start, size, stride=None):
    return pl.ds(start, size) if stride is None else pl.ds(start, size, stride=stride)


def call(body, outs, args, scratch=(), smem=(), hbm=(), hbm_outs=(), sems=0, cost=0, vmem=40, pinned=()):
    def place(i, slow):
        if i in slow:
            return pl.BlockSpec(memory_space=pltpu.HBM)
        return pl.BlockSpec(memory_space=pltpu.SMEM if slow is hbm and i in smem else pltpu.VMEM)

    shapes = [o if isinstance(o, jax.ShapeDtypeStruct) else jax.ShapeDtypeStruct(o, F32) for o in outs]
    shapes = [pltpu.VMEM(o.shape, o.dtype) if i in pinned else o for i, o in enumerate(shapes)]
    space = [o if not isinstance(o, tuple) else pltpu.VMEM(o, F32) for o in scratch]
    if sems:
        space.append(pltpu.SemaphoreType.DMA((sems,)))
    estimate = None
    if cost:
        estimate = pl.CostEstimate(flops=cost, bytes_accessed=cost, transcendentals=0)
    return pl.pallas_call(
        body,
        out_shape=shapes,
        in_specs=[place(i, hbm) for i in range(len(args))],
        out_specs=[place(i, hbm_outs) for i in range(len(outs))],
        scratch_shapes=space,
        cost_estimate=estimate,
        compiler_params=pltpu.CompilerParams(vmem_limit_bytes=vmem * 1024 * 1024),
    )(*args)


def flag(cond):
    return jnp.where(cond, 1.0, 0.0).astype(F32)


def row_of(shape):
    return lax.broadcasted_iota(jnp.int32, shape, 0)


def lane_of(shape):
    return lax.broadcasted_iota(jnp.int32, shape, 1)


def diff_z(f):
    lane = lane_of(f.shape)
    up = jnp.where(lane == NZ - 1, 0.0, pltpu.roll(f, NZ - 1, 1))
    down = jnp.where(lane == 0, 0.0, pltpu.roll(f, 1, 1))
    return up - down


def diff_y(f, below, above):
    row = row_of(f.shape)
    up = jnp.where(row == CY - 1, above, pltpu.roll(f, CY - 1, 0))
    down = jnp.where(row == 0, below, pltpu.roll(f, 1, 0))
    return up - down


def right_sides(f, s, dx, dy, dz):
    curl_h = (dy[5] - dz[4], dz[3] - dx[5], dx[4] - dy[3])
    curl_e = (dy[2] - dz[1], dz[0] - dx[2], dx[1] - dy[0])
    electric = [s * f[m] + (0.5 / HALF) * curl_h[m] for m in range(3)]
    magnetic = [s * (f[3 + m] - (0.5 * HALF) * curl_e[m]) for m in range(3)]
    return electric + magnetic


def lookup(m, perm):
    e = jnp.broadcast_to(perm[0], m.shape)
    for k in range(1, 16):
        e = jnp.where(m == k, perm[k], e)
    return e


def edges_body(f, mat, xh, xl, yh, yl, rows, mats, sem):
    copies = []

    def fetch(source, target):
        copy = pltpu.make_async_copy(source, target, sem.at[len(copies)])
        copy.start()
        copies.append(copy)

    for i, y in enumerate(EDGES):
        fetch(f.at[:, ds(y, 1), :], rows.at[i])
    for i, y in enumerate((CY - 1, 0)):
        fetch(mat.at[:, ds(y, 1), :], mats.at[i])
    for i, c in enumerate(XC):
        fetch(f.at[c * CX + CX - 1], xh.at[ds(i * CY, CY), :])
        fetch(f.at[c * CX], xl.at[ds(i * CY, CY), :])
    for copy in copies:
        copy.wait()
    for k, out in enumerate((yh, yl)):
        for c in range(6):
            out[ds(c * CX, CX), :] = rows[2 * k, ds(c * CX, CX), 0, :]
        for i, c in enumerate(YC):
            out[ds((6 + i) * CX, CX), :] = rows[2 * k + 1, ds(c * CX, CX), 0, :]
        out[ds(10 * CX, CX), :] = mats[k, :, 0, :].astype(F32)


def inner_body(
    f, mat, perm_hbm, scaled, right, gx_out, lsp, rsp, gy_out, ly, ry, perm_rows, perm, yls, sem
):
    copy = pltpu.make_async_copy(perm_hbm, perm, sem.at[0])
    copy.start()
    copy.wait()
    for k in range(16):
        perm_rows[ds(k, 1), :] = jnp.full((1, NZ), perm[k], F32)

    def main(c, x):
        return f[ds((c * CX + x) * CY, CY), :]

    one, zero = jnp.ones((CY, NZ), F32), jnp.zeros((CY, NZ), F32)
    wg, yl = one, one
    for x in range(CX):
        at = ds(x * CY, CY)
        s = lookup(mat[at, :], perm) * (1.0 / (HALF * HALF))
        scaled[at, :] = s
        w = s + wg
        g = 1.0 / (1.0 + w)
        wg = w * g
        gx_out[at, :] = g
        yl = yl * g
        lsp[at, :] = yl
        fm = [main(c, x) for c in range(6)]
        dx, dy, dz = {}, {}, {}
        for c in XC:
            up = main(c, x + 1) if x < CX - 1 else zero
            down = main(c, x - 1) if x > 0 else zero
            dx[c] = up - down
        for c in YC:
            dy[c] = diff_y(fm[c], 0.0, 0.0)
        for c in (0, 1, 3, 4):
            dz[c] = diff_z(fm[c])
        for c, r in enumerate(right_sides(fm, s, dx, dy, dz)):
            right[ds((c * CX + x) * CY, CY), :] = r
    ul, ur = zero, one
    for x in reversed(range(CX)):
        at = ds(x * CY, CY)
        g = gx_out[at, :]
        ul = lsp[at, :] + g * ul
        ur = g * ur
        lsp[at, :] = ul
        rsp[at, :] = ur
    one, zero = jnp.ones((CX, NZ), F32), jnp.zeros((CX, NZ), F32)
    wg, yl = one, one
    for y in range(CY):
        w = scaled[ds(y, CX, CY), :] + wg
        g = 1.0 / (1.0 + w)
        wg = w * g
        gy_out[ds(y * CX, CX), :] = g
        yl = yl * g
        yls[ds(y * CX, CX), :] = yl
    ul, ur = zero, one
    for y in reversed(range(CY)):
        g = gy_out[ds(y * CX, CX), :]
        ul = yls[ds(y * CX, CX), :] + g * ul
        ur = g * ur
        ly[ds(y, CX, CY), :] = ul
        ry[ds(y, CX, CY), :] = ur


def first_body(
    f, scaled, right, gxs, lsp, rsp, xlo, xhi, ylo, yhi, perm_rows,
    sol, lsp_h, rsp_h, send, ht, hu, hd, he, gs,
):
    gx, gy = lax.axis_index("gx"), lax.axis_index("gy")
    mxl, mxh = flag(gx > 0), flag(gx < NB - 1)
    myl, myh = flag(gy > 0), flag(gy < NBY - 1)
    ht[...] = jnp.zeros(ht.shape, F32)
    hu[...] = jnp.zeros(hu.shape, F32)
    hd[...] = jnp.zeros(hd.shape, F32)
    he[...] = jnp.ones(he.shape, F32)
    for c in range(6):
        ht[ds(c * 128, CX, 8), :] = ylo[ds(c * CX, CX), :] * myl
        ht[ds(c * 128 + 1, CX, 8), :] = yhi[ds(c * CX, CX), :] * myh
    for i, c in enumerate(YC):
        hu[ds(i * 128, CX, 8), :] = f[ds(c * CX * CY, CX, CY), :]
        hu[ds(i * 128 + 1, CX, 8), :] = yhi[ds((6 + i) * CX, CX), :] * myh
        hd[ds(i * 128, CX, 8), :] = ylo[ds((6 + i) * CX, CX), :] * myl
        hd[ds(i * 128 + 1, CX, 8), :] = f[ds(c * CX * CY + CY - 1, CX, CY), :]
    perm = [perm_rows[ds(k, 1), :] for k in range(16)]
    he[ds(0, CX, 8), :] = jnp.where(myl > 0, lookup(ylo[ds(10 * CX, CX), :], perm), 1.0)
    he[ds(1, CX, 8), :] = jnp.where(myh > 0, lookup(yhi[ds(10 * CX, CX), :], perm), 1.0)
    row8 = row_of((8, NZ))
    inside = jnp.where(row8 == 0, myl, jnp.where(row8 == 1, myh, 0.0))
    zero8, one8 = jnp.zeros((8, NZ), F32), jnp.ones((8, NZ), F32)
    e_scale, h_scale = 0.5 / HALF, 0.5 * HALF

    def halo(ref, i, x):
        return ref[ds(i * 128 + x * 8, 8), :]

    def x_side(i, x):
        if x == 0:
            return -xlo[ds(i * CY, CY), :] * mxl
        return xhi[ds(i * CY, CY), :] * mxh

    wg, yl = one8, one8
    ys = [jnp.zeros((ROWS, NZ), F32)] * 6
    for x in range(CX):
        fh = [halo(ht, c, x) for c in range(6)]
        dx, dy, dz = {}, {}, {}
        for c in XC:
            up = halo(ht, c, x + 1) if x < CX - 1 else zero8
            down = halo(ht, c, x - 1) if x > 0 else zero8
            dx[c] = up - down
        for i, c in enumerate(YC):
            dy[c] = halo(hu, i, x) - halo(hd, i, x)
        for c in (0, 1, 3, 4):
            dz[c] = diff_z(fh[c])
        s_h = halo(he, 0, x) * (1.0 / (HALF * HALF))
        right_h = right_sides(fh, s_h, dx, dy, dz)
        w = s_h + wg
        g_h = 1.0 / (1.0 + w)
        wg = w * g_h
        yl = yl * g_h
        gs[ds(x * 8, 8), :] = g_h
        lsp_h[ds(x * 8, 8), :] = yl
        s = scaled[ds(x * CY, CY), :]
        g = jnp.concatenate([gxs[ds(x * CY, CY), :], g_h], axis=0)
        own = [right[ds((c * CX + x) * CY, CY), :] for c in range(6)]
        if x in (0, CX - 1):
            own[1] = own[1] - e_scale * x_side(3, x)
            own[2] = own[2] + e_scale * x_side(2, x)
            own[4] = own[4] + h_scale * s * x_side(1, x)
            own[5] = own[5] - h_scale * s * x_side(0, x)
        side = {}
        for c in YC:
            low = jnp.where(row8 == 0, -fh[c][0:1], 0.0)
            high = jnp.where(row8 == 7, fh[c][1:2], 0.0)
            side[c] = (low, high)

        def at_rows(value, weight, c):
            low, high = side[c]
            return jnp.concatenate(
                [value[:8] + weight[:8] * low, value[8:16], value[16:] + weight[16:] * high], axis=0
            )

        h_weight = h_scale * s
        e_weight = jnp.full((CY, NZ), e_scale, F32)
        own[0] = at_rows(own[0], e_weight, 5)
        own[2] = at_rows(own[2], -e_weight, 3)
        own[3] = at_rows(own[3], -h_weight, 2)
        own[5] = at_rows(own[5], h_weight, 0)
        for c in range(6):
            r = jnp.concatenate([own[c], right_h[c] * inside], axis=0)
            ys[c] = (r + ys[c]) * g
            sol[ds((c * CX + x) * ROWS, ROWS), :] = ys[c]
    tail = list(ys)
    ul, ur, us = zero8, one8, [jnp.zeros((ROWS, NZ), F32)] * 6
    right_last = None
    for x in reversed(range(CX)):
        g_h = gs[ds(x * 8, 8), :]
        g = jnp.concatenate([gxs[ds(x * CY, CY), :], g_h], axis=0)
        ul = lsp_h[ds(x * 8, 8), :] + g_h * ul
        ur = g_h * ur
        if x == CX - 1:
            right_last = ur
        lsp_h[ds(x * 8, 8), :] = ul
        rsp_h[ds(x * 8, 8), :] = ur
        for c in range(6):
            here = ds((c * CX + x) * ROWS, ROWS)
            us[c] = sol[here, :] + g * us[c]
            sol[here, :] = us[c]
    lead = us
    last = CX - 1
    left_first = jnp.concatenate([lsp[ds(0, CY), :], ul], axis=0)
    right_first = jnp.concatenate([rsp[ds(0, CY), :], ur], axis=0)
    right_last = jnp.concatenate([rsp[ds(last * CY, CY), :], right_last], axis=0)

    def with_halo(value, extra):
        return jnp.concatenate([value[:CY], extra], axis=0)

    lead_rows, tail_rows = list(lead), list(tail)
    lead_rows[1] = with_halo(lead[1], halo(ht, 1, 0))
    tail_rows[1] = with_halo(tail[1], halo(ht, 1, last))
    lead_rows[4] = with_halo(lead[4], halo(he, 0, 0) * e_scale)
    tail_rows[4] = with_halo(tail[4], halo(he, 0, last) * e_scale)
    lead_rows[2] = with_halo(lead[2], lead[2][CY:] + e_scale * halo(ht, 4, 0))
    tail_rows[2] = with_halo(tail[2], tail[2][CY:] - e_scale * halo(ht, 4, last))
    for c in range(6):
        send[ds(c, ROWS, 16), :] = lead_rows[c]
        send[ds(8 + c, ROWS, 16), :] = tail_rows[c]
    send[ds(6, ROWS, 16), :] = left_first
    send[ds(7, ROWS, 16), :] = right_first
    send[ds(14, ROWS, 16), :] = right_first
    send[ds(15, ROWS, 16), :] = right_last


def join_body(rec, back, phis, psis, ms, ns):
    gx = lax.axis_index("gx")
    row8 = row_of((8, NZ))
    shifted = (row8 == 5) & ((gx == CY) | (gx == CY + 1))

    def line(b, k):
        return jnp.broadcast_to(rec[ds(b * 16 + k, 1), :], (8, NZ))

    def shifts(b):
        low = high = jnp.zeros((8, NZ), F32)
        if b > 0:
            low = jnp.where(shifted, line(b, 4) * line(b - 1, 9), 0.0)
        if b < NB - 1:
            high = jnp.where(shifted, -line(b, 12) * line(b + 1, 1), 0.0)
        return low, high

    m = n = jnp.zeros((8, NZ), F32)
    for b in range(NB):
        low, high = shifts(b)
        a, cross, d = line(b, 6), line(b, 7), line(b, 15)
        p = rec[ds(b * 16, 8), :] + a * low + cross * high
        q = rec[ds(b * 16 + 8, 8), :] + cross * low + d * high
        ms[ds(b * 8, 8), :] = m
        ns[ds(b * 8, 8), :] = n
        gain = 1.0 / (1.0 - a * n)
        phi = gain * (p + a * m)
        psi = gain * cross
        phis[ds(b * 8, 8), :] = phi
        psis[ds(b * 8, 8), :] = psi
        m = q + cross * (m + n * phi)
        n = d + cross * (n * psi)
    ahead = jnp.zeros((8, NZ), F32)
    for b in reversed(range(NB)):
        low, high = shifts(b)
        lead = phis[ds(b * 8, 8), :] + psis[ds(b * 8, 8), :] * ahead
        back[ds(b * 16, 8), :] = ms[ds(b * 8, 8), :] + ns[ds(b * 8, 8), :] * lead + low
        back[ds(b * 16 + 8, 8), :] = ahead + high
        ahead = lead


def second_body(
    back, sol, lsp, rsp, lsp_h, rsp_h, scaled, gys, ly, ry, r2, rec, mid, inc, out
):
    for c in range(6):
        inc[ds(c * ROWS, ROWS), :] = back[ds(c, ROWS, 16), :]
        out[ds(c * ROWS, ROWS), :] = back[ds(8 + c, ROWS, 16), :]

    def settle(x, carry):
        at, at_h = ds(pl.multiple_of(x * CY, 8), CY), ds(pl.multiple_of(x * 8, 8), 8)
        left = jnp.concatenate([lsp[at, :], lsp_h[at_h, :]], axis=0)
        right = jnp.concatenate([rsp[at, :], rsp_h[at_h, :]], axis=0)
        for c in range(6):
            here = ds(pl.multiple_of((c * CX + x) * ROWS, 8), ROWS)
            mid[here, :] = (
                sol[here, :]
                + left * inc[ds(c * ROWS, ROWS), :]
                + right * out[ds(c * ROWS, ROWS), :]
            )
        return carry

    lax.fori_loop(0, CX, settle, 0, unroll=CX)

    def main(c, x):
        return mid[ds((c * CX + x) * ROWS, CY), :]

    for x in range(CX):
        f = [main(c, x) for c in range(6)]
        dx, dy, dz = {}, {}, {}
        for c in XC:
            up = main(c, x + 1) if x < CX - 1 else out[ds(c * ROWS, CY), :]
            down = main(c, x - 1) if x > 0 else inc[ds(c * ROWS, CY), :]
            dx[c] = up - down
        for c in YC:
            edge = mid[ds((c * CX + x) * ROWS + CY, 8), :]
            dy[c] = diff_y(f[c], edge[0:1], edge[1:2])
        for c in (0, 1, 3, 4):
            dz[c] = diff_z(f[c])
        s = scaled[ds(x * CY, CY), :]
        for c, r in enumerate(right_sides(f, s, dx, dy, dz)):
            r2[ds((c * CX + x) * CY, CY), :] = r

    ys = [jnp.zeros((CX, NZ), F32)] * 6
    for y in range(CY):
        g = gys[ds(y * CX, CX), :]
        for c in range(6):
            here = ds(c * CX * CY + y, CX, CY)
            ys[c] = (r2[here, :] + ys[c]) * g
            r2[here, :] = ys[c]
    for c in range(6):
        rec[ds((8 + c) * CX, CX), :] = ys[c]
    us = [jnp.zeros((CX, NZ), F32)] * 6
    for y in reversed(range(CY)):
        g = gys[ds(y * CX, CX), :]
        for c in range(6):
            here = ds(c * CX * CY + y, CX, CY)
            us[c] = r2[here, :] + g * us[c]
    for c in range(6):
        rec[ds(c * CX, CX), :] = us[c]
    rec[ds(6 * CX, CX), :] = ly[ds(0, CX, CY), :]
    rec[ds(7 * CX, CX), :] = ry[ds(0, CX, CY), :]
    rec[ds(14 * CX, CX), :] = ry[ds(CY - 1, CX, CY), :]


WIDTH = NZ // SLOTS


def patches_body(
    cell_row, owner_row, cell_hbm, reduced, gys, ly, ry,
    soly, hot, spread, ranks, table, base, z_hot, x_left, x_right, lines, cell, sem,
):
    copy = pltpu.make_async_copy(cell_hbm, cell, sem.at[0])
    copy.start()
    gx, gy = lax.axis_index("gx"), lax.axis_index("gy")
    owner = jnp.broadcast_to(owner_row[...], (PATCH, PATCH))
    rows, lanes = row_of((PATCH, PATCH)), lane_of((PATCH, PATCH))
    owner_col = jnp.sum(jnp.where(rows == lanes, owner, 0), axis=1, keepdims=True)
    earlier = (owner == owner_col) & (rows < lanes)
    rank = jnp.sum(jnp.where(earlier, 1, 0), axis=0, keepdims=True)
    ranks[...] = jnp.broadcast_to(rank, (8, PATCH))
    hot[...] = jnp.where(row_of((NZ, PATCH)) == owner[:NZ], 1.0, 0.0).astype(BF16)
    place = jnp.broadcast_to(cell_row[...], (8, PATCH))
    line, pz = place >> 7, place & 127
    x = (line * 2731) >> 16
    px, py = gx * CX + x, gy * CY + line - x * CY
    row8 = row_of((8, PATCH))
    place = jnp.where(row8 == 0, px, jnp.where(row8 == 1, py, jnp.where(row8 == 2, pz, 0)))
    place = place.astype(F32)
    spread[...] = jnp.zeros(spread.shape, F32)
    for k in range(SLOTS):
        spread[ds(k * WIDTH + 8, 8), :] = jnp.where(ranks[...] == k, place, 0.0)
    sector = gx * NBY + gy
    angle = row_of((NZ, NZ)).astype(F32)
    sin_theta, cos_theta = sine_cosine(math.pi * (angle + 0.5) / NZ)
    turn = jnp.full((8, NZ), sector, jnp.int32).astype(F32) * (2.0 * math.pi / (NB * NBY))
    sin_phi, cos_phi = sine_cosine(turn)
    table[ds(0, NZ), :] = KAPPA * sin_theta * cos_phi[0:1]
    table[ds(NZ, NZ), :] = KAPPA * sin_theta * sin_phi[0:1]
    table[ds(2 * NZ, NZ), :] = KAPPA * cos_theta
    us = [jnp.zeros((CX, NZ), F32)] * 6
    for y in reversed(range(CY)):
        g = gys[ds(y * CX, CX), :]
        for c in range(6):
            at = ds(c * CX * CY + y, CX, CY)
            us[c] = reduced[at, :] + g * us[c]
            soly[at, :] = us[c]
            lines[ds(y * 8 + c, CX, CY * 8), :] = us[c]
    for x_own in range(CX):
        at = ds(x_own * CY, CY)
        lines[ds(x_own * (CY * 8) + 6, CY, 8), :] = ly[at, :]
        lines[ds(x_own * (CY * 8) + 7, CY, 8), :] = ry[at, :]
    copy.wait()
    lane = lane_of((8, NZ))
    halves = []
    for half in range(PATCH // NZ):

        def pick(j, acc):
            at = cell[half * NZ + j]
            values = lines[ds(pl.multiple_of((at >> 7) * 8, 8), 8), :]
            moved = pltpu.roll(values, (j - (at & 127)) & 127, 1)
            return jnp.where(lane == j, moved, acc)

        halves.append(lax.fori_loop(0, NZ, pick, jnp.zeros((8, NZ), F32), unroll=PICKS))
    samples = jnp.concatenate(halves, axis=1)
    base[...] = jnp.where(row8 < 6, samples, 0.0)
    z_hot[...] = jnp.where(row_of((NZ, PATCH)) == pz[0:1], 1.0, 0.0).astype(BF16)
    here = row_of((CX, PATCH)) == x[0:1]
    x_left[...] = jnp.where(here, samples[6:7], 0.0)
    x_right[...] = jnp.where(here, samples[7:8], 0.0)


def in_parts(value):
    parts = []
    for _ in range(3):
        parts.append(value.astype(BF16))
        value = value - parts[-1].astype(F32)
    return parts


def finish_body(
    rec0, rec1, rec2, rec3, base, z_hot, x_left, x_right, hot, static, ranks, soly, ly, ry,
    new, send, inc, out, spread,
):
    gy = lax.axis_index("gy")

    def get(choices, k):
        value = choices[-1][ds(k * CX, CX), :]
        for at, rec in choices[:-1]:
            value = jnp.where(gy == at, rec[ds(k * CX, CX), :], value)
        return value

    zero = jnp.zeros((CX, NZ), F32)

    def sweep(order, up):
        m, n = [zero] * 6, zero
        near, far, mine, other = (8, 0, 14, 6) if up else (0, 8, 6, 14)
        for rec, valid in order:
            cross = get(rec, 7)
            gain = 1.0 / (1.0 - get(rec, other) * n)
            value = [
                get(rec, near + c)
                + cross * (m[c] + n * (gain * (get(rec, far + c) + get(rec, other) * m[c])))
                for c in range(6)
            ]
            m = [jnp.where(valid, v, old) for v, old in zip(value, m)]
            n = jnp.where(valid, get(rec, mine) + cross * (n * (gain * cross)), n)
        return m, n

    below, below_gain = sweep(
        [
            (((1, rec1), (2, rec2), rec3), gy >= 1),
            (((2, rec3), rec2), gy >= 2),
            ((rec1,), gy >= 3),
        ],
        True,
    )
    above, above_gain = sweep(
        [
            (((0, rec3), (1, rec2), rec1), gy <= 2),
            (((0, rec2), rec3), gy <= 1),
            ((rec1,), gy <= 0),
        ],
        False,
    )
    own = (rec0,)
    a, cross, d = get(own, 6), get(own, 7), get(own, 14)
    ll, lt = 1.0 - a * below_gain, -cross * above_gain
    tl, tt = -cross * below_gain, 1.0 - d * above_gain
    over = 1.0 / (ll * tt - lt * tl)
    for c in range(6):
        p = get(own, c) + a * below[c] + cross * above[c]
        q = get(own, 8 + c) + cross * below[c] + d * above[c]
        lead, tail = (p * tt - lt * q) * over, (ll * q - tl * p) * over
        inc[ds(c * CX, CX), :] = below[c] + below_gain * lead
        out[ds(c * CX, CX), :] = above[c] + above_gain * tail

    reach = jnp.zeros((12 * CX, PATCH), F32)
    for part in in_parts(jnp.concatenate([inc[...], out[...]], axis=0)):
        reach += jnp.dot(part, z_hot[...], preferred_element_type=F32)
    added = []
    for c in range(6):
        low, high = reach[c * CX : (c + 1) * CX], reach[(6 + c) * CX : (7 + c) * CX]
        weighed = low * x_left[...] + high * x_right[...]
        added.append(jnp.sum(weighed, axis=0, keepdims=True))
    samples = base[...] + jnp.concatenate(added + [jnp.zeros((2, PATCH), F32)], axis=0)
    spread[...] = static[...]
    for k in range(SLOTS):
        spread[ds(k * WIDTH, 8), :] = jnp.where(ranks[...] == k, samples, 0.0)
    total = jnp.zeros((NZ, NZ), F32)
    for part in in_parts(spread[...]):
        total += lax.dot_general(
            hot[...], part, (((1,), (1,)), ((), ())), preferred_element_type=F32
        )
    send[...] = total
    for x in range(CX):
        left, right = ly[ds(x * CY, CY), :], ry[ds(x * CY, CY), :]
        for c in range(6):
            here = ds((c * CX + x) * CY, CY)
            new[here, :] = (
                soly[here, :]
                + left * inc[ds(c * CX + x, 1), :]
                + right * out[ds(c * CX + x, 1), :]
            )


def sine_cosine(v):
    k = (v * (2.0 / math.pi) + 12582912.0) - 12582912.0
    r = ((v - k * 1.5703125) - k * 4.837512969970703125e-4) - k * 7.54978995489188e-8
    z = r * r
    s = ((-1.9515295891e-4 * z + 8.3321608736e-3) * z - 1.6666654611e-1) * z * r + r
    c = ((2.443315711809948e-5 * z - 1.388731625493765e-3) * z + 4.166664568298827e-2) * (z * z)
    c = c - 0.5 * z + 1.0
    q = k.astype(jnp.int32)
    odd = (q & 1) == 1
    sine, cosine = jnp.where(odd, c, s), jnp.where(odd, s, c)
    sine = jnp.where((q & 2) == 2, -sine, sine)
    cosine = jnp.where(((q + 1) & 2) == 2, -cosine, cosine)
    return sine, cosine


def sector_body(recv, table, made, far, new, sem):
    copies = []
    for k in range(OUTS):
        part = ds(k * (6 * CX * CY // OUTS), 6 * CX * CY // OUTS)
        copies.append(pltpu.make_async_copy(made.at[part, :], new.at[part, :], sem.at[k]))
        copies[-1].start()
    flipped = jnp.transpose(recv[...])
    along = [table[ds(i * NZ, NZ), :] for i in range(3)]
    parts, cosines, sines = [], [], []
    for k in range(SLOTS):
        parts.append(flipped[k * WIDTH : k * WIDTH + 8])
        px, py, pz = (flipped[k * WIDTH + 8 + i : k * WIDTH + 9 + i] for i in range(3))
        sine, cosine = sine_cosine((px * along[0] + py * along[1]) + pz * along[2])
        cosines.append(cosine)
        sines.append(sine)
    value = jnp.concatenate(parts, axis=1)
    wave = jnp.concatenate(
        [jnp.concatenate(cosines, axis=1), jnp.concatenate(sines, axis=1)], axis=0
    )
    value_high = value.astype(BF16)
    value_low = (value - value_high.astype(F32)).astype(BF16)
    wave_high = wave.astype(BF16)
    wave_low = (wave - wave_high.astype(F32)).astype(BF16)
    sums = jnp.zeros((8, 2 * NZ), F32)
    for a, b in ((value_high, wave_high), (value_low, wave_high), (value_high, wave_low)):
        sums += lax.dot_general(a, b, (((1,), (1,)), ((), ())), preferred_element_type=F32)
    scale = 1.0 / math.sqrt(PATCH)
    far[0:6, :] = sums[0:6, :NZ] * scale
    far[6:12, :] = sums[0:6, NZ:] * scale
    for copy in copies:
        copy.wait()


def shift(value, axis, by):
    count = lax.axis_size(axis)
    return lax.ppermute(value, axis, [(i, (i + by) % count) for i in range(count)])


def local(fields, material, permittivity, patch_cell, patch_owner):
    f = fields.reshape(6 * CX * CY, NZ)
    mat = material.reshape(CX * CY, NZ)
    plane, cells, block = (len(XC) * CY, NZ), (CX * CY, NZ), (6 * CX * CY, NZ)
    edge, halo = (11 * CX, NZ), (CX * 8, NZ)
    table16 = pltpu.SMEM((16,), F32)
    xh, xl, yh, yl = call(
        edges_body,
        [(184, NZ), (184, NZ), edge, edge],
        [fields.reshape(6 * CX, CY, NZ), material],
        [(4, 6 * CX, 1, NZ), pltpu.VMEM((2, CX, 1, NZ), jnp.int32)],
        hbm=(0, 1),
        sems=6 + 2 * len(XC),
        vmem=VM,
        pinned=(0, 1, 2, 3),
    )
    xlo, xhi = shift(xh, "gx", 1), shift(xl, "gx", -1)
    ylo, yhi = shift(yh, "gy", 1), shift(yl, "gy", -1)
    scaled, right, gxs, lsp, rsp, gys, ly, ry, perm_rows = call(
        inner_body,
        [cells, block] + [cells] * 6 + [(16, NZ)],
        [f, mat, permittivity],
        [table16, cells],
        hbm=(2,),
        sems=1,
        cost=COST,
    )
    sol, lsp_h, rsp_h, send = call(
        first_body,
        [(6 * CX * ROWS, NZ), halo, halo, (ROWS * 16, NZ)],
        [f, scaled, right, gxs, lsp, rsp, xlo, xhi, ylo, yhi, perm_rows],
        [(6 * 128, NZ), (4 * 128, NZ), (4 * 128, NZ), halo, halo],
    )
    rec = lax.all_to_all(send.reshape(NB, 16, NZ), "gx", 0, 0, tiled=True)
    (back,) = call(join_body, [(NB * 16, NZ)], [rec.reshape(NB * 16, NZ)], [(NB * 8, NZ)] * 4)
    back = lax.all_to_all(back.reshape(NB, 16, NZ), "gx", 0, 0, tiled=True)
    reduced, rec = call(
        second_body,
        [block, (15 * CX, NZ)],
        [back.reshape(NB * 16, NZ), sol, lsp, rsp, lsp_h, rsp_h, scaled, gys, ly, ry],
        [(6 * CX * ROWS, NZ), (6 * ROWS, NZ), (6 * ROWS, NZ)],
    )
    others = [
        lax.ppermute(rec, "gy", [(i, i ^ k) for i in range(NBY)]) for k in (1, 2, 3)
    ]
    ints, sampled = jax.ShapeDtypeStruct((8, PATCH), jnp.int32), (CX, PATCH)
    ones = jax.ShapeDtypeStruct((NZ, PATCH), BF16)
    soly, hot, static, ranks, table, base, z_hot, x_left, x_right = call(
        patches_body,
        [block, ones, (NZ, PATCH), ints, (3 * NZ, NZ), (8, PATCH), ones, sampled, sampled],
        [
            patch_cell.reshape(1, PATCH), patch_owner.reshape(1, PATCH), patch_cell,
            reduced, gys, ly, ry,
        ],
        [(CX * CY * 8, NZ), pltpu.SMEM((PATCH,), jnp.int32)],
        hbm=(2,),
        sems=1,
        cost=COST,
    )
    new, send = call(
        finish_body,
        [block, (NB * NBY, NZ)],
        [rec, *others, base, z_hot, x_left, x_right, hot, static, ranks, soly, ly, ry],
        [(6 * CX, NZ), (6 * CX, NZ), (NZ, PATCH)],
        pinned=(0,),
    )
    recv = lax.all_to_all(send, ("gx", "gy"), 0, 0, tiled=True)
    far, new = call(
        sector_body, [(12, NZ), block], [recv, table, new], hbm_outs=(1,), sems=OUTS
    )
    return new.reshape(6, CX, CY, NZ), far


def solution(mesh):
    return jax.shard_map(
        local,
        mesh=mesh,
        in_specs=(
            P(None, "gx", "gy", None),
            P("gx", "gy", None),
            P(),
            P(("gx", "gy")),
            P(("gx", "gy"), None),
        ),
        out_specs=(P(None, "gx", "gy", None), P(None, ("gx", "gy"))),
        check_vma=False,
    )
```
